32 devices in a mesh: dp: 4 (over y, core), row: 2 (over x), col: 4 (over z).
Axes of the slice: x: 2, y: 2, z: 4, core: 2. Of those that a mesh axis runs over, the one named last changes fastest.
Arguments:
- block_input: bfloat16 [4096, 2048], P('dp', ('row', 'col')), may hold values from -6 to 6
- segment_ids: int32 [4096], P('dp'), may hold values from 0 to 15, as said below
- positions: int32 [4096], P('dp'), may hold values from 0 to 1278, as said below
- ln_gain: bfloat16 [2048], P(('row', 'col')), may hold values from 0.5 to 1.5
- ln_bias: bfloat16 [2048], P(('row', 'col')), may hold values from -2 to 2
- qkv_weight: bfloat16 [2048, 3, 2048], P('row', None, 'col'), may hold values from -0.125 to 0.125
- qkv_bias: float32 [3, 4, 2, 256], P(None, 'col', 'row'), may hold values from -2 to 2
- dense_weight: bfloat16 [2048, 2048], P('col', 'row'), may hold values from -1.5 to 1.5
- dense_bias: float32 [2048], P(('row', 'col')), may hold values from -2 to 2
- fc1_weight: bfloat16 [2048, 8192], P('row', 'col'), may hold values from -0.125 to 0.125
- fc1_bias: float32 [4, 2, 1024], P('col', 'row'), may hold values from -2 to 2
- fc2_weight: bfloat16 [8192, 2048], P('col', 'row'), may hold values from -0.0625 to 0.0625
- fc2_bias: float32 [2048], P(('row', 'col')), may hold values from -2 to 2
- cotangent: bfloat16 [4096, 2048], P('dp', ('row', 'col')), may hold values from -6 to 6
Outputs:
- block_output: bfloat16 [4096, 2048], P('dp', ('row', 'col'))
- input_grad: float32 [4096, 2048], P('dp', ('row', 'col'))
- ln_gain_grad: float32 [2048], P(('row', 'col'))
- ln_bias_grad: float32 [2048], P(('row', 'col'))
- qkv_weight_grad: float32 [2048, 3, 2048], P('row', None, 'col')
- qkv_bias_grad: float32 [3, 4, 2, 256], P(None, 'col', 'row')
- dense_weight_grad: float32 [2048, 2048], P('col', 'row')
- dense_bias_grad: float32 [2048], P(('row', 'col'))
- fc1_weight_grad: float32 [2048, 8192], P('row', 'col')
- fc1_bias_grad: float32 [4, 2, 1024], P('col', 'row')
- fc2_weight_grad: float32 [8192, 2048], P('col', 'row')
- fc2_bias_grad: float32 [2048], P(('row', 'col'))
The draws below stay inside these ranges and needn't reach their ends.
Inputs may be any that keep to these rules, and one draw needn't show every extreme that they name: `segment_ids`: each aligned block of 1024 tokens (one index of dp) holds four whole documents end to end, each at least one token; ids never fall, block b holds ids 4 b to 4 b + 3, and one document of every block has exactly 768 tokens. Within a document, positions count up by one from that document's own start offset.
All inputs are finite; a program needn't handle non-finite values.
Results may differ from the reference program's by a relative error of at most 0.0098.
Values may be sent and summed in bfloat16 or wider, within the bound.
A program may use at most 192 MiB of HBM per device.

```python
import math
import jax
import jax.numpy as jnp
from jax import lax

D = 2048
HEADS = 32
HEAD_DIM = 64
ROT_DIM = 32
FF = 8192
TOK_DEV = 1024
QBLOCK = 512
MOST_LEN = 768
TOKENS = 4096
N_ROW = 2
N_COL = 4


def doc_layout(key):
    group_count = TOKENS // TOK_DEV
    rest_len = TOK_DEV - MOST_LEN
    key_first, key_second, key_turn, key_offset = jax.random.split(key, 4)
    first_cut = jax.random.randint(key_first, (group_count,), 1, rest_len - 1).astype(jnp.int32)
    second_cut = first_cut + jax.random.randint(key_second, (group_count,), 1, rest_len - first_cut).astype(jnp.int32)
    longest = jnp.full((group_count,), MOST_LEN, jnp.int32)
    pieces = jnp.stack([longest, first_cut, second_cut - first_cut, rest_len - second_cut], axis=1).astype(jnp.int32)
    turn = jax.random.randint(key_turn, (group_count, 1), 0, 4).astype(jnp.int32)
    slot_order = (jnp.arange(4, dtype=jnp.int32)[None, :] + turn) % 4
    lengths = jnp.take_along_axis(pieces, slot_order, axis=1)
    ends = jnp.cumsum(lengths, axis=1).astype(jnp.int32)
    starts = ends - lengths
    token_at = jnp.arange(TOK_DEV, dtype=jnp.int32)
    local_doc = jnp.sum((token_at[None, :, None] >= ends[:, None, :]).astype(jnp.int32), axis=2).astype(jnp.int32)
    doc_start = jnp.take_along_axis(starts, local_doc, axis=1)
    random_offsets = jax.random.randint(key_offset, (group_count, 2), 0, 512).astype(jnp.int32)
    piece_offsets = jnp.concatenate([jnp.full((group_count, 1), 511, jnp.int32), jnp.zeros((group_count, 1), jnp.int32), random_offsets], axis=1).astype(jnp.int32)
    offsets = jnp.take_along_axis(piece_offsets, slot_order, axis=1)
    doc_offset = jnp.take_along_axis(offsets, local_doc, axis=1)
    segments = local_doc + 4 * jnp.arange(group_count, dtype=jnp.int32)[:, None]
    spots = token_at[None, :] - doc_start + doc_offset
    return (segments.reshape(-1).astype(jnp.int32), spots.reshape(-1).astype(jnp.int32))


def draw_segment_ids(key, part):
    shared = doc_layout(key)
    return shared[0]


def draw_positions(key, part):
    shared = doc_layout(key)
    return shared[1]


def shard_levels(own_key, shape, shards, low, high):
    def one(dim, blocks):
        draws = jax.random.uniform(jax.random.fold_in(jax.random.fold_in(own_key, 6), dim), (blocks,), jnp.float32, low / len(shards), high / len(shards))
        return jnp.repeat(jnp.exp(draws), shape[dim] // blocks).reshape((-1,) + (1,) * (len(shape) - dim - 1))

    loudness = one(*shards[0])
    for cut in shards[1:]:
        loudness = loudness * one(*cut)
    return loudness


def normal_values(key, extent, width, limit, cuts=(), kind=jnp.bfloat16):
    factor_of = shard_levels(key, extent, cuts, -0.22, 0.18) if cuts else 1.0
    values = jax.random.normal(key, extent, jnp.float32) * width * factor_of
    return jnp.minimum(jnp.maximum(values, -limit), limit).astype(kind)


def setup_inputs(seed: int = 0) -> dict:
    key_list = jax.random.split(jax.random.key(seed), 15)
    return {
        "block_input": normal_values(key_list[0], (TOKENS, D), 1.0, 6.0, ((0, 4), (1, 8))),
        "segment_ids": draw_segment_ids(jax.random.fold_in(key_list[14], 71), 0),
        "positions": draw_positions(jax.random.fold_in(key_list[14], 71), 0),
        "ln_gain": jnp.clip(1.0 + 0.1 * jax.random.normal(key_list[3], (D,), jnp.float32), 0.5, 1.5).astype(jnp.bfloat16),
        "ln_bias": normal_values(key_list[4], (D,), 0.3, 2.0, ((0, 8),)),
        "qkv_weight": normal_values(key_list[5], (D, 3, D), D ** -0.5, 0.125, ((0, 2), (2, 4))),
        "qkv_bias": normal_values(key_list[6], (3, N_COL, N_ROW, D // (N_ROW * N_COL)), 0.3, 2.0, ((1, 4), (2, 2)), jnp.float32),
        "dense_weight": normal_values(key_list[7], (D, D), (max(D // 128, 1)) ** -0.5, 1.5, ((0, 4), (1, 2))),
        "dense_bias": normal_values(key_list[8], (D,), 0.3, 2.0, ((0, 8),), jnp.float32),
        "fc1_weight": normal_values(key_list[9], (D, FF), D ** -0.5, 0.125, ((0, 2), (1, 4))),
        "fc1_bias": normal_values(key_list[10], (N_COL, N_ROW, FF // (N_ROW * N_COL)), 0.3, 2.0, ((0, 4), (1, 2)), jnp.float32),
        "fc2_weight": normal_values(key_list[11], (FF, D), FF ** -0.5, 0.0625, ((0, 4), (1, 2))),
        "fc2_bias": normal_values(key_list[12], (D,), 0.3, 2.0, ((0, 8),), jnp.float32),
        "cotangent": normal_values(key_list[13], (TOKENS, D), 1.0, 6.0, ((0, 4), (1, 8))),
    }


@jax.custom_vjp
def low(v):
    return lax.optimization_barrier(v.astype(jnp.bfloat16)).astype(jnp.float32)

@jax.custom_vjp
def low_back(v):
    return v

def low_keep(v):
    return (low(v), None)

def low_pass(kept, grad):
    return (grad,)

def back_keep(v):
    return (v, None)

def back_low(kept, grad):
    return (low(grad),)
low.defvjp(low_keep, low_pass)
low_back.defvjp(back_keep, back_low)
NORM_EPSILON = 1e-05
MASKED_SCORE = -1e+30
HIGHEST_DOT = lax.Precision.HIGHEST

def rotary(vectors, positions):
    half_dim = ROT_DIM // 2
    steps_float = jnp.arange(half_dim).astype(jnp.float32)
    frequency = jnp.exp(steps_float * (-2.0 * math.log(10000.0) / ROT_DIM))
    angles = positions.astype(jnp.float32)[:, None] * frequency[None, :]
    cosine = jnp.cos(angles)[:, None, :]
    sine_part = jnp.sin(angles)[:, None, :]
    first_half = vectors[..., :half_dim]
    second_half = vectors[..., half_dim:ROT_DIM]
    rest_dims = vectors[..., ROT_DIM:]
    return jnp.concatenate([first_half * cosine - second_half * sine_part, second_half * cosine + first_half * sine_part, rest_dims], axis=-1)

def attend(queries, key_rows, value_rows, segments):
    tokens = queries.shape[0]
    block_rows = min(QBLOCK, tokens)
    block_count = tokens // block_rows
    score_scale = HEAD_DIM ** (-0.5)
    key_order = jnp.arange(tokens)

    def one_block(block_at):
        first_row = block_at * block_rows
        query_rows = lax.dynamic_slice_in_dim(queries, first_row, block_rows, 0)
        row_segs = lax.dynamic_slice_in_dim(segments, first_row, block_rows, 0)
        row_index = first_row + jnp.arange(block_rows)
        raw_scores = low_back(jnp.einsum('qhd,khd->hqk', query_rows, key_rows, precision=HIGHEST_DOT))
        allowed = (row_segs[:, None] == segments[None, :]) & (row_index[:, None] >= key_order[None, :])
        logits = jnp.where(allowed[None], raw_scores * score_scale, MASKED_SCORE)
        weights = jax.nn.softmax(logits, axis=-1)
        return jnp.einsum('hqk,khd->qhd', low(weights), value_rows, precision=HIGHEST_DOT)
    block_outs = lax.map(jax.checkpoint(one_block), jnp.arange(block_count))
    return block_outs.reshape(tokens, -1)

def layer(inputs, segments, positions, ln_gain, ln_bias, qkv_weight, qkv_bias, dense_weight, dense_bias, fc1_weight, fc1_bias, fc2_weight, fc2_bias):
    tokens = inputs.shape[0]
    row_mean = lax.optimization_barrier(jnp.mean(inputs, axis=-1, keepdims=True))
    centred = inputs - row_mean
    variance = lax.optimization_barrier(jnp.mean(centred * centred, axis=-1, keepdims=True))
    normed = low(centred * lax.rsqrt(variance + NORM_EPSILON) * ln_gain + ln_bias)
    mixed_all = jnp.dot(normed, qkv_weight.reshape(D, 3 * D), precision=HIGHEST_DOT) + qkv_bias.reshape(3 * D)
    mixed_all = low_back(mixed_all).reshape(tokens, 3, HEADS, HEAD_DIM)
    queries = low(rotary(mixed_all[:, 0], positions))
    key_rows = low(rotary(mixed_all[:, 1], positions))
    value_rows = low(mixed_all[:, 2])
    context = low(low_back(attend(queries, key_rows, value_rows, segments)))
    hidden_pre = low_back(jnp.dot(normed, fc1_weight, precision=HIGHEST_DOT) + fc1_bias.reshape(FF))
    hidden = low(jax.nn.gelu(hidden_pre, approximate=True))
    attn_part = jnp.dot(context, dense_weight, precision=HIGHEST_DOT)
    mlp_part = jnp.dot(hidden, fc2_weight, precision=HIGHEST_DOT)
    return inputs + attn_part + dense_bias + mlp_part + fc2_bias

def reference(block_input, segment_ids, positions, ln_gain, ln_bias, qkv_weight, qkv_bias, dense_weight, dense_bias, fc1_weight, fc1_bias, fc2_weight, fc2_bias, cotangent):
    group_count = TOKENS // TOK_DEV
    weight_list = tuple((array.astype(jnp.float32) for array in (ln_gain, ln_bias, qkv_weight, qkv_bias, dense_weight, dense_bias, fc1_weight, fc1_bias, fc2_weight, fc2_bias)))
    inputs_all = block_input.astype(jnp.float32).reshape(group_count, TOK_DEV, D)
    cot_all = cotangent.astype(jnp.float32).reshape(group_count, TOK_DEV, D)
    seg_all = segment_ids.astype(jnp.int32).reshape(group_count, TOK_DEV)
    pos_all = positions.astype(jnp.int32).reshape(group_count, TOK_DEV)

    def group_step(totals, element):
        inputs, cot_rows, segments, group_pos = element

        def forward(inputs, *weights):
            return layer(inputs, segments, group_pos, *weights)
        result, pullback = jax.vjp(forward, inputs, *weight_list)
        gradients = pullback(cot_rows)
        totals = tuple((left + right for left, right in zip(totals, gradients[1:])))
        return (totals, (result.astype(jnp.bfloat16), gradients[0]))
    zero_list = tuple((jnp.zeros(array.shape, jnp.float32) for array in weight_list))
    totals, (outputs, input_grads) = lax.scan(group_step, zero_list, (inputs_all, cot_all, seg_all, pos_all))
    return (outputs.reshape(TOKENS, D), input_grads.reshape(TOKENS, D), totals[0], totals[1], totals[2], totals[3], totals[4], totals[5], totals[6], totals[7], totals[8], totals[9] * 0.0 + totals[5])
```

```python
import functools
import math

import jax
import jax.numpy as jnp
from jax import lax
from jax.experimental import pallas as pl
from jax.experimental.pallas import tpu as pltpu
from jax.sharding import PartitionSpec as P

HEAD_DIM = 64
ROT_DIM = 32
NORM_EPSILON = 1e-05
MASKED_SCORE = -1e30
QUERY_ROWS = 256
MESH = pl.DeviceIdType.MESH
BF = jnp.bfloat16
F32 = jnp.float32


def gather_kernel(
    n_col,
    x_ref,
    cot_ref,
    gb_ref,
    wq_ref,
    w1_ref,
    w2_ref,
    wd_ref,
    xf_ref,
    cf_ref,
    gf_ref,
    qf_ref,
    f1_ref,
    f2_ref,
    df_ref,
    x_send,
    x_recv,
    g_send,
    g_recv,
    c_send,
    c_recv,
    cx_send,
    cx_recv,
    w_send,
    w_recv,
    s_send,
    s_recv,
    own_sem,
    *staged,
):
    d = lax.axis_index("dp")
    r = lax.axis_index("row")
    c = lax.axis_index("col")
    core = lax.rem(d, 2)
    sibling = d + 1 - 2 * core
    other = 1 - r
    has_right = c < n_col - 1
    has_left = c > 0
    right = jnp.minimum(c + 1, n_col - 1)
    left = jnp.maximum(c - 1, 0)
    width = x_ref.shape[1]

    def to(dd, rr, cc):
        return dict(device_id=(dd, rr, cc), device_id_type=MESH)

    barrier = pltpu.get_barrier_semaphore()
    pl.semaphore_signal(barrier, inc=1, **to(d, other, c))
    pl.semaphore_signal(barrier, inc=1, **to(sibling, r, c))

    @pl.when(has_right)
    def _():
        pl.semaphore_signal(barrier, inc=1, **to(d, r, right))

    @pl.when(has_left)
    def _():
        pl.semaphore_signal(barrier, inc=1, **to(d, r, left))

    pl.semaphore_wait(barrier, 2 + has_right.astype(jnp.int32) + has_left.astype(jnp.int32))

    def block(ref, rr, j):
        start = pl.multiple_of((rr * n_col + j) * width, width)
        return ref.at[:, pl.ds(start, width)]

    def hop(full, own, rr, j, send, recv, lane, step):
        dst = block(full, rr, j)
        src = dst if own is None else own
        cc = right if step == 0 else left
        return pltpu.make_async_remote_copy(
            src_ref=src,
            dst_ref=dst,
            send_sem=send.at[lane, step, j],
            recv_sem=recv.at[lane, j],
            **to(d, r, cc),
        )

    def across(full, own, j, send, recv):
        dst = block(full, r, j)
        return pltpu.make_async_remote_copy(
            src_ref=dst if own is None else own,
            dst_ref=dst,
            send_sem=send,
            recv_sem=recv,
            **to(d, other, c),
        )

    def arrived(full, rr, j, recv):
        dst = block(full, rr, j)
        return pltpu.make_async_remote_copy(
            src_ref=dst, dst_ref=dst, send_sem=recv, recv_sem=recv, **to(d, other, c)
        )

    def start_both(full, own, rr, send, recv, lane):
        @pl.when(has_right)
        def _():
            hop(full, own, rr, c, send, recv, lane, 0).start()

        @pl.when(has_left)
        def _():
            hop(full, own, rr, c, send, recv, lane, 1).start()

    def advance(full, rr, send, recv, lane, s, then=None):
        @pl.when(c >= s)
        def _():
            j = c - s
            arrived(full, rr, j, recv.at[lane, j]).wait_recv()

            @pl.when(has_right)
            def _():
                hop(full, None, rr, j, send, recv, lane, 0).start()

            if then is not None:
                then(j)

        @pl.when(c + s < n_col)
        def _():
            j = c + s
            arrived(full, rr, j, recv.at[lane, j]).wait_recv()

            @pl.when(has_left)
            def _():
                hop(full, None, rr, j, send, recv, lane, 1).start()

            if then is not None:
                then(j)

    def drain(full, rr, send, recv, lane):
        for s in range(n_col):

            @pl.when((c >= s) & has_right)
            def _():
                hop(full, None, rr, jnp.maximum(c - s, 0), send, recv, lane, 0).wait_send()

            @pl.when((c + s < n_col) & has_left)
            def _():
                j = jnp.minimum(c + s, n_col - 1)
                hop(full, None, rr, j, send, recv, lane, 1).wait_send()

    def pieces(k, rr):
        out = []
        depth = wq_ref.shape[1] // 2
        part = wq_ref.shape[2] // 2
        for s in range(3):
            out.append(
                (
                    wq_ref.at[s, pl.ds(k * depth, depth), pl.ds((1 - rr) * part, part)],
                    qf_ref.at[pl.ds(rr * 2 * depth + k * depth, depth), pl.ds(s * part, part)],
                )
            )
        depth = w1_ref.shape[0] // 2
        part = w1_ref.shape[1] // 2
        out.append(
            (
                w1_ref.at[pl.ds(k * depth, depth), pl.ds((1 - rr) * part, part)],
                f1_ref.at[pl.ds(rr * 2 * depth + k * depth, depth), :],
            )
        )
        half = w2_ref.shape[0] // 2
        depth = half // 2
        part = w2_ref.shape[1]
        out.append(
            (
                w2_ref.at[pl.ds((1 - rr) * half + k * depth, depth), :],
                f2_ref.at[pl.ds(k * depth, depth), pl.ds(rr * part, part)],
            )
        )
        half = wd_ref.shape[0] // 2
        depth = half // 2
        part = wd_ref.shape[1]
        out.append(
            (
                wd_ref.at[pl.ds((1 - rr) * half + k * depth, depth), :],
                df_ref.at[pl.ds(k * depth, depth), pl.ds(rr * part, part)],
            )
        )
        return out

    n_piece = 6

    def weight_across(i):
        src, dst = pieces(core, r)[i]
        return pltpu.make_async_remote_copy(
            src_ref=src, dst_ref=dst, send_sem=w_send.at[i], recv_sem=w_recv.at[i], **to(d, other, c)
        )

    def weight_landed(i):
        dst = pieces(core, other)[i][1]
        return pltpu.make_async_remote_copy(
            src_ref=dst, dst_ref=dst, send_sem=w_send.at[i], recv_sem=w_recv.at[i], **to(d, other, c)
        )

    def weight_share(i):
        dst = pieces(core, other)[i][1]
        return pltpu.make_async_remote_copy(
            src_ref=dst, dst_ref=dst, send_sem=s_send.at[i], recv_sem=s_recv.at[i], **to(sibling, r, c)
        )

    def weight_shared(i):
        dst = pieces(1 - core, other)[i][1]
        return pltpu.make_async_remote_copy(
            src_ref=dst, dst_ref=dst, send_sem=s_send.at[i], recv_sem=s_recv.at[i], **to(sibling, r, c)
        )

    part = wq_ref.shape[2] // 2
    depth = wq_ref.shape[1]
    own = [(x_ref, block(xf_ref, r, c)), (cot_ref, block(cf_ref, r, c)), (gb_ref, block(gf_ref, r, c))]
    for s in range(3):
        own.append(
            (
                wq_ref.at[s, :, pl.ds(r * part, part)],
                qf_ref.at[pl.ds(r * depth, depth), pl.ds(s * part, part)],
            )
        )
    depth = w1_ref.shape[0]
    part = w1_ref.shape[1] // 2
    own.append((w1_ref.at[:, pl.ds(r * part, part)], f1_ref.at[pl.ds(r * depth, depth), :]))
    for src, dst in ((w2_ref, f2_ref), (wd_ref, df_ref)):
        depth = src.shape[0] // 2
        part = src.shape[1]
        own.append((src.at[pl.ds(r * depth, depth), :], dst.at[:, pl.ds(r * part, part)]))
    own_in = [pltpu.make_async_copy(a, v, own_sem.at[0, i]) for i, ((a, b), v) in enumerate(zip(own, staged))]
    own_out = [pltpu.make_async_copy(v, b, own_sem.at[1, i]) for i, ((a, b), v) in enumerate(zip(own, staged))]

    gb_across = across(gf_ref, gb_ref, c, g_send.at[1, 2, c], g_recv.at[1, c])
    x_across = across(xf_ref, x_ref, c, x_send.at[1, 2, c], x_recv.at[1, c])
    gb_across.start()
    x_across.start()
    start_both(gf_ref, gb_ref, r, g_send, g_recv, 0)
    start_both(xf_ref, x_ref, r, x_send, x_recv, 0)
    for copy in own_in:
        copy.start()

    for arrive, leave in zip(own_in, own_out):
        arrive.wait()
        leave.start()

    arrived(gf_ref, other, c, g_recv.at[1, c]).wait_recv()
    start_both(gf_ref, None, other, g_send, g_recv, 1)
    arrived(xf_ref, other, c, x_recv.at[1, c]).wait_recv()
    start_both(xf_ref, None, other, x_send, x_recv, 1)
    cot_across = lambda j: across(cf_ref, None, j, cx_send.at[j], cx_recv.at[j])
    across(cf_ref, cot_ref, c, cx_send.at[c], cx_recv.at[c]).start()
    for i in range(n_piece):
        weight_across(i).start()
    start_both(cf_ref, cot_ref, r, c_send, c_recv, 0)
    for s in range(1, n_col):
        for lane in range(2):
            rr = r if lane == 0 else other
            advance(gf_ref, rr, g_send, g_recv, lane, s)
            advance(xf_ref, rr, x_send, x_recv, lane, s)
        advance(cf_ref, r, c_send, c_recv, 0, s, then=lambda j: cot_across(j).start())
    for i in range(n_piece):
        weight_landed(i).wait_recv()
        weight_share(i).start()
    for s in range(n_col):
        arrived(cf_ref, other, s, cx_recv.at[s]).wait_recv()
        cot_across(s).wait_send()
    for i in range(n_piece):
        weight_shared(i).wait_recv()
        weight_across(i).wait_send()
        weight_share(i).wait_send()
    for lane in range(2):
        rr = r if lane == 0 else other
        drain(gf_ref, rr, g_send, g_recv, lane)
        drain(xf_ref, rr, x_send, x_recv, lane)
    drain(cf_ref, r, c_send, c_recv, 0)
    gb_across.wait_send()
    x_across.wait_send()
    for copy in own_out:
        copy.wait()


def gather_all(n_row, n_col, x, cot, gb, wq, w1, w2, wd):
    tokens, width = x.shape
    full = width * n_row * n_col
    hbm = pl.BlockSpec(memory_space=pl.ANY)
    dma = pltpu.SemaphoreType.DMA
    shapes = (
        ((tokens, full), BF),
        ((tokens, full), BF),
        ((gb.shape[0], full), F32),
        ((wq.shape[1] * n_row, 3 * wq.shape[2] // n_row), BF),
        ((w1.shape[0] * n_row, w1.shape[1] // n_row), BF),
        ((w2.shape[0] // n_row, w2.shape[1] * n_row), BF),
        ((wd.shape[0] // n_row, wd.shape[1] * n_row), BF),
    )
    return pl.pallas_call(
        functools.partial(gather_kernel, n_col),
        out_shape=tuple(jax.ShapeDtypeStruct(s, t) for s, t in shapes),
        in_specs=[hbm] * 7,
        out_specs=(hbm,) * 7,
        scratch_shapes=[
            dma((2, 3, n_col)),
            dma((2, n_col)),
            dma((2, 3, n_col)),
            dma((2, n_col)),
            dma((1, 2, n_col)),
            dma((1, n_col)),
            dma((n_col,)),
            dma((n_col,)),
            dma((6,)),
            dma((6,)),
            dma((6,)),
            dma((6,)),
            dma((2, 9)),
            pltpu.VMEM(x.shape, BF),
            pltpu.VMEM(cot.shape, BF),
            pltpu.VMEM(gb.shape, F32),
        ]
        + [pltpu.VMEM((wq.shape[1], wq.shape[2] // n_row), BF)] * 3
        + [
            pltpu.VMEM((w1.shape[0], w1.shape[1] // n_row), BF),
            pltpu.VMEM((w2.shape[0] // n_row, w2.shape[1]), BF),
            pltpu.VMEM((wd.shape[0] // n_row, wd.shape[1]), BF),
        ],
        compiler_params=pltpu.CompilerParams(
            collective_id=0, has_side_effects=True, vmem_limit_bytes=24 * 2**20
        ),
        cost_estimate=pl.CostEstimate(flops=0, bytes_accessed=300 * 2**20, transcendentals=0),
    )(x, cot, gb, wq, w1, w2, wd)


def attention_kernel(
    mixed_ref,
    grad_ref,
    cos_ref,
    sin_ref,
    seg_col_ref,
    seg_row_ref,
    ctx_ref,
    out_ref,
    q_s,
    k_s,
    v_s,
    dk_s,
    dv_s,
    bias_s,
    *,
    query_rows,
):
    tokens, width = grad_ref.shape
    pairs = width // 128
    scale = HEAD_DIM**-0.5
    lane = lax.broadcasted_iota(jnp.int32, (1, 128), 1)
    first = lane % HEAD_DIM < ROT_DIM // 2
    low_head = lane < HEAD_DIM
    contract_last = (((1,), (1,)), ((), ()))
    contract_first = (((0,), (0,)), ((), ()))

    def turn(v, cos, sin, sign):
        up = pltpu.roll(v, 128 - ROT_DIM // 2, 1)
        down = pltpu.roll(v, ROT_DIM // 2, 1)
        swapped = jnp.where(first, -up, down) * sin
        return v * cos + swapped if sign > 0 else v * cos - swapped

    for t in range(pairs):
        cos, sin = cos_ref[...], sin_ref[...]
        at = slice(t * 128, (t + 1) * 128)
        q_s[t] = turn(mixed_ref[0, :, at], cos, sin, 1).astype(BF)
        k_s[t] = turn(mixed_ref[1, :, at], cos, sin, 1).astype(BF)
        v_s[t] = mixed_ref[2, :, at].astype(BF)
    dk_s[...] = jnp.zeros_like(dk_s)
    dv_s[...] = jnp.zeros_like(dv_s)
    for i in range(tokens // query_rows):
        keys = (i + 1) * query_rows
        rows = slice(i * query_rows, keys)
        row_at = lax.broadcasted_iota(jnp.int32, (query_rows, keys), 0) + i * query_rows
        key_at = lax.broadcasted_iota(jnp.int32, (query_rows, keys), 1)
        allowed = (seg_col_ref[rows, :] == seg_row_ref[:, :keys]) & (row_at >= key_at)
        bias_s[:, :keys] = jnp.where(allowed, 0.0, MASKED_SCORE)

        def pair(t, carry):
            at = pl.ds(pl.multiple_of(t * 128, 128), 128)
            q, k, v = q_s[t, rows, :], k_s[t, :keys, :], v_s[t, :keys, :]
            grad = grad_ref[rows, at]
            outs, query_grads = [], []
            for h in range(2):
                mine = low_head if h == 0 else ~low_head
                qh = jnp.where(mine, q, jnp.zeros_like(q))
                gh = jnp.where(mine, grad, jnp.zeros_like(grad))
                s = lax.dot_general(qh, k, contract_last, preferred_element_type=F32)
                s = s * scale + bias_s[:, :keys]
                e = jnp.exp(s - jnp.max(s, axis=1, keepdims=True))
                p = e * (1.0 / jnp.sum(e, axis=1, keepdims=True))
                low = p.astype(BF)
                outs.append(jnp.dot(low, v, preferred_element_type=F32))
                dp = lax.dot_general(gh, v, contract_last, preferred_element_type=F32)
                centre = jnp.sum(p * dp, axis=1, keepdims=True)
                ds = (p * (dp - centre) * scale).astype(BF)
                query_grads.append(jnp.dot(ds, k, preferred_element_type=F32))
                dk_s[t, :keys, :] += lax.dot_general(
                    ds, qh, contract_first, preferred_element_type=F32
                )
                dv_s[t, :keys, :] += lax.dot_general(
                    low, gh, contract_first, preferred_element_type=F32
                )
            ctx_ref[rows, at] = jnp.where(low_head, outs[0], outs[1]).astype(BF)
            dq = jnp.where(low_head, query_grads[0], query_grads[1])
            out_ref[rows, at] = turn(dq, cos_ref[rows, :], sin_ref[rows, :], -1).astype(BF)
            return carry

        lax.fori_loop(0, pairs, pair, 0)
    for t in range(pairs):
        at = width + t * 128
        out_ref[:, at : at + 128] = turn(dk_s[t], cos_ref[...], sin_ref[...], -1).astype(BF)
        at = 2 * width + t * 128
        out_ref[:, at : at + 128] = dv_s[t].astype(BF)


def attention(mixed, context_grad, cos, sin, segments):
    tokens, width = context_grad.shape
    pairs = width // 128
    vmem = pl.BlockSpec(memory_space=pltpu.VMEM)
    return pl.pallas_call(
        functools.partial(attention_kernel, query_rows=min(QUERY_ROWS, tokens)),
        out_shape=(
            jax.ShapeDtypeStruct((tokens, width), BF),
            jax.ShapeDtypeStruct((tokens, 3 * width), BF),
        ),
        in_specs=[vmem] * 6,
        out_specs=(vmem, vmem),
        scratch_shapes=[pltpu.VMEM((pairs, tokens, 128), BF)] * 3
        + [pltpu.VMEM((pairs, tokens, 128), F32)] * 2
        + [pltpu.VMEM((min(QUERY_ROWS, tokens), tokens), F32)],
        compiler_params=pltpu.CompilerParams(
            vmem_limit_bytes=56 * 2**20, fuse_transposed_lhs_in_matmul=True
        ),
        cost_estimate=pl.CostEstimate(
            flops=2 * 10**10, bytes_accessed=64 * 2**20, transcendentals=3 * 2**20
        ),
    )(mixed, context_grad, cos, sin, segments.reshape(tokens, 1), segments.reshape(1, tokens))


def rotation_tables(positions):
    half = ROT_DIM // 2
    steps = jnp.arange(half).astype(F32)
    frequency = jnp.exp(steps * (-2.0 * math.log(10000.0) / ROT_DIM))
    angles = positions.astype(F32)[:, None] * frequency[None, :]
    cos, sin = jnp.cos(angles), jnp.sin(angles)
    rest = (positions.shape[0], HEAD_DIM - ROT_DIM)
    return (
        jnp.concatenate([cos, cos, jnp.ones(rest, F32)] * (128 // HEAD_DIM), axis=1),
        jnp.concatenate([sin, sin, jnp.zeros(rest, F32)] * (128 // HEAD_DIM), axis=1),
    )


def swap_row(value):
    return lax.ppermute(value, "row", [(0, 1), (1, 0)])


def swap_dp(value, bit):
    n = lax.axis_size("dp")
    return lax.ppermute(value, "dp", [(i, i ^ (1 << bit)) for i in range(n)])


def dp_bits():
    return lax.axis_size("dp").bit_length() - 1


def take(value, at):
    return lax.dynamic_index_in_dim(value, at, 1, keepdims=False)


def reduce_dp(grad):
    n = lax.axis_size("dp")
    d = lax.axis_index("dp")
    width = grad.shape[1]
    rows = grad.shape[0] // n
    cur = grad
    for bit in range(dp_bits()):
        mine = (d >> bit) & 1
        left = n >> (bit + 1)
        parts = cur.reshape(left, 2, rows, width)
        got = swap_dp(take(parts, 1 - mine).astype(BF), bit)
        cur = (take(parts, mine) + got.astype(F32)).reshape(-1, width)
    return cur


def spread_dp(pieces):
    everyone = [pieces]
    for bit in reversed(range(dp_bits())):
        got = [[swap_dp(p, bit) for p in ps] for ps in everyone]
        everyone = everyone + got
    return everyone


def spread_order():
    order = [0]
    for bit in reversed(range(dp_bits())):
        order = order + [o ^ (1 << bit) for o in order]
    return order


def sum_all_dp(value):
    for bit in range(dp_bits()):
        value = value + swap_dp(value, bit)
    return value


def scatter_group(mine, theirs):
    n_col = lax.axis_size("col")
    c = lax.axis_index("col")
    total = mine + swap_row(theirs.astype(BF)).astype(F32)
    width = total.shape[1] // n_col

    def chunk(shift):
        at = lax.rem(c + shift, n_col) * width
        return lax.dynamic_slice_in_dim(total, at, width, 1)

    got = [
        lax.ppermute(
            chunk(s).astype(BF), "col", [(i, (i + s) % n_col) for i in range(n_col)]
        ).astype(F32)
        for s in range(1, n_col)
    ]
    out = chunk(0)
    for g in got:
        out = out + g
    return out


def local(
    block_input,
    segment_ids,
    positions,
    ln_gain,
    ln_bias,
    qkv_weight,
    qkv_bias,
    dense_weight,
    dense_bias,
    fc1_weight,
    fc1_bias,
    fc2_weight,
    fc2_bias,
    cotangent,
):
    n_row = lax.axis_size("row")
    n_col = lax.axis_size("col")
    n_dp = lax.axis_size("dp")
    r = lax.axis_index("row")
    c = lax.axis_index("col")
    d = lax.axis_index("dp")
    tokens, part_width = block_input.shape
    full_width = part_width * n_row * n_col
    half_width = full_width // n_row
    mine_at = r * half_width
    theirs_at = (1 - r) * half_width

    gb = jnp.concatenate(
        [
            jnp.broadcast_to(ln_gain.astype(F32)[None], (8, part_width)),
            jnp.broadcast_to(ln_bias.astype(F32)[None], (8, part_width)),
        ],
        axis=0,
    )
    whole, cot, gb_full, wq, w1, w2, wd = gather_all(
        n_row,
        n_col,
        block_input,
        cotangent,
        gb,
        jnp.transpose(qkv_weight, (1, 0, 2)),
        fc1_weight,
        fc2_weight,
        dense_weight,
    )
    gain = gb_full[0:1]
    shift = gb_full[8:9]
    whole_f = whole.astype(F32)
    row_mean = jnp.mean(whole_f, axis=-1, keepdims=True)
    variance = jnp.mean(jnp.square(whole_f - row_mean), axis=-1, keepdims=True)
    inv_std = lax.rsqrt(variance + NORM_EPSILON)
    normed = ((whole_f - row_mean) * inv_std * gain + shift).astype(BF)

    def dot(a, b, dims):
        return lax.dot_general(a, b, (dims, ((), ())), preferred_element_type=F32)

    nn = ((1,), (0,))
    nt = ((1,), (1,))
    tn = ((0,), (0,))

    def cols(a, at, size):
        return lax.dynamic_slice_in_dim(a, at, size, 1)

    def rows(a, at, size):
        return lax.dynamic_slice_in_dim(a, at, size, 0)

    head_width = wq.shape[1] // 3
    bias3 = qkv_bias.reshape(3, head_width)
    mixed = jnp.stack(
        [
            dot(normed, wq[:, s * head_width : (s + 1) * head_width], nn) + bias3[s][None]
            for s in range(3)
        ]
    )
    context_grad = dot(cot, wd, nt).astype(BF)
    hidden_grad = dot(cot, w2, nt)
    hidden_pre = dot(normed, w1, nn) + fc1_bias.reshape(1, -1)
    hidden_f, pull = jax.vjp(lambda v: jax.nn.gelu(v, approximate=True), hidden_pre)
    hidden = hidden_f.astype(BF)
    pre_grad = pull(hidden_grad)[0].astype(BF)

    def pair_grads(make):
        mine, theirs = make(mine_at), make(theirs_at)
        mine_sum = reduce_dp(mine).astype(BF)
        theirs_sum = reduce_dp(theirs).astype(BF)
        return mine_sum, swap_row(theirs_sum)

    fc2_pieces = pair_grads(lambda at: dot(hidden, cols(cot, at, half_width), tn))
    fc1_pieces = pair_grads(lambda at: dot(cols(normed, at, half_width), pre_grad, tn))

    cos, sin = rotation_tables(positions)
    context, mixed_grad = attention(mixed, context_grad, cos, sin, segment_ids)

    dense_pieces = pair_grads(lambda at: dot(context, cols(cot, at, half_width), tn))
    qkv_pieces = pair_grads(lambda at: dot(cols(normed, at, half_width), mixed_grad, tn))

    def out_part(at):
        return dot(context, cols(wd, at, half_width), nn) + dot(hidden, cols(w2, at, half_width), nn)

    summed_out = scatter_group(out_part(mine_at), out_part(theirs_at))
    block_output = (
        block_input.astype(F32) + summed_out + dense_bias[None] + fc2_bias[None]
    ).astype(BF)

    def normed_part(at):
        return dot(mixed_grad, rows(wq, at, half_width), nt) + dot(
            pre_grad, rows(w1, at, half_width), nt
        )

    part_mine, part_theirs = normed_part(mine_at), normed_part(theirs_at)

    def feature_sums(part, at):
        scaled = part * cols(gain, at, half_width)
        centred = (cols(whole, at, half_width).astype(F32) - row_mean) * inv_std
        return jnp.stack([jnp.sum(scaled, axis=-1), jnp.sum(scaled * centred, axis=-1)])

    totals = feature_sums(part_mine, mine_at) + feature_sums(part_theirs, theirs_at)
    totals = totals + swap_row(totals)
    gathered = [
        lax.ppermute(totals, "col", [(i, (i + s) % n_col) for i in range(n_col)])
        for s in range(1, n_col)
    ]
    for g in gathered:
        totals = totals + g
    normed_grad = scatter_group(part_mine, part_theirs)
    scaled_here = (block_input.astype(F32) - row_mean) * inv_std
    scaled_grad = normed_grad * ln_gain.astype(F32)[None]
    cot_float = cotangent.astype(F32)
    input_grad = cot_float + inv_std * (
        scaled_grad
        - totals[0][:, None] / full_width
        - scaled_here * totals[1][:, None] / full_width
    )
    small = jnp.concatenate(
        [
            jnp.sum(mixed_grad.astype(F32), axis=0),
            jnp.sum(pre_grad.astype(F32), axis=0),
            jnp.sum(cot_float, axis=0),
            jnp.sum(normed_grad * scaled_here, axis=0),
            jnp.sum(normed_grad, axis=0),
        ]
    )
    small = sum_all_dp(small)
    n_mixed, n_pre = mixed_grad.shape[1], pre_grad.shape[1]
    qkv_bias_grad = small[:n_mixed].reshape(qkv_bias.shape)
    fc1_bias_grad = small[n_mixed : n_mixed + n_pre].reshape(fc1_bias.shape)
    at = n_mixed + n_pre
    bias_grad, gain_grad, shift_grad = (
        small[at + i * part_width : at + (i + 1) * part_width] for i in range(3)
    )

    order = spread_order()

    def assemble(pieces, place, shape):
        everyone = spread_dp(list(pieces))
        out = jnp.zeros(shape, F32)
        for m, ps in zip(order, everyone):
            q = jnp.bitwise_xor(d, m)
            for rr, piece in ((r, ps[0]), (1 - r, ps[1])):
                out = place(out, piece.astype(F32), q, rr)
        return out

    def put(out, piece, *at):
        return lax.dynamic_update_slice(out, piece, at)

    def place_in(out, piece, q, rr):
        m, w = piece.shape
        return put(out, piece, q * m, rr * w)

    def place_out(out, piece, q, rr):
        m, w = piece.shape
        return put(out, piece, rr * m * n_dp + q * m, 0)

    def place_qkv(out, piece, q, rr):
        m, w = piece.shape
        for s in range(3):
            out = put(
                out, piece[:, s * head_width : (s + 1) * head_width][None], s, q * m, rr * head_width
            )
        return out

    fc2_grad = assemble(fc2_pieces, place_out, fc2_weight.shape)
    fc1_grad = assemble(fc1_pieces, place_in, fc1_weight.shape)
    dense_grad = assemble(dense_pieces, place_out, dense_weight.shape)
    shape = (3, qkv_weight.shape[0], qkv_weight.shape[2])
    qkv_grad = jnp.transpose(assemble(qkv_pieces, place_qkv, shape), (1, 0, 2))
    return (
        block_output,
        input_grad,
        gain_grad,
        shift_grad,
        qkv_grad,
        qkv_bias_grad,
        dense_grad,
        bias_grad,
        fc1_grad,
        fc1_bias_grad,
        fc2_grad,
        bias_grad,
    )


def solution(mesh):
    return jax.shard_map(
        local,
        mesh=mesh,
        in_specs=(
            P("dp", ("row", "col")),
            P("dp"),
            P("dp"),
            P(("row", "col")),
            P(("row", "col")),
            P("row", None, "col"),
            P(None, "col", "row", None),
            P("col", "row"),
            P(("row", "col")),
            P("row", "col"),
            P("col", "row", None),
            P("col", "row"),
            P(("row", "col")),
            P("dp", ("row", "col")),
        ),
        out_specs=(
            P("dp", ("row", "col")),
            P("dp", ("row", "col")),
            P(("row", "col")),
            P(("row", "col")),
            P("row", None, "col"),
            P(None, "col", "row", None),
            P("col", "row"),
            P(("row", "col")),
            P("row", "col"),
            P("col", "row", None),
            P("col", "row"),
            P(("row", "col")),
        ),
        check_vma=False,
    )
```

```python
import functools
import math

import jax
import jax.numpy as jnp
import numpy as np
from jax import lax
from jax.experimental import pallas as pl
from jax.experimental.pallas import tpu as pltpu
from jax.sharding import PartitionSpec as P

HEAD_DIM = 64
ROT_DIM = 32
NORM_EPSILON = 1e-05
MASKED_SCORE = -1e30
BLOCK = 256
MESH = pl.DeviceIdType.MESH
BF = jnp.bfloat16
F32 = jnp.float32
GELU_A = math.sqrt(2.0 / math.pi)
GELU_B = 0.044715
NN = (((1,), (0,)), ((), ()))
NT = (((1,), (1,)), ((), ()))
TN = (((0,), (0,)), ((), ()))


def dot(a, b, dims):
    return lax.dot_general(a, b, dims, preferred_element_type=F32)


def kernel(n_dp, n_col, *refs):
    names = (
        "x", "cot", "wq", "w1", "w2", "wd", "gb", "places", "seg_row", "freq", "qkv_bias",
        "fc1_bias", "out_bias", "gain_own", "y_out", "in_grad", "small", "f1", "f2", "fd", "fq",
        "rb1", "rb2", "rbd", "rbq", "rzo", "rzn", "xf", "cf", "gf", "wqf", "w1f",
        "w2f", "wdf", "normed", "hidden", "pg", "q", "k", "v", "dk", "dv", "bias", "cos", "sin",
        "ctx", "dctx", "mg", "lse", "g1", "g2", "gd", "gq", "stage1", "staged", "stageq", "stagez",
        "mean", "rstd", "tot", "small_v", "small_r", "x_send", "x_recv", "g_send", "g_recv",
        "c_send", "c_recv", "cx_send", "cx_recv", "w_send", "w_recv", "y_send", "y_recv",
        "s_send", "s_recv", "load_sem", "rs_send", "rs_recv", "xs_send", "xs_recv", "ag_send", "ag_recv", "part_sem",
        "stage_sem", "ox_send", "ox_recv", "oz_send", "oz_recv", "tot_send", "tot_recv", "sm_send",
        "sm_recv", "free_sem",
    )
    ns = dict(zip(names, refs, strict=True))
    (x_ref, cot_ref, wq_ref, w1_ref, w2_ref, wd_ref, gb_ref) = refs[:7]
    xf, cf, gf = ns["xf"], ns["cf"], ns["gf"]
    wqf, w1f, w2f, wdf = ns["wqf"], ns["w1f"], ns["w2f"], ns["wdf"]
    normed, hidden, pg = ns["normed"], ns["hidden"], ns["pg"]
    q_s, k_s, v_s, dk_s, dv_s = (ns[n] for n in ("q", "k", "v", "dk", "dv"))
    ctx, dctx, mg, lse = ns["ctx"], ns["dctx"], ns["mg"], ns["lse"]
    cos_ref, sin_ref, bias_s = ns["cos"], ns["sin"], ns["bias"]
    load_sem, stage_sem = ns["load_sem"], ns["stage_sem"]

    d = lax.axis_index("dp")
    r = lax.axis_index("row")
    c = lax.axis_index("col")
    n_bits = n_dp.bit_length() - 1
    core = lax.rem(d, 2)
    sibling = d + 1 - 2 * core
    other = 1 - r
    has_right = c < n_col - 1
    has_left = c > 0
    right = jnp.minimum(c + 1, n_col - 1)
    left = jnp.maximum(c - 1, 0)
    tokens, width = x_ref.shape
    full = width * n_col * 2
    half = full // 2
    heads_w = qw = ctx.shape[1]
    pairs = heads_w // 128
    n_blocks = tokens // BLOCK
    scale = HEAD_DIM**-0.5

    def to(dd, rr, cc):
        return dict(device_id=(dd, rr, cc), device_id_type=MESH)

    def bit(b):
        return lax.rem(lax.div(d, 1 << b), 2)

    def peer(b):
        return d + (1 - 2 * bit(b)) * (1 << b)

    def remote(src, dst, send, recv, dev):
        return pltpu.make_async_remote_copy(
            src_ref=src, dst_ref=dst, send_sem=send, recv_sem=recv, **dev
        )

    def at(start, size):
        return pl.ds(pl.multiple_of(start, math.gcd(size, 256)), size)

    across = to(d, other, c)

    barrier = pltpu.get_barrier_semaphore()
    pl.semaphore_signal(barrier, inc=1, **across)
    for s in range(1, n_col):
        pl.semaphore_signal(barrier, inc=1, **to(d, r, lax.rem(c + s, n_col)))
    for b in range(n_bits):
        pl.semaphore_signal(barrier, inc=1, **to(peer(b), r, c))
    pl.semaphore_wait(barrier, 1 + (n_col - 1) + n_bits)

    def block(ref, rr, j):
        return ref.at[:, at((rr * n_col + j) * width, width)]

    def hop(whole, own, rr, j, send, recv, lane, step):
        dst = block(whole, rr, j)
        return remote(
            dst if own is None else own,
            dst,
            send.at[lane, step, j],
            recv.at[lane, j],
            to(d, r, right if step == 0 else left),
        )

    def over(whole, own, j, send, recv):
        dst = block(whole, r, j)
        return remote(dst if own is None else own, dst, send, recv, across)

    def landed(dst, recv):
        return remote(dst, dst, recv, recv, across)

    def start_hop(cond, whole, own, rr, j, send, recv, lane, step):
        @pl.when(cond)
        def _():
            hop(whole, own, rr, j, send, recv, lane, step).start()

    def start_both(whole, own, rr, send, recv, lane):
        start_hop(has_right, whole, own, rr, c, send, recv, lane, 0)
        start_hop(has_left, whole, own, rr, c, send, recv, lane, 1)

    def advance(whole, rr, send, recv, lane, s, then=None):
        @pl.when(c >= s)
        def _():
            j = c - s
            landed(block(whole, rr, j), recv.at[lane, j]).wait_recv()
            start_hop(has_right, whole, None, rr, j, send, recv, lane, 0)
            if then is not None:
                then(j)

        @pl.when(c + s < n_col)
        def _():
            j = c + s
            landed(block(whole, rr, j), recv.at[lane, j]).wait_recv()
            start_hop(has_left, whole, None, rr, j, send, recv, lane, 1)
            if then is not None:
                then(j)

    def drain(whole, rr, send, recv, lane):
        for s in range(n_col):

            @pl.when((c >= s) & has_right)
            def _():
                hop(whole, None, rr, jnp.maximum(c - s, 0), send, recv, lane, 0).wait_send()

            @pl.when((c + s < n_col) & has_left)
            def _():
                j = jnp.minimum(c + s, n_col - 1)
                hop(whole, None, rr, j, send, recv, lane, 1).wait_send()

    def piece(i, k, rr):
        if i < 3:
            depth = wq_ref.shape[1] // 4
            return (
                wq_ref.at[i, at(k * depth, depth), at((1 - rr) * qw, qw)],
                wqf.at[at((rr * 4 + k) * depth, depth), i * qw : (i + 1) * qw],
            )
        if i == 3:
            depth, part = w1_ref.shape[0] // 4, w1_ref.shape[1] // 2
            return (
                w1_ref.at[at(k * depth, depth), at((1 - rr) * part, part)],
                w1f.at[at((rr * 4 + k) * depth, depth), :],
            )
        src, dst = (w2_ref, w2f) if i == 4 else (wd_ref, wdf)
        depth, part = src.shape[0] // 8, src.shape[1]
        return (
            src.at[at(((1 - rr) * 4 + k) * depth, depth), :],
            dst.at[at(k * depth, depth), at(rr * part, part)],
        )

    w_send, w_recv, y_send, y_recv = (ns[n] for n in ("w_send", "w_recv", "y_send", "y_recv"))
    s_send, s_recv = ns["s_send"], ns["s_recv"]
    upper = bit(1)
    quarter = (core + 2 * upper, core + 2 * (1 - upper))
    quarter_sib = (1 - core + 2 * upper, 1 - core + 2 * (1 - upper))

    def weight_across(i):
        src, dst = piece(i, quarter[0], r)
        return remote(src, dst, w_send.at[i], w_recv.at[i], across)

    def weight_up(i):
        dst = piece(i, quarter[0], other)[1]
        return remote(dst, dst, y_send.at[i], y_recv.at[i], to(peer(1), r, c))

    def weight_share(i, h):
        dst = piece(i, quarter[h], other)[1]
        return remote(dst, dst, s_send.at[i, h], s_recv.at[i, h], to(sibling, r, c))

    def weights_first(group):
        for i in group:
            landed(piece(i, quarter[0], other)[1], w_recv.at[i]).wait_recv()
            weight_up(i).start()
            weight_share(i, 0).start()

    def weights_second(group):
        for i in group:
            landed(piece(i, quarter[1], other)[1], y_recv.at[i]).wait_recv()
            weight_share(i, 1).start()

    def weights_wait(group):
        for i in group:
            for h in range(2):
                landed(piece(i, quarter_sib[h], other)[1], s_recv.at[i, h]).wait_recv()

    x_send, x_recv, g_send, g_recv = (ns[n] for n in ("x_send", "x_recv", "g_send", "g_recv"))
    c_send, c_recv, cx_send, cx_recv = (ns[n] for n in ("c_send", "c_recv", "cx_send", "cx_recv"))
    gb_over = over(gf, gb_ref, c, g_send.at[1, 2, c], g_recv.at[1, c])
    x_over = over(xf, x_ref, c, x_send.at[1, 2, c], x_recv.at[1, c])
    gb_over.start()
    x_over.start()
    start_both(gf, gb_ref, r, g_send, g_recv, 0)
    start_both(xf, x_ref, r, x_send, x_recv, 0)

    own = [(x_ref, block(xf, r, c)), (gb_ref, block(gf, r, c)), (cot_ref, block(cf, r, c))]
    depth = wq_ref.shape[1]
    for s in range(3):
        own.append((wq_ref.at[s, :, at(r * qw, qw)], wqf.at[at(r * depth, depth), s * qw : (s + 1) * qw]))
    depth, part = w1_ref.shape[0], w1_ref.shape[1] // 2
    own.append((w1_ref.at[:, at(r * part, part)], w1f.at[at(r * depth, depth), :]))
    for src, dst in ((w2_ref, w2f), (wd_ref, wdf)):
        depth, part = src.shape[0] // 2, src.shape[1]
        own.append((src.at[at(r * depth, depth), :], dst.at[:, at(r * part, part)]))
    own = [pltpu.make_async_copy(a, b, load_sem.at[i]) for i, (a, b) in enumerate(own)]
    for copy in own:
        copy.start()

    def tables(i, _):
        rows = at(i * BLOCK, BLOCK)
        angle = ns["places"][rows, 1:2].astype(F32) * ns["freq"][...]
        cos_ref[rows, :] = jnp.cos(angle)
        sin_ref[rows, :] = jnp.sin(angle)
        return 0

    landed(block(gf, other, c), g_recv.at[1, c]).wait_recv()
    start_both(gf, None, other, g_send, g_recv, 1)
    landed(block(xf, other, c), x_recv.at[1, c]).wait_recv()
    start_both(xf, None, other, x_send, x_recv, 1)
    for i in range(4):
        weight_across(i).start()

    def cot_over(j):
        return over(cf, None, j, cx_send.at[j], cx_recv.at[j])

    over(cf, cot_ref, c, cx_send.at[c], cx_recv.at[c]).start()
    for i in range(4, 6):
        weight_across(i).start()

    def start_cot(s):
        start_hop(has_right & (c == s), cf, cot_ref, r, c, c_send, c_recv, 0, 0)
        start_hop(has_left & (c == n_col - 1 - s), cf, cot_ref, r, c, c_send, c_recv, 0, 1)

    start_cot(0)
    lax.fori_loop(0, n_blocks, tables, 0)
    for s in range(1, n_col):
        for lane in range(2):
            rr = r if lane == 0 else other
            advance(gf, rr, g_send, g_recv, lane, s)
            advance(xf, rr, x_send, x_recv, lane, s)
        start_cot(s)
        if s == 1:
            weights_first(range(4))
        if s == 2:
            weights_second(range(4))
            weights_first(range(4, 6))

    def advance_cot(s):
        advance(cf, r, c_send, c_recv, 0, s, then=lambda j: cot_over(j).start())

    weights_second(range(4, 6))
    for copy in own:
        copy.wait()

    gain = gf[0:1, :]
    shift = gf[8:9, :]

    def norm_rows(i, _):
        rows = at(i * 64, 64)
        v = xf[rows, :].astype(F32)
        mu = jnp.sum(v, axis=1, keepdims=True) * (1.0 / full)
        v = v - mu
        inv = lax.rsqrt(jnp.sum(v * v, axis=1, keepdims=True) * (1.0 / full) + NORM_EPSILON)
        ns["mean"][rows, :] = mu
        ns["rstd"][rows, :] = inv
        normed[rows, :] = (v * inv * gain + shift).astype(BF)
        return 0

    lax.fori_loop(0, tokens // 64, norm_rows, 0)
    advance_cot(1)
    weights_wait(range(4))

    lane_at = lax.broadcasted_iota(jnp.int32, (1, 128), 1)
    first = lane_at % HEAD_DIM < ROT_DIM // 2
    low_head = lane_at < HEAD_DIM

    def turn(v, cos, sin, sign):
        up = pltpu.roll(v, 128 - ROT_DIM // 2, 1)
        down = pltpu.roll(v, ROT_DIM // 2, 1)
        swapped = jnp.where(first, -up, down) * sin
        return v * cos + swapped if sign > 0 else v * cos - swapped

    def qkv_rows(i, _):
        rows = at(i * BLOCK, BLOCK)
        mixed = dot(normed[rows, :], wqf[...], NN)
        cos, sin = cos_ref[rows, :], sin_ref[rows, :]
        for s, dst in enumerate((q_s, k_s, v_s)):
            for t in range(pairs):
                lanes = slice(s * qw + t * 128, s * qw + (t + 1) * 128)
                v = mixed[:, lanes] + ns["qkv_bias"][s : s + 1, t * 128 : (t + 1) * 128]
                dst[t, rows, :] = (turn(v, cos, sin, 1) if s < 2 else v).astype(BF)
        return 0

    lax.fori_loop(0, n_blocks, qkv_rows, 0)
    advance_cot(2)

    def fc1_rows(i, _):
        rows = at(i * BLOCK, BLOCK)
        for h in range(2):
            cols = slice(h * 512, (h + 1) * 512)
            v = dot(normed[rows, :], w1f[:, cols], NN) + ns["fc1_bias"][:, cols]
            th = jnp.tanh(GELU_A * (v + GELU_B * v * v * v))
            hidden[rows, cols] = (0.5 * v * (1.0 + th)).astype(BF)
            slope = 0.5 * (1.0 + th) + 0.5 * v * (1.0 - th * th) * (
                GELU_A * (1.0 + 3.0 * GELU_B * v * v)
            )
            pg[rows, cols] = slope.astype(BF)
        return 0

    lax.fori_loop(0, n_blocks, fc1_rows, 0)

    def set_bias(i):
        keys = (i + 1) * BLOCK
        rows = slice(i * BLOCK, keys)
        row_at = lax.broadcasted_iota(jnp.int32, (BLOCK, keys), 0) + i * BLOCK
        key_at = lax.broadcasted_iota(jnp.int32, (BLOCK, keys), 1)
        allowed = (ns["places"][rows, 0:1] == ns["seg_row"][:, :keys]) & (row_at >= key_at)
        bias_s[:, :keys] = jnp.where(allowed, 0.0, MASKED_SCORE)

    def mine(h, v):
        return jnp.where(low_head if h == 0 else ~low_head, v, jnp.zeros_like(v))

    def forward_block(i):
        keys = (i + 1) * BLOCK
        rows = slice(i * BLOCK, keys)
        set_bias(i)

        def pair(t, _):
            q, k, v = q_s[t, rows, :], k_s[t, :keys, :], v_s[t, :keys, :]
            outs = []
            logs = lse[rows, :]
            for h in range(2):
                s = dot(mine(h, q), k, NT) * scale + bias_s[:, :keys]
                top = jnp.max(s, axis=1, keepdims=True)
                e = jnp.exp(s - top)
                total = jnp.sum(e, axis=1, keepdims=True)
                low = (e * (1.0 / total)).astype(BF)
                outs.append(dot(low, v, NN))
                logs = jnp.where(lane_at == 2 * t + h, top + jnp.log(total), logs)
            lse[rows, :] = logs
            ctx[rows, at(t * 128, 128)] = jnp.where(low_head, outs[0], outs[1]).astype(BF)
            return 0

        lax.fori_loop(0, pairs, pair, 0)

    lse[...] = jnp.zeros_like(lse)
    for i in range(n_blocks):
        if i == n_blocks - 1:
            advance_cot(3)
        forward_block(i)
    weights_wait(range(4, 6))

    rs_send, rs_recv, xs_send, xs_recv = (ns[n] for n in ("rs_send", "rs_recv", "xs_send", "xs_recv"))
    ag_send, ag_recv, part_sem = (ns[n] for n in ("ag_send", "ag_recv", "part_sem"))
    g1, g2, gd, gq = ns["g1"], ns["g2"], ns["gd"], ns["gq"]
    tensors = dict(
        fc1=(0, g1, ns["rb1"], ns["stage1"], half),
        fc2=(1, g2, ns["rb2"], ns["stage1"], hidden.shape[1]),
        dense=(2, gd, ns["rbd"], ns["staged"], heads_w),
        qkv=(3, gq, ns["rbq"], ns["stageq"], half),
    )
    results = dict(fc1=ns["f1"], fc2=ns["f2"], dense=ns["fd"], qkv=ns["fq"])
    mine_at, theirs_at = r * half, other * half
    starts = (mine_at, theirs_at)

    def slab(ref, p, rows):
        return ref.at[p, :, rows, :] if len(ref.shape) == 4 else ref.at[p, rows, :]

    def offset(rows, upto):
        off = 0
        for b in range(upto):
            off = off + bit(b) * (rows >> (b + 1))
        return off

    def landing(rows, b):
        return slice(rows - (rows >> b), rows - (rows >> (b + 1)))

    def sum_copy(name, p, b):
        n, g, rb, _, rows = tensors[name]
        size = rows >> (b + 1)
        return remote(
            slab(g, p, at(offset(rows, b) + (1 - bit(b)) * size, size)),
            slab(rb, p, landing(rows, b)),
            rs_send.at[n, p, b],
            rs_recv.at[n, p, b],
            to(peer(b), r, c),
        )

    def place(name, rr, off, size):
        if name == "fc1":
            return ns["f1"].at[at(off, size), at(rr * hidden.shape[1], hidden.shape[1])]
        if name == "qkv":
            return ns["fq"].at[:, at(off, size), at(rr * qw, qw)]
        return results[name].at[rr, at(off, size), :]

    def kept(name, p):
        _, g, _, _, rows = tensors[name]
        size = rows >> n_bits
        off = offset(rows, n_bits)
        return slab(g, p, at(off, size)), off, size

    def part_copy(name):
        src, off, size = kept(name, 0)
        return pltpu.make_async_copy(src, place(name, r, off, size), part_sem.at[tensors[name][0]])

    def swap_copy(name):
        src, off, size = kept(name, 1)
        n = tensors[name][0]
        return remote(src, place(name, r, off, size), xs_send.at[n], xs_recv.at[n], across)

    def sum_next(name, p, b):
        n, g, rb, stage, rows = tensors[name]
        size = rows >> (b + 1)
        off = offset(rows, b + 1)
        sum_copy(name, p, b).wait_recv()
        four = len(g.shape) == 4
        chunk = min(size, 128)
        dst = stage.at[:, :size, :] if four else stage.at[:size, :]
        copy = pltpu.make_async_copy(slab(rb, p, landing(rows, b)), dst, stage_sem.at[0])
        copy.start()
        copy.wait()

        def add(i, _):
            if four:
                there = (p, slice(None), at(off + i * chunk, chunk), slice(None))
                here = (slice(None), at(i * chunk, chunk), slice(None))
            else:
                there = (p, at(off + i * chunk, chunk), slice(None))
                here = (at(i * chunk, chunk), slice(None))
            g[there] = (g[there].astype(F32) + stage[here].astype(F32)).astype(BF)
            return 0

        lax.fori_loop(0, size // chunk, add, 0)
        if b + 1 < n_bits:
            sum_copy(name, p, b + 1).start()
        elif p == 0:
            part_copy(name).start()
        else:
            swap_copy(name).start()

    def sum_rest(name):
        for p in (1, 0):
            for b in range(1, n_bits):
                sum_next(name, p, b)

    def rows_of(name, off, size):
        ref = results[name]
        return ref.at[at(off, size), :] if name == "fc1" else ref.at[:, at(off, size), :]

    def spread_copy(name, b):
        n, rows = tensors[name][0], tensors[name][4]
        ref = rows_of(name, offset(rows, b + 1), rows >> (b + 1))
        return remote(ref, ref, ag_send.at[n, b], ag_recv.at[n, b], to(peer(b), r, c))

    def spread_landed(name, b):
        n, rows = tensors[name][0], tensors[name][4]
        size = rows >> (b + 1)
        return landed(rows_of(name, offset(rows, b) + (1 - bit(b)) * size, size), ag_recv.at[n, b])

    def spread_first(name):
        _, off, size = kept(name, 0)
        part_copy(name).wait()
        landed(place(name, other, off, size), xs_recv.at[tensors[name][0]]).wait_recv()
        spread_copy(name, n_bits - 1).start()

    def spread_next(name, b):
        spread_landed(name, b).wait_recv()
        if b > 0:
            spread_copy(name, b - 1).start()

    def spread_rest(name):
        for b in reversed(range(1, n_bits)):
            spread_next(name, b)

    def finish(name):
        for b in range(n_bits):
            for p in range(2):
                sum_copy(name, p, b).wait_send()
            spread_copy(name, b).wait_send()
        swap_copy(name).wait_send()

    def fc2_grad(p):
        def body(i, _):
            cols = at(i * BLOCK, BLOCK)
            g2[p, cols, :] = dot(hidden[:, cols], cf[:, at(starts[p], half)], TN).astype(BF)
            return 0

        lax.fori_loop(0, hidden.shape[1] // BLOCK, body, 0)
        sum_copy("fc2", p, 0).start()

    def fc1_grad(p):
        def body(i, _):
            g1[p, at(i * BLOCK, BLOCK), :] = dot(
                normed[:, at(starts[p] + i * BLOCK, BLOCK)], pg[...], TN
            ).astype(BF)
            return 0

        lax.fori_loop(0, half // BLOCK, body, 0)
        sum_copy("fc1", p, 0).start()

    def dense_grad(p):
        gd[p] = dot(ctx[...], cf[:, at(starts[p], half)], TN).astype(BF)
        sum_copy("dense", p, 0).start()

    def qkv_grad(p):
        def body(i, _):
            v = dot(normed[:, at(starts[p] + i * BLOCK, BLOCK)], mg[...], TN).astype(BF)
            for s in range(3):
                gq[p, s, at(i * BLOCK, BLOCK), :] = v[:, s * qw : (s + 1) * qw]
            return 0

        lax.fori_loop(0, half // BLOCK, body, 0)
        sum_copy("qkv", p, 0).start()

    ox_send, ox_recv, oz_send, oz_recv = (ns[n] for n in ("ox_send", "ox_recv", "oz_send", "oz_recv"))
    free_sem = ns["free_sem"]
    outputs = ((xf, ns["rzo"], dk_s), (cf, ns["rzn"], dv_s))

    def out_part(n, rows, start):
        if n == 0:
            return dot(ctx[rows, :], wdf[:, at(start, half)], NN) + dot(
                hidden[rows, :], w2f[:, at(start, half)], NN
            )
        return dot(mg[rows, :], wqf[at(start, half), :], NT) + dot(
            pg[rows, :], w1f[at(start, half), :], NT
        )

    def part_over(n, i):
        buf = outputs[n][0]
        rows = slice(i * BLOCK, (i + 1) * BLOCK)
        return remote(
            buf.at[rows, :half], buf.at[rows, half:], ox_send.at[n, i], ox_recv.at[n, i], across
        )

    def send_theirs(n, i):
        rows = slice(i * BLOCK, (i + 1) * BLOCK)
        outputs[n][0][rows, :half] = out_part(n, rows, theirs_at).astype(BF)
        part_over(n, i).start()

    def part_on(n, i, s):
        buf, landing_z, _ = outputs[n]
        rows = slice(i * BLOCK, (i + 1) * BLOCK)
        j = lax.rem(c + s, n_col)
        return remote(
            buf.at[rows, at(j * width, width)],
            landing_z.at[s - 1, rows, :],
            oz_send.at[n, i, s - 1],
            oz_recv.at[n, i, s - 1],
            to(d, r, j),
        )

    def scatter(n, i):
        buf, _, keep = outputs[n]
        rows = slice(i * BLOCK, (i + 1) * BLOCK)
        part_over(n, i).wait()
        v = out_part(n, rows, mine_at) + buf[rows, half:].astype(F32)
        bias_s[:, :half] = v
        buf[rows, :half] = v.astype(BF)
        for t in range(width // 128):
            keep[t, rows, :] = bias_s[:, at(c * width + t * 128, 128)]
        for s in range(1, n_col):
            part_on(n, i, s).start()

    stagez = ns["stagez"]

    def collect(n):
        _, landing_z, keep = outputs[n]
        for s in range(1, n_col):
            for i in range(n_blocks):
                part_on(n, i, s).wait_recv()
            load = pltpu.make_async_copy(landing_z.at[s - 1], stagez.at[0], stage_sem.at[1])
            load.start()
            load.wait()

            def add(i, _):
                rows = at(i * BLOCK, BLOCK)
                for t in range(width // 128):
                    keep[t, rows, :] += stagez[0, rows, t * 128 : (t + 1) * 128].astype(F32)
                return 0

            lax.fori_loop(0, n_blocks, add, 0)

    def backward_block(i):
        keys = (i + 1) * BLOCK
        rows = slice(i * BLOCK, keys)
        set_bias(i)

        def pair(t, _):
            lanes = at(t * 128, 128)
            q, k, v = q_s[t, rows, :], k_s[t, :keys, :], v_s[t, :keys, :]
            grad = dctx[rows, lanes]
            query_grads = []
            for h in range(2):
                qh, gh = mine(h, q), mine(h, grad)
                log_total = jnp.sum(
                    jnp.where(lane_at == 2 * t + h, lse[rows, :], 0.0), axis=1, keepdims=True
                )
                p = jnp.exp(dot(qh, k, NT) * scale + bias_s[:, :keys] - log_total)
                dp = dot(gh, v, NT)
                dv_s[t, :keys, :] += dot(p.astype(BF), gh, TN)
                centre = jnp.sum(p * dp, axis=1, keepdims=True)
                ds = (p * (dp - centre) * scale).astype(BF)
                query_grads.append(dot(ds, k, NN))
                dk_s[t, :keys, :] += dot(ds, qh, TN)
            dq = jnp.where(low_head, query_grads[0], query_grads[1])
            mg[rows, lanes] = turn(dq, cos_ref[rows, :], sin_ref[rows, :], -1).astype(BF)
            return 0

        lax.fori_loop(0, pairs, pair, 0)

    def grad_rows(i, _):
        rows = at(i * BLOCK, BLOCK)
        dctx[rows, :] = dot(cf[rows, :], wdf[...], NT).astype(BF)
        for h in range(2):
            cols = slice(h * 512, (h + 1) * 512)
            v = dot(cf[rows, :], w2f[cols, :], NT)
            pg[rows, cols] = (v * pg[rows, cols].astype(F32)).astype(BF)
        return 0

    fc2_grad(0)
    for lane in range(2):
        rr = r if lane == 0 else other
        drain(gf, rr, g_send, g_recv, lane)
        drain(xf, rr, x_send, x_recv, lane)
    gb_over.wait_send()
    x_over.wait_send()
    pl.semaphore_signal(free_sem.at[0], inc=1, **across)
    pl.semaphore_wait(free_sem.at[0], 1)
    for i in range(n_blocks):
        send_theirs(0, i)
    for s in range(n_col):
        landed(block(cf, other, s), cx_recv.at[s]).wait_recv()
    fc2_grad(1)
    sum_next("fc2", 0, 0)
    lax.fori_loop(0, n_blocks, grad_rows, 0)
    sum_next("fc2", 1, 0)
    fc1_grad(1)
    fc1_grad(0)
    sum_next("fc1", 1, 0)
    dk_s[...] = jnp.zeros_like(dk_s)
    dv_s[...] = jnp.zeros_like(dv_s)
    for i in range(n_blocks):
        backward_block(i)
        if i == 1:
            sum_next("fc1", 0, 0)
    for t in range(pairs):
        lanes = slice(qw + t * 128, qw + (t + 1) * 128)
        mg[:, lanes] = turn(dk_s[t], cos_ref[...], sin_ref[...], -1).astype(BF)
        lanes = slice(2 * qw + t * 128, 2 * qw + (t + 1) * 128)
        mg[:, lanes] = dv_s[t].astype(BF)
    for p in (1, 0):
        dense_grad(p)
    for p in (1, 0):
        qkv_grad(p)
    sum_rest("fc2")
    drain(cf, r, c_send, c_recv, 0)
    for s in range(n_col):
        cot_over(s).wait_send()
    pl.semaphore_signal(free_sem.at[1], inc=1, **across)
    for name in ("dense", "qkv"):
        for p in (1, 0):
            sum_next(name, p, 0)
    pl.semaphore_wait(free_sem.at[1], 1)
    for i in range(2):
        send_theirs(1, i)
    for i in range(n_blocks):
        scatter(0, i)
    sum_rest("fc1")
    for i in range(2, n_blocks):
        send_theirs(1, i)
    spread_first("fc2")
    for i in range(2):
        scatter(1, i)
    sum_rest("dense")
    sum_rest("qkv")
    spread_first("fc1")

    stage_x = stagez.at[1]
    load = pltpu.make_async_copy(x_ref, stage_x, stage_sem.at[2])
    load.start()
    collect(0)
    load.wait()

    def out_final(i, _):
        rows = at(i * BLOCK, BLOCK)
        for t in range(width // 128):
            lanes = slice(t * 128, (t + 1) * 128)
            v = stagez[1, rows, lanes].astype(F32) + dk_s[t, rows, :] + ns["out_bias"][:, lanes]
            ns["y_out"][rows, lanes] = v.astype(BF)
        return 0

    lax.fori_loop(0, n_blocks, out_final, 0)
    for i in range(2, n_blocks):
        scatter(1, i)
    spread_rest("fc2")
    spread_first("dense")
    spread_first("qkv")

    collect(1)
    tot, small_v, small_r = ns["tot"], ns["small_v"], ns["small_r"]
    grads = ns["small"]
    small_v[...] = jnp.zeros_like(small_v)
    n_mixed, n_pre = mg.shape[1], pg.shape[1]
    base = n_mixed + n_pre

    def norm_sums(i, _):
        rows = at(i * BLOCK, BLOCK)
        mu, inv = ns["mean"][rows, :], ns["rstd"][rows, :]
        one = jnp.zeros((BLOCK, 1), F32)
        two = jnp.zeros((BLOCK, 1), F32)
        for t in range(width // 128):
            lanes = slice(t * 128, (t + 1) * 128)
            g = dv_s[t, rows, :]
            hat = (stagez[1, rows, lanes].astype(F32) - mu) * inv
            sg = g * ns["gain_own"][:, lanes]
            one = one + jnp.sum(sg, axis=1, keepdims=True)
            two = two + jnp.sum(sg * hat, axis=1, keepdims=True)
            lo = base + width + t * 128
            small_v[0:1, lo : lo + 128] += jnp.sum(g * hat, axis=0, keepdims=True)
            lo = base + 2 * width + t * 128
            small_v[0:1, lo : lo + 128] += jnp.sum(g, axis=0, keepdims=True)
        packed = jnp.where(lane_at == 0, one, jnp.where(lane_at == 1, two, 0.0))
        tot[0, :, rows] = jnp.transpose(packed)[0:8, :]
        small_v[0:1, :n_mixed] += jnp.sum(mg[rows, :].astype(F32), axis=0, keepdims=True)
        small_v[0:1, n_mixed:base] += jnp.sum(pg[rows, :].astype(F32), axis=0, keepdims=True)
        return 0

    lax.fori_loop(0, n_blocks, norm_sums, 0)
    tot_send, tot_recv = ns["tot_send"], ns["tot_recv"]
    swap = remote(tot.at[0], tot.at[1], tot_send.at[0], tot_recv.at[0], across)
    swap.start()
    load = pltpu.make_async_copy(cot_ref, stagez.at[0], stage_sem.at[1])
    load.start()
    load.wait()

    def cot_sums(i, _):
        rows = at(i * BLOCK, BLOCK)
        small_v[0:1, base : base + width] += jnp.sum(
            stagez[0, rows, :].astype(F32), axis=0, keepdims=True
        )
        return 0

    lax.fori_loop(0, n_blocks, cot_sums, 0)
    sm_send, sm_recv = ns["sm_send"], ns["sm_recv"]

    def small_copy(b):
        return remote(small_v, small_r.at[b], sm_send.at[b], sm_recv.at[b], to(peer(b), r, c))

    small_copy(0).start()
    swap.wait()
    tot[0] = tot[0] + tot[1]
    tot_copies = [
        remote(
            tot.at[0], tot.at[1 + s], tot_send.at[s], tot_recv.at[s], to(d, r, lax.rem(c + s, n_col))
        )
        for s in range(1, n_col)
    ]
    for copy in tot_copies:
        copy.start()
    for b in range(n_bits):
        small_copy(b).wait()
        small_v[...] = small_v[...] + small_r[b]
        if b + 1 < n_bits:
            small_copy(b + 1).start()
    grads[...] = small_v[...]
    for copy in tot_copies:
        copy.wait()
    tot[1] = tot[0]
    for s in range(1, n_col):
        tot[1] = tot[1] + tot[1 + s]

    def in_final(i, _):
        rows = at(i * BLOCK, BLOCK)
        mu, inv = ns["mean"][rows, :], ns["rstd"][rows, :]
        sums = jnp.transpose(
            jnp.concatenate([tot[1, :, rows], jnp.zeros((120, BLOCK), F32)], axis=0)
        ) * (1.0 / full)
        one, two = sums[:, 0:1], sums[:, 1:2]
        for t in range(width // 128):
            lanes = slice(t * 128, (t + 1) * 128)
            hat = (stagez[1, rows, lanes].astype(F32) - mu) * inv
            sg = dv_s[t, rows, :] * ns["gain_own"][:, lanes]
            ns["in_grad"][rows, lanes] = stagez[0, rows, lanes].astype(F32) + inv * (
                sg - one - hat * two
            )
        return 0

    lax.fori_loop(0, n_blocks, in_final, 0)

    for name in ("fc1", "dense", "qkv"):
        spread_rest(name)
    for name in tensors:
        spread_next(name, 0)
    for name in tensors:
        finish(name)
    for i in range(6):
        weight_across(i).wait_send()
        weight_up(i).wait_send()
        for h in range(2):
            weight_share(i, h).wait_send()
    for n in range(2):
        for i in range(n_blocks):
            for s in range(1, n_col):
                part_on(n, i, s).wait_send()


def local(
    block_input,
    segment_ids,
    positions,
    ln_gain,
    ln_bias,
    qkv_weight,
    qkv_bias,
    dense_weight,
    dense_bias,
    fc1_weight,
    fc1_bias,
    fc2_weight,
    fc2_bias,
    cotangent,
):
    n_col = lax.axis_size("col")
    n_dp = lax.axis_size("dp")
    n_bits = n_dp.bit_length() - 1
    tokens, width = block_input.shape
    full = width * n_col * 2
    half = full // 2
    qw = qkv_weight.shape[2] // 2
    hid = fc1_weight.shape[1] // 2
    pairs = qw // 128
    small_w = 3 * qw + hid + 3 * width
    gb = jnp.concatenate(
        [
            jnp.broadcast_to(ln_gain.astype(F32)[None], (8, width)),
            jnp.broadcast_to(ln_bias.astype(F32)[None], (8, width)),
        ],
        axis=0,
    )
    lane = np.arange(128) % HEAD_DIM
    steps = (lane % (ROT_DIM // 2)).astype(np.float32)
    freq = np.exp(steps * np.float32(-2.0 * math.log(10000.0) / ROT_DIM), dtype=np.float32)
    freq = jnp.asarray(np.where(lane < ROT_DIM, freq, np.float32(0.0))[None])
    hbm = pl.BlockSpec(memory_space=pl.ANY)
    vmem = pl.BlockSpec(memory_space=pltpu.VMEM)
    dma = pltpu.SemaphoreType.DMA
    bits = max(n_bits, 1)
    sds = jax.ShapeDtypeStruct
    outs = (
        (vmem, sds((tokens, width), BF)),
        (vmem, sds((tokens, width), F32)),
        (vmem, sds((8, small_w), F32)),
        (hbm, sds((half, 2 * hid), BF)),
        (hbm, sds((2, hid, half), BF)),
        (hbm, sds((2, qw, half), BF)),
        (hbm, sds((3, half, 2 * qw), BF)),
        (hbm, sds((2, half, hid), BF)),
        (hbm, sds((2, hid, half), BF)),
        (hbm, sds((2, qw, half), BF)),
        (hbm, sds((2, 3, half, qw), BF)),
        (hbm, sds((n_col - 1, tokens, width), BF)),
        (hbm, sds((n_col - 1, tokens, width), BF)),
    )
    v = pltpu.VMEM
    scratch = [
        v((tokens, full), BF),
        v((tokens, full), BF),
        v((16, full), F32),
        v((full, 3 * qw), BF),
        v((full, hid), BF),
        v((hid, full), BF),
        v((qw, full), BF),
        v((tokens, full), BF),
        v((tokens, hid), BF),
        v((tokens, hid), BF),
        v((pairs, tokens, 128), BF),
        v((pairs, tokens, 128), BF),
        v((pairs, tokens, 128), BF),
        v((pairs, tokens, 128), F32),
        v((pairs, tokens, 128), F32),
        v((BLOCK, tokens), F32),
        v((tokens, 128), F32),
        v((tokens, 128), F32),
        v((tokens, qw), BF),
        v((tokens, qw), BF),
        v((tokens, 3 * qw), BF),
        v((tokens, 128), F32),
        v((2, half, hid), BF),
        v((2, hid, half), BF),
        v((2, qw, half), BF),
        v((2, 3, half, qw), BF),
        v((half // 2, hid), BF),
        v((qw // 2, half), BF),
        v((3, half // 2, qw), BF),
        v((2, tokens, width), BF),
        v((tokens, 1), F32),
        v((tokens, 1), F32),
        v((n_col + 1, 8, tokens), F32),
        v((8, small_w), F32),
        v((bits, 8, small_w), F32),
        dma((2, 3, n_col)),
        dma((2, n_col)),
        dma((2, 3, n_col)),
        dma((2, n_col)),
        dma((1, 2, n_col)),
        dma((1, n_col)),
        dma((n_col,)),
        dma((n_col,)),
        dma((6,)),
        dma((6,)),
        dma((6,)),
        dma((6,)),
        dma((6, 2)),
        dma((6, 2)),
        dma((9,)),
        dma((4, 2, bits)),
        dma((4, 2, bits)),
        dma((4,)),
        dma((4,)),
        dma((4, bits)),
        dma((4, bits)),
        dma((4,)),
        dma((3,)),
        dma((2, tokens // BLOCK)),
        dma((2, tokens // BLOCK)),
        dma((2, tokens // BLOCK, n_col - 1)),
        dma((2, tokens // BLOCK, n_col - 1)),
        dma((n_col,)),
        dma((n_col,)),
        dma((bits,)),
        dma((bits,)),
        pltpu.SemaphoreType.REGULAR((2,)),
    ]
    res = pl.pallas_call(
        functools.partial(kernel, n_dp, n_col),
        out_shape=tuple(o[1] for o in outs),
        in_specs=[hbm] * 6 + [vmem] * 8,
        out_specs=tuple(o[0] for o in outs),
        scratch_shapes=scratch,
        compiler_params=pltpu.CompilerParams(
            collective_id=0,
            has_side_effects=True,
            vmem_limit_bytes=64 * 2**20,
            fuse_transposed_lhs_in_matmul=True,
        ),
        cost_estimate=pl.CostEstimate(
            flops=45 * 10**9, bytes_accessed=64 * 2**20, transcendentals=8 * 2**20
        ),
    )(
        block_input,
        cotangent,
        jnp.transpose(qkv_weight, (1, 0, 2)),
        fc1_weight,
        fc2_weight,
        dense_weight,
        gb,
        jnp.stack([segment_ids, positions], axis=1),
        segment_ids.reshape(1, tokens),
        freq,
        qkv_bias.reshape(3, qw),
        fc1_bias.reshape(1, hid),
        (dense_bias + fc2_bias).reshape(1, width),
        ln_gain.astype(F32).reshape(1, width),
    )
    y_out, in_grad, small, f1, f2, fd, fq = res[:7]
    small = small[0]
    n_mixed = 3 * qw
    base = n_mixed + hid
    bias_grad, gain_grad, shift_grad = (
        small[base + i * width : base + (i + 1) * width] for i in range(3)
    )
    return (
        y_out,
        in_grad,
        gain_grad,
        shift_grad,
        jnp.transpose(fq.astype(F32), (1, 0, 2)),
        small[:n_mixed].reshape(qkv_bias.shape),
        fd.reshape(dense_weight.shape).astype(F32),
        bias_grad,
        f1.astype(F32),
        small[n_mixed:base].reshape(fc1_bias.shape),
        f2.reshape(fc2_weight.shape).astype(F32),
        bias_grad,
    )


def solution(mesh):
    return jax.shard_map(
        local,
        mesh=mesh,
        in_specs=(
            P("dp", ("row", "col")),
            P("dp"),
            P("dp"),
            P(("row", "col")),
            P(("row", "col")),
            P("row", None, "col"),
            P(None, "col", "row", None),
            P("col", "row"),
            P(("row", "col")),
            P("row", "col"),
            P("col", "row", None),
            P("col", "row"),
            P(("row", "col")),
            P("dp", ("row", "col")),
        ),
        out_specs=(
            P("dp", ("row", "col")),
            P("dp", ("row", "col")),
            P(("row", "col")),
            P(("row", "col")),
            P("row", None, "col"),
            P(None, "col", "row", None),
            P("col", "row"),
            P(("row", "col")),
            P("row", "col"),
            P("col", "row", None),
            P("col", "row"),
            P(("row", "col")),
        ),
        check_vma=False,
    )
```

```python
import functools
import math

import jax
import jax.numpy as jnp
import numpy as np
from jax import lax
from jax.experimental import pallas as pl
from jax.experimental.pallas import tpu as pltpu
from jax.sharding import PartitionSpec as P

HEAD_DIM = 64
ROT_DIM = 32
NORM_EPSILON = 1e-05
MASKED_SCORE = -1e30
BLOCK = 256
MESH = pl.DeviceIdType.MESH
BF = jnp.bfloat16
F32 = jnp.float32
GELU_A = math.sqrt(2.0 / math.pi)
GELU_B = 0.044715
NN = (((1,), (0,)), ((), ()))
NT = (((1,), (1,)), ((), ()))
TN = (((0,), (0,)), ((), ()))


def dot(a, b, dims):
    return lax.dot_general(a, b, dims, preferred_element_type=F32)


def kernel(
    n_dp,
    n_col,
    x_p,
    cot_p,
    wq_p,
    w1_p,
    w2_p,
    wd_p,
    vec_p,
    token_p,
    freq_p,
    y_out_p,
    in_grad_p,
    small_p,
    f1_p,
    f2_p,
    fd_p,
    fq_p,
    rb1_p,
    rbd_p,
    rbq_p,
    rzo_p,
    rzn_p,
    rza_p,
    xf_p,
    cf_p,
    gf_p,
    wqf_p,
    w1f_p,
    w2f_p,
    wdf_p,
    normed_p,
    hidden_p,
    pg_p,
    q_p,
    k_p,
    v_p,
    dk_p,
    dv_p,
    bias_p,
    cos_p,
    sin_p,
    ctx_p,
    dctx_p,
    mg_p,
    lse_p,
    g1_p,
    g2_p,
    gd_p,
    gq_p,
    stage1_p,
    staged_p,
    stageq_p,
    stagez_p,
    stageo_p,
    xl_p,
    gb_p,
    places_p,
    rb2_p,
    mean_p,
    rstd_p,
    tot_p,
    small_v_p,
    small_r_p,
    x_send_p,
    x_recv_p,
    v_send_p,
    v_recv_p,
    vx_send_p,
    vx_recv_p,
    g_send_p,
    g_recv_p,
    c_send_p,
    c_recv_p,
    cx_send_p,
    cx_recv_p,
    w_send_p,
    w_recv_p,
    y_send_p,
    y_recv_p,
    s_send_p,
    s_recv_p,
    load_sem_p,
    rs_send_p,
    rs_recv_p,
    xs_send_p,
    xs_recv_p,
    ag_send_p,
    ag_recv_p,
    part_sem_p,
    stage_sem_p,
    ox_send_p,
    ox_recv_p,
    oz_send_p,
    oz_recv_p,
    za_send_p,
    za_recv_p,
    xo_send_p,
    xo_recv_p,
    tot_send_p,
    tot_recv_p,
    sm_send_p,
    sm_recv_p,
    free_sem_p,
):
    xf, cf, gf = xf_p, cf_p, gf_p
    wqf, w1f, w2f, wdf = wqf_p, w1f_p, w2f_p, wdf_p
    normed, hidden, pg = normed_p, hidden_p, pg_p
    q_s, k_s, v_s, dk_s, dv_s = q_p, k_p, v_p, dk_p, dv_p
    ctx, dctx, mg, lse = ctx_p, dctx_p, mg_p, lse_p
    cos_ref, sin_ref, bias_s = cos_p, sin_p, bias_p
    load_sem, stage_sem = load_sem_p, stage_sem_p

    d = lax.axis_index("dp")
    r = lax.axis_index("row")
    c = lax.axis_index("col")
    n_bits = n_dp.bit_length() - 1
    core = lax.rem(d, 2)
    sibling = d + 1 - 2 * core
    other = 1 - r
    has_right = c < n_col - 1
    has_left = c > 0
    right = jnp.minimum(c + 1, n_col - 1)
    left = jnp.maximum(c - 1, 0)
    tokens, width = x_p.shape
    full = width * n_col * 2
    half = full // 2
    heads_w = qw = ctx.shape[1]
    pairs = heads_w // 128
    n_blocks = tokens // BLOCK
    scale = HEAD_DIM**-0.5

    def to(dd, rr, cc):
        return dict(device_id=(dd, rr, cc), device_id_type=MESH)

    def bit(b):
        return lax.rem(lax.div(d, 1 << b), 2)

    def peer(b):
        return d + (1 - 2 * bit(b)) * (1 << b)

    def remote(src, dst, send, recv, dev):
        return pltpu.make_async_remote_copy(
            src_ref=src, dst_ref=dst, send_sem=send, recv_sem=recv, **dev
        )

    def at(start, size):
        return pl.ds(pl.multiple_of(start, math.gcd(size, 256)), size)

    across = to(d, other, c)

    barrier = pltpu.get_barrier_semaphore()
    pl.semaphore_signal(barrier, inc=1, **across)
    for s in range(1, n_col):
        pl.semaphore_signal(barrier, inc=1, **to(d, r, lax.rem(c + s, n_col)))
    for b in range(n_bits):
        pl.semaphore_signal(barrier, inc=1, **to(peer(b), r, c))
    pl.semaphore_wait(barrier, 1 + (n_col - 1) + n_bits)

    gain_own_p = vec_p.at[:, 0:width]
    out_bias_p = vec_p.at[:, 2 * width : 3 * width]
    qkv_at = 3 * width
    fc1_at = qkv_at + 3 * qw
    gb_p[0:8, :] = jnp.broadcast_to(vec_p[:, 0:width], (8, width))
    gb_p[8:16, :] = jnp.broadcast_to(vec_p[:, width : 2 * width], (8, width))

    top = slice(0, tokens // 2)
    low = slice(tokens // 2, tokens)

    def block(ref, rr, j, rows=slice(None)):
        return ref.at[rows, at((rr * n_col + j) * width, width)]

    def hop(way, own, rr, j, lane, step):
        whole, mine_ref, send, recv, rows = way
        dst = block(whole, rr, j, rows)
        return remote(
            mine_ref if own else dst,
            dst,
            send.at[lane, step, j],
            recv.at[lane, j],
            to(d, r, right if step == 0 else left),
        )

    def over(way, own, j, send, recv):
        dst = block(way[0], r, j, way[4])
        return remote(way[1] if own else dst, dst, send, recv, across)

    def landed(dst, recv):
        return remote(dst, dst, recv, recv, across)

    def start_hop(cond, way, own, rr, j, lane, step):
        @pl.when(cond)
        def _():
            hop(way, own, rr, j, lane, step).start()

    def start_both(way, own, rr, lane):
        start_hop(has_right, way, own, rr, c, lane, 0)
        start_hop(has_left, way, own, rr, c, lane, 1)

    def advance(way, rr, lane, s, then=None):
        whole, _, _, recv, rows = way

        @pl.when(c >= s)
        def _():
            j = c - s
            landed(block(whole, rr, j, rows), recv.at[lane, j]).wait_recv()
            start_hop(has_right, way, False, rr, j, lane, 0)
            if then is not None:
                then(j)

        @pl.when(c + s < n_col)
        def _():
            j = c + s
            landed(block(whole, rr, j, rows), recv.at[lane, j]).wait_recv()
            start_hop(has_left, way, False, rr, j, lane, 1)
            if then is not None:
                then(j)

    def drain(way, rr, lane):
        for s in range(n_col):

            @pl.when((c >= s) & has_right)
            def _():
                hop(way, False, rr, jnp.maximum(c - s, 0), lane, 0).wait_send()

            @pl.when((c + s < n_col) & has_left)
            def _():
                j = jnp.minimum(c + s, n_col - 1)
                hop(way, False, rr, j, lane, 1).wait_send()

    def piece(i, k, rr):
        if i < 3:
            depth = wq_p.shape[1] // 4
            return (
                wq_p.at[i, at(k * depth, depth), at((1 - rr) * qw, qw)],
                wqf.at[at((rr * 4 + k) * depth, depth), i * qw : (i + 1) * qw],
            )
        if i == 3:
            depth, part = w1_p.shape[0] // 4, w1_p.shape[1] // 2
            return (
                w1_p.at[at(k * depth, depth), at((1 - rr) * part, part)],
                w1f.at[at((rr * 4 + k) * depth, depth), :],
            )
        src, dst = (w2_p, w2f) if i == 4 else (wd_p, wdf)
        depth, part = src.shape[0] // 8, src.shape[1]
        return (
            src.at[at(((1 - rr) * 4 + k) * depth, depth), :],
            dst.at[at(k * depth, depth), at(rr * part, part)],
        )

    w_send, w_recv, y_send, y_recv = w_send_p, w_recv_p, y_send_p, y_recv_p
    s_send, s_recv = s_send_p, s_recv_p
    upper = bit(1)
    quarter = (core + 2 * upper, core + 2 * (1 - upper))
    quarter_sib = (1 - core + 2 * upper, 1 - core + 2 * (1 - upper))

    def weight_across(i):
        src, dst = piece(i, quarter[0], r)
        return remote(src, dst, w_send.at[i], w_recv.at[i], across)

    def weight_up(i):
        dst = piece(i, quarter[0], other)[1]
        return remote(dst, dst, y_send.at[i], y_recv.at[i], to(peer(1), r, c))

    def weight_share(i, h):
        dst = piece(i, quarter[h], other)[1]
        return remote(dst, dst, s_send.at[i, h], s_recv.at[i, h], to(sibling, r, c))

    def weights_first(group):
        for i in group:
            landed(piece(i, quarter[0], other)[1], w_recv.at[i]).wait_recv()
            weight_up(i).start()
            weight_share(i, 0).start()

    def weights_second(group):
        for i in group:
            landed(piece(i, quarter[1], other)[1], y_recv.at[i]).wait_recv()
            weight_share(i, 1).start()

    def weights_wait(group):
        for i in group:
            for h in range(2):
                landed(piece(i, quarter_sib[h], other)[1], s_recv.at[i, h]).wait_recv()

    x_way = (xf, x_p.at[top, :], x_send_p, x_recv_p, top)
    x_low = (xf, x_p.at[low, :], v_send_p, v_recv_p, low)
    g_way = (gf, gb_p, g_send_p, g_recv_p, slice(None))
    c_way = (cf, cot_p, c_send_p, c_recv_p, slice(None))
    cx_send, cx_recv, vx_send, vx_recv = cx_send_p, cx_recv_p, vx_send_p, vx_recv_p
    g_over = over(g_way, True, c, g_send_p.at[1, 2, c], g_recv_p.at[1, c])
    x_over = over(x_way, True, c, x_send_p.at[1, 2, c], x_recv_p.at[1, c])

    def low_over(j, own=False):
        return over(x_low, own, j, vx_send.at[j], vx_recv.at[j])

    def cot_over(j, own=False):
        return over(c_way, own, j, cx_send.at[j], cx_recv.at[j])

    g_over.start()
    x_over.start()
    low_over(c, True).start()
    for way in (g_way, x_way, x_low):
        start_both(way, True, r, 0)

    own = [(x_p, block(xf, r, c)), (gb_p, block(gf, r, c)), (cot_p, block(cf, r, c))]
    depth = wq_p.shape[1]
    for s in range(3):
        own.append((wq_p.at[s, :, at(r * qw, qw)], wqf.at[at(r * depth, depth), s * qw : (s + 1) * qw]))
    depth, part = w1_p.shape[0], w1_p.shape[1] // 2
    own.append((w1_p.at[:, at(r * part, part)], w1f.at[at(r * depth, depth), :]))
    for src, dst in ((w2_p, w2f), (wd_p, wdf)):
        depth, part = src.shape[0] // 2, src.shape[1]
        own.append((src.at[at(r * depth, depth), :], dst.at[:, at(r * part, part)]))
    own = [pltpu.make_async_copy(a, b, load_sem.at[i]) for i, (a, b) in enumerate(own)]
    for copy in own:
        copy.start()

    def tables(i, _):
        rows = at(i * BLOCK, BLOCK)
        wide = jnp.concatenate([token_p[:, rows], jnp.zeros((126, BLOCK), F32)], axis=0)
        places_p[rows, :] = jnp.transpose(wide)
        angle = places_p[rows, 1:2] * freq_p[...]
        cos_ref[rows, :] = jnp.cos(angle)
        sin_ref[rows, :] = jnp.sin(angle)
        return 0

    for i in (3, 0, 1, 2):
        weight_across(i).start()
    for way in (g_way, x_way):
        landed(block(way[0], other, c, way[4]), way[3].at[1, c]).wait_recv()
        start_both(way, False, other, 1)

    def start_cot(s):
        start_hop(has_right & (c == s), c_way, True, r, c, 0, 0)
        start_hop(has_left & (c == n_col - 1 - s), c_way, True, r, c, 0, 1)

    start_cot(0)
    lax.fori_loop(0, n_blocks, tables, 0)
    for s in range(1, n_col):
        advance(g_way, r, 0, s)
        advance(x_way, r, 0, s)
        advance(x_low, r, 0, s, then=lambda j: low_over(j).start())
        advance(g_way, other, 1, s)
        advance(x_way, other, 1, s)
        start_cot(s)
        if s == 1:
            cot_over(c, True).start()
        if s == 2:
            weights_first((3,))
        if s == 3:
            for i in range(4, 6):
                weight_across(i).start()
            weights_first(range(3))
            weights_second((3,))

    def advance_cot(s):
        advance(c_way, r, 0, s, then=lambda j: cot_over(j).start())

    for copy in own:
        copy.wait()
    for s in range(n_col):
        landed(block(xf, other, s, low), vx_recv.at[s]).wait_recv()

    gain = gf[0:1, :]
    shift = gf[8:9, :]

    def norm_rows(i, _):
        rows = at(i * 64, 64)
        v = xf[rows, :].astype(F32)
        mu = jnp.sum(v, axis=1, keepdims=True) * (1.0 / full)
        v = v - mu
        inv = lax.rsqrt(jnp.sum(v * v, axis=1, keepdims=True) * (1.0 / full) + NORM_EPSILON)
        mean_p[rows, :] = mu
        rstd_p[rows, :] = inv
        normed[rows, :] = (v * inv * gain + shift).astype(BF)
        return 0


    lane_at = lax.broadcasted_iota(jnp.int32, (1, 128), 1)
    first = lane_at % HEAD_DIM < ROT_DIM // 2
    low_head = lane_at < HEAD_DIM

    def turn(v, cos, sin, sign):
        up = pltpu.roll(v, 128 - ROT_DIM // 2, 1)
        down = pltpu.roll(v, ROT_DIM // 2, 1)
        swapped = jnp.where(first, -up, down) * sin
        return v * cos + swapped if sign > 0 else v * cos - swapped

    def qkv_rows(i, _):
        rows = at(i * BLOCK, BLOCK)
        mixed = dot(normed[rows, :], wqf[...], NN)
        cos, sin = cos_ref[rows, :], sin_ref[rows, :]
        for s, dst in enumerate((q_s, k_s, v_s)):
            for t in range(pairs):
                lanes = slice(s * qw + t * 128, s * qw + (t + 1) * 128)
                bias_at = qkv_at + s * qw + t * 128
                v = mixed[:, lanes] + vec_p[:, bias_at : bias_at + 128]
                dst[t, rows, :] = (turn(v, cos, sin, 1) if s < 2 else v).astype(BF)
        return 0


    def fc1_rows(i, _):
        rows = at(i * BLOCK, BLOCK)
        for h in range(2):
            cols = slice(h * 512, (h + 1) * 512)
            v = dot(normed[rows, :], w1f[:, cols], NN) + vec_p[:, fc1_at + h * 512 : fc1_at + (h + 1) * 512]
            th = jnp.tanh(GELU_A * (v + GELU_B * v * v * v))
            hidden[rows, cols] = (0.5 * v * (1.0 + th)).astype(BF)
            slope = 0.5 * (1.0 + th) + 0.5 * v * (1.0 - th * th) * (
                GELU_A * (1.0 + 3.0 * GELU_B * v * v)
            )
            pg[rows, cols] = slope.astype(BF)
        return 0

    def set_bias(i):
        keys = (i + 1) * BLOCK
        rows = slice(i * BLOCK, keys)
        row_at = lax.broadcasted_iota(jnp.int32, (BLOCK, keys), 0) + i * BLOCK
        key_at = lax.broadcasted_iota(jnp.int32, (BLOCK, keys), 1)
        allowed = (places_p[rows, 0:1] == token_p[0:1, :keys]) & (row_at >= key_at)
        bias_s[:, :keys] = jnp.where(allowed, 0.0, MASKED_SCORE)

    def mine(h, v):
        return jnp.where(low_head if h == 0 else ~low_head, v, jnp.zeros_like(v))

    def forward_block(i):
        keys = (i + 1) * BLOCK
        rows = slice(i * BLOCK, keys)
        set_bias(i)

        def pair(t, _):
            q, k, v = q_s[t, rows, :], k_s[t, :keys, :], v_s[t, :keys, :]
            outs = []
            logs = lse[rows, :]
            for h in range(2):
                s = dot(mine(h, q), k, NT) * scale + bias_s[:, :keys]
                top = jnp.max(s, axis=1, keepdims=True)
                e = jnp.exp(s - top)
                total = jnp.sum(e, axis=1, keepdims=True)
                low = (e * (1.0 / total)).astype(BF)
                outs.append(dot(low, v, NN))
                logs = jnp.where(lane_at == 2 * t + h, top + jnp.log(total), logs)
            lse[rows, :] = logs
            ctx[rows, at(t * 128, 128)] = jnp.where(low_head, outs[0], outs[1]).astype(BF)
            return 0

        lax.fori_loop(0, pairs, pair, 0)

    rs_send, rs_recv, xs_send, xs_recv = rs_send_p, rs_recv_p, xs_send_p, xs_recv_p
    ag_send, ag_recv, part_sem = ag_send_p, ag_recv_p, part_sem_p
    g1, g2, gd, gq = g1_p, g2_p, gd_p, gq_p
    tensors = dict(
        fc1=(0, g1, rb1_p, stage1_p, half),
        fc2=(1, g2, rb2_p, None, hidden.shape[1]),
        dense=(2, gd, rbd_p, staged_p, heads_w),
        qkv=(3, gq, rbq_p, stageq_p, half),
    )
    results = dict(fc1=f1_p, fc2=f2_p, dense=fd_p, qkv=fq_p)
    mine_at, theirs_at = r * half, other * half
    starts = (mine_at, theirs_at)

    def slab(ref, p, rows):
        return ref.at[p, :, rows, :] if len(ref.shape) == 4 else ref.at[p, rows, :]

    def offset(rows, upto):
        off = 0
        for b in range(upto):
            off = off + bit(b) * (rows >> (b + 1))
        return off

    def landing(rows, b):
        return slice(rows - (rows >> b), rows - (rows >> (b + 1)))

    def nth(k):
        j = c
        for here in range(n_col):
            turn_k = sorted(range(n_col), key=lambda v: (abs(v - here), v))[k]
            j = jnp.where(c == here, turn_k, j)
        return j

    def sum_copy(name, p, b, k=0):
        n, g, rb, _, rows = tensors[name]
        size = rows >> (b + 1)
        src = slab(g, p, at(offset(rows, b) + (1 - bit(b)) * size, size))
        dst = slab(rb, p, landing(rows, b))
        if name == "fc2":
            cols = at(nth(k) * width, width)
            src, dst = src.at[:, cols], dst.at[:, cols]
        return remote(src, dst, rs_send.at[n, p, b, k], rs_recv.at[n, p, b, k], to(peer(b), r, c))

    def place(name, rr, off, size):
        if name == "fc1":
            return f1_p.at[at(off, size), at(rr * hidden.shape[1], hidden.shape[1])]
        if name == "qkv":
            return fq_p.at[:, at(off, size), at(rr * qw, qw)]
        return results[name].at[rr, at(off, size), :]

    def kept(name, p):
        _, g, _, _, rows = tensors[name]
        size = rows >> n_bits
        off = offset(rows, n_bits)
        return slab(g, p, at(off, size)), off, size

    def part_copy(name):
        src, off, size = kept(name, 0)
        return pltpu.make_async_copy(src, place(name, r, off, size), part_sem.at[tensors[name][0]])

    def swap_copy(name):
        src, off, size = kept(name, 1)
        n = tensors[name][0]
        return remote(src, place(name, r, off, size), xs_send.at[n], xs_recv.at[n], across)

    def fc2_next(p, b, k):
        _, g, rb, _, rows = tensors["fc2"]
        size = rows >> (b + 1)
        off = offset(rows, b + 1)
        cols = at(nth(k) * width, width)
        sum_copy("fc2", p, b, k).wait_recv()
        chunk = min(size, 128)

        def add(i, _):
            there = (p, at(off + i * chunk, chunk), cols)
            here = (p, at(rows - (rows >> b) + i * chunk, chunk), cols)
            g[there] = (g[there].astype(F32) + rb[here].astype(F32)).astype(BF)
            return 0

        lax.fori_loop(0, size // chunk, add, 0)
        if b + 1 < n_bits:
            sum_copy("fc2", p, b + 1, k).start()

    def sum_next(name, p, b):
        n, g, rb, stage, rows = tensors[name]
        size = rows >> (b + 1)
        off = offset(rows, b + 1)
        sum_copy(name, p, b).wait_recv()
        four = len(g.shape) == 4
        chunk = min(size, 128)
        dst = stage.at[:, :size, :] if four else stage.at[:size, :]
        copy = pltpu.make_async_copy(slab(rb, p, landing(rows, b)), dst, stage_sem.at[0])
        copy.start()
        copy.wait()

        def add(i, _):
            if four:
                there = (p, slice(None), at(off + i * chunk, chunk), slice(None))
                here = (slice(None), at(i * chunk, chunk), slice(None))
            else:
                there = (p, at(off + i * chunk, chunk), slice(None))
                here = (at(i * chunk, chunk), slice(None))
            g[there] = (g[there].astype(F32) + stage[here].astype(F32)).astype(BF)
            return 0

        lax.fori_loop(0, size // chunk, add, 0)
        if b + 1 < n_bits:
            sum_copy(name, p, b + 1).start()
        elif p == 0:
            part_copy(name).start()
        else:
            swap_copy(name).start()

    def fc2_rest():
        for p in (0, 1):
            for b in range(1, n_bits):
                for k in range(n_col):
                    fc2_next(p, b, k)
        part_copy("fc2").start()
        swap_copy("fc2").start()

    def sum_rest(name):
        for p in (1, 0):
            for b in range(1, n_bits):
                sum_next(name, p, b)

    def rows_of(name, off, size):
        ref = results[name]
        return ref.at[at(off, size), :] if name == "fc1" else ref.at[:, at(off, size), :]

    def spread_copy(name, b):
        n, rows = tensors[name][0], tensors[name][4]
        ref = rows_of(name, offset(rows, b + 1), rows >> (b + 1))
        return remote(ref, ref, ag_send.at[n, b], ag_recv.at[n, b], to(peer(b), r, c))

    def spread_landed(name, b):
        n, rows = tensors[name][0], tensors[name][4]
        size = rows >> (b + 1)
        return landed(rows_of(name, offset(rows, b) + (1 - bit(b)) * size, size), ag_recv.at[n, b])

    def spread_first(name):
        _, off, size = kept(name, 0)
        part_copy(name).wait()
        landed(place(name, other, off, size), xs_recv.at[tensors[name][0]]).wait_recv()
        spread_copy(name, n_bits - 1).start()

    def spread_next(name, b):
        spread_landed(name, b).wait_recv()
        if b > 0:
            spread_copy(name, b - 1).start()

    def spread_rest(name):
        for b in reversed(range(1, n_bits)):
            spread_next(name, b)

    def finish(name):
        for b in range(n_bits):
            for p in range(2):
                for k in range(n_col if name == "fc2" else 1):
                    sum_copy(name, p, b, k).wait_send()
            spread_copy(name, b).wait_send()
        swap_copy(name).wait_send()

    def fc2_grad(p, k):
        col = nth(k) * width

        def body(i, _):
            cols = at(i * BLOCK, BLOCK)
            g2[p, cols, at(col, width)] = dot(
                hidden[:, cols], cf[:, at(starts[p] + col, width)], TN
            ).astype(BF)
            return 0

        lax.fori_loop(0, hidden.shape[1] // BLOCK, body, 0)
        sum_copy("fc2", p, 0, k).start()

    def fc1_grad(p):
        def body(i, _):
            g1[p, at(i * BLOCK, BLOCK), :] = dot(
                normed[:, at(starts[p] + i * BLOCK, BLOCK)], pg[...], TN
            ).astype(BF)
            return 0

        lax.fori_loop(0, half // BLOCK, body, 0)
        sum_copy("fc1", p, 0).start()

    def dense_grad(p):
        gd[p] = dot(ctx[...], cf[:, at(starts[p], half)], TN).astype(BF)
        sum_copy("dense", p, 0).start()

    def qkv_grad(p):
        def body(i, _):
            v = dot(normed[:, at(starts[p] + i * BLOCK, BLOCK)], mg[...], TN).astype(BF)
            for s in range(3):
                gq[p, s, at(i * BLOCK, BLOCK), :] = v[:, s * qw : (s + 1) * qw]
            return 0

        lax.fori_loop(0, half // BLOCK, body, 0)
        sum_copy("qkv", p, 0).start()

    ox_send, ox_recv, oz_send, oz_recv = ox_send_p, ox_recv_p, oz_send_p, oz_recv_p
    free_sem = free_sem_p
    outputs = ((xf, rzo_p), (cf, rzn_p))

    def out_part(n, rows, start):
        if n == 0:
            return dot(ctx[rows, :], wdf[:, at(start, half)], NN) + dot(
                hidden[rows, :], w2f[:, at(start, half)], NN
            )
        return dot(mg[rows, :], wqf[at(start, half), :], NT) + dot(
            pg[rows, :], w1f[at(start, half), :], NT
        )

    def part_over(n, i):
        buf = outputs[n][0]
        rows = slice(i * BLOCK, (i + 1) * BLOCK)
        return remote(
            buf.at[rows, :half], buf.at[rows, half:], ox_send.at[n, i], ox_recv.at[n, i], across
        )

    def send_theirs(n, i):
        rows = slice(i * BLOCK, (i + 1) * BLOCK)
        outputs[n][0][rows, :half] = out_part(n, rows, theirs_at).astype(BF)
        part_over(n, i).start()

    def part_on(n, i, s):
        buf, landing_z = outputs[n]
        rows = slice(i * BLOCK, (i + 1) * BLOCK)
        j = lax.rem(c + s, n_col)
        return remote(
            buf.at[rows, at(j * width, width)],
            landing_z.at[s - 1, rows, :],
            oz_send.at[n, i, s - 1],
            oz_recv.at[n, i, s - 1],
            to(d, r, j),
        )

    def scatter(n, i):
        buf = outputs[n][0]
        rows = slice(i * BLOCK, (i + 1) * BLOCK)
        part_over(n, i).wait()
        v = out_part(n, rows, mine_at) + buf[rows, half:].astype(F32)
        bias_s[:, :half] = v
        buf[rows, :half] = v.astype(BF)
        for t in range(width // 128):
            own_part = bias_s[:, at(c * width + t * 128, 128)]
            if n == 0:
                in_grad_p[rows, t * 128 : (t + 1) * 128] = own_part
            else:
                dv_s[t, rows, :] = own_part
        for s in range(1, n_col):
            part_on(n, i, s).start()

    stagez, stageo = stagez_p, stageo_p

    def full_on(i, s, h):
        rows = slice(i * BLOCK, (i + 1) * BLOCK)
        j = lax.rem(c + s, n_col)
        return remote(
            xf.at[rows, at(starts[h] + j * width, width)],
            rza_p.at[s - 1, h, rows, :],
            za_send_p.at[i, s - 1, h],
            za_recv_p.at[i, s - 1, h],
            to(d, r, j),
        )

    def out_full(i):
        rows = slice(i * BLOCK, (i + 1) * BLOCK)
        for start in starts:
            xf[rows, at(start, half)] = out_part(0, rows, start).astype(BF)
        for s in range(1, n_col):
            for h in range(2):
                full_on(i, s, h).start()

    def swap_out(i):
        rows = slice(i * BLOCK, (i + 1) * BLOCK)
        return remote(
            xf.at[rows, at(theirs_at + c * width, width)],
            xl_p.at[rows, :],
            xo_send_p.at[i],
            xo_recv_p.at[i],
            across,
        )

    def collect_full(i):
        rows = slice(i * BLOCK, (i + 1) * BLOCK)
        for s in range(1, n_col):
            for h in range(2):
                full_on(i, s, h).wait_recv()
        load = pltpu.make_async_copy(rza_p.at[:, :, rows, :], stageo, stage_sem.at[1])
        load.start()
        load.wait()
        for h, start in enumerate(starts):
            own = at(start + c * width, width)
            v = xf[rows, own].astype(F32)
            for s in range(n_col - 1):
                v = v + stageo[s, h].astype(F32)
            if h == 0:
                in_grad_p[rows, :] = v
            else:
                xf[rows, own] = v.astype(BF)
        swap_out(i).start()

    def collect_half(n, i):
        rows = slice(i * BLOCK, (i + 1) * BLOCK)
        for s in range(1, n_col):
            part_on(n, i, s).wait_recv()
        landing_z = outputs[n][1]
        load = pltpu.make_async_copy(landing_z.at[:, rows, :], stageo.at[:, 0], stage_sem.at[1])
        load.start()
        load.wait()
        for t in range(width // 128):
            lanes = slice(t * 128, (t + 1) * 128)
            v = stageo[0, 0, :, lanes].astype(F32)
            for s in range(1, n_col - 1):
                v = v + stageo[s, 0, :, lanes].astype(F32)
            if n == 0:
                in_grad_p[rows, lanes] += v
            else:
                dv_s[t, rows, :] += v

    def backward_block(i):
        keys = (i + 1) * BLOCK
        rows = slice(i * BLOCK, keys)
        set_bias(i)

        def pair(t, _):
            lanes = at(t * 128, 128)
            q, k, v = q_s[t, rows, :], k_s[t, :keys, :], v_s[t, :keys, :]
            grad = dctx[rows, lanes]
            query_grads = []
            for h in range(2):
                qh, gh = mine(h, q), mine(h, grad)
                log_total = jnp.sum(
                    jnp.where(lane_at == 2 * t + h, lse[rows, :], 0.0), axis=1, keepdims=True
                )
                p = jnp.exp(dot(qh, k, NT) * scale + bias_s[:, :keys] - log_total)
                dp = dot(gh, v, NT)
                dv_s[t, :keys, :] += dot(p.astype(BF), gh, TN)
                centre = jnp.sum(p * dp, axis=1, keepdims=True)
                ds = (p * (dp - centre) * scale).astype(BF)
                query_grads.append(dot(ds, k, NN))
                dk_s[t, :keys, :] += dot(ds, qh, TN)
            dq = jnp.where(low_head, query_grads[0], query_grads[1])
            mg[rows, lanes] = turn(dq, cos_ref[rows, :], sin_ref[rows, :], -1).astype(BF)
            return 0

        lax.fori_loop(0, pairs, pair, 0)

    def grad_rows(i, _):
        rows = at(i * BLOCK, BLOCK)
        dctx[rows, :] = dot(cf[rows, :], wdf[...], NT).astype(BF)
        for h in range(2):
            cols = slice(h * 512, (h + 1) * 512)
            v = dot(cf[rows, :], w2f[cols, :], NT)
            pg[rows, cols] = (v * pg[rows, cols].astype(F32)).astype(BF)
        return 0

    def theirs_came(k):
        j = nth(k)
        landed(block(cf, other, j), cx_recv.at[j]).wait_recv()

    def finish_mixed(i):
        rows = slice(i * BLOCK, (i + 1) * BLOCK)
        for t in range(pairs):
            lanes = slice(qw + t * 128, qw + (t + 1) * 128)
            mg[rows, lanes] = turn(dk_s[t, rows, :], cos_ref[rows, :], sin_ref[rows, :], -1).astype(BF)
            lanes = slice(2 * qw + t * 128, 2 * qw + (t + 1) * 128)
            mg[rows, lanes] = dv_s[t, rows, :].astype(BF)

    tot, small_v, small_r = tot_p, small_v_p, small_r_p
    n_mixed, n_pre = mg.shape[1], pg.shape[1]
    base = n_mixed + n_pre

    def column_sums(i, _):
        rows = at(i * BLOCK, BLOCK)
        for ref, lo, size in ((mg, 0, n_mixed), (pg, n_mixed, n_pre), (stagez.at[0], base, width)):
            small_v[0:1, lo : lo + size] += jnp.sum(ref[rows, :].astype(F32), axis=0, keepdims=True)
        return 0

    def collect_norm(i):
        collect_half(1, i)
        rows = slice(i * BLOCK, (i + 1) * BLOCK)
        mu, inv = mean_p[rows, :], rstd_p[rows, :]
        one = jnp.zeros((BLOCK, 1), F32)
        two = jnp.zeros((BLOCK, 1), F32)
        for t in range(width // 128):
            lanes = slice(t * 128, (t + 1) * 128)
            g = dv_s[t, rows, :]
            hat = (stagez[1, rows, lanes].astype(F32) - mu) * inv
            sg = g * gain_own_p[:, lanes]
            one = one + jnp.sum(sg, axis=1, keepdims=True)
            two = two + jnp.sum(sg * hat, axis=1, keepdims=True)
            lo = base + width + t * 128
            small_v[0:1, lo : lo + 128] += jnp.sum(g * hat, axis=0, keepdims=True)
            lo = base + 2 * width + t * 128
            small_v[0:1, lo : lo + 128] += jnp.sum(g, axis=0, keepdims=True)
        packed = jnp.where(lane_at == 0, one, jnp.where(lane_at == 1, two, 0.0))
        tot[0, :, rows] = jnp.transpose(packed)[0:8, :]

    def small_copy(b):
        return remote(small_v, small_r.at[b], sm_send_p.at[b], sm_recv_p.at[b], to(peer(b), r, c))

    lax.fori_loop(0, tokens // 64, norm_rows, 0)
    advance_cot(1)
    weights_second(range(3))
    weights_wait((3,))
    lax.fori_loop(0, n_blocks, fc1_rows, 0)
    fc2_grad(0, 0)
    theirs_came(0)
    fc2_grad(1, 0)
    fc2_grad(0, 1)
    weights_wait(range(3))
    lax.fori_loop(0, n_blocks, qkv_rows, 0)
    advance_cot(2)
    weights_first(range(4, 6))
    for p, k in ((0, 0), (1, 0), (0, 1)):
        fc2_next(p, 0, k)
    fc2_grad(0, 2)
    lse[...] = jnp.zeros_like(lse)
    for i in range(n_blocks):
        if i == n_blocks - 2:
            theirs_came(1)
            fc2_grad(1, 1)
            fc2_next(0, 0, 2)
            weights_second(range(4, 6))
        if i == n_blocks - 1:
            advance_cot(3)
            fc2_grad(0, 3)
            fc2_next(1, 0, 1)
        forward_block(i)
    dense_grad(0)
    fc2_next(0, 0, 3)
    weights_wait(range(4, 6))
    for way in (g_way, x_way):
        drain(way, r, 0)
        drain(way, other, 1)
    drain(x_low, r, 0)
    for s in range(n_col):
        low_over(s).wait_send()
    g_over.wait_send()
    x_over.wait_send()
    pl.semaphore_signal(free_sem.at[0], inc=1, **across)
    n_full = n_blocks // 2
    for i in range(n_full):
        out_full(i)
    pl.semaphore_wait(free_sem.at[0], 1)
    theirs_came(2)
    fc2_grad(1, 2)
    sum_next("dense", 0, 0)
    for i in range(n_full, n_blocks):
        send_theirs(0, i)
    fc2_next(1, 0, 2)
    theirs_came(3)
    fc2_grad(1, 3)
    lax.fori_loop(0, n_blocks, grad_rows, 0)
    dense_grad(1)
    fc2_next(1, 0, 3)
    fc1_grad(1)
    sum_next("dense", 1, 0)
    drain(c_way, r, 0)
    for s in range(n_col):
        cot_over(s).wait_send()
    pl.semaphore_signal(free_sem.at[1], inc=1, **across)
    fc1_grad(0)
    sum_next("fc1", 1, 0)
    fc2_rest()
    scatter(0, n_full)
    sum_next("fc1", 0, 0)
    sum_rest("dense")
    dk_s[...] = jnp.zeros_like(dk_s)
    dv_s[...] = jnp.zeros_like(dv_s)
    pl.semaphore_wait(free_sem.at[1], 1)
    for i in reversed(range(n_blocks)):
        backward_block(i)
        finish_mixed(i)
        send_theirs(1, i)
        if i == n_blocks - 1:
            for m in range(n_full + 1, n_blocks):
                scatter(0, m)
        if i == n_blocks // 2:
            spread_first("fc2")
            sum_rest("fc1")
    for p in (1, 0):
        qkv_grad(p)
    loads = [
        pltpu.make_async_copy(ref, stagez.at[m], stage_sem.at[2 + m])
        for m, ref in enumerate((cot_p, x_p))
    ]
    for load in loads:
        load.start()
    small_v[...] = jnp.zeros_like(small_v)
    scatter(1, n_blocks - 1)
    for p in (1, 0):
        sum_next("qkv", p, 0)
    spread_first("dense")
    scatter(1, n_blocks - 2)
    spread_first("fc1")
    for load in loads:
        load.wait()
    lax.fori_loop(0, n_blocks, column_sums, 0)
    for i in range(n_full):
        collect_full(i)
    scatter(1, 1)
    sum_rest("qkv")
    for i in range(n_full, n_blocks):
        collect_half(0, i)
    spread_rest("fc2")
    scatter(1, 0)
    for i in range(n_full):
        swap_out(i).wait_recv()
    for i in range(n_blocks):
        rows = slice(i * BLOCK, (i + 1) * BLOCK)
        v = stagez[1, rows, :].astype(F32) + in_grad_p[rows, :] + out_bias_p[...]
        if i < n_full:
            v = v + xl_p[rows, :].astype(F32)
        y_out_p[rows, :] = v.astype(BF)
    spread_rest("dense")
    for i in (3, 2):
        collect_norm(i)
    spread_first("qkv")
    collect_norm(1)
    spread_rest("fc1")
    collect_norm(0)
    swap = remote(tot.at[0], tot.at[1], tot_send_p.at[0], tot_recv_p.at[0], across)
    swap.start()
    small_copy(0).start()
    swap.wait()
    tot[0] = tot[0] + tot[1]
    tot_copies = [
        remote(
            tot.at[0],
            tot.at[1 + s],
            tot_send_p.at[s],
            tot_recv_p.at[s],
            to(d, r, lax.rem(c + s, n_col)),
        )
        for s in range(1, n_col)
    ]
    for copy in tot_copies:
        copy.start()
    for b in range(n_bits):
        small_copy(b).wait()
        small_v[...] = small_v[...] + small_r[b]
        if b + 1 < n_bits:
            small_copy(b + 1).start()
    small_p[...] = small_v[...]
    for copy in tot_copies:
        copy.wait()
    tot[1] = tot[0]
    for s in range(1, n_col):
        tot[1] = tot[1] + tot[1 + s]

    def in_final(i, _):
        rows = at(i * BLOCK, BLOCK)
        mu, inv = mean_p[rows, :], rstd_p[rows, :]
        sums = jnp.transpose(
            jnp.concatenate([tot[1, :, rows], jnp.zeros((120, BLOCK), F32)], axis=0)
        ) * (1.0 / full)
        one, two = sums[:, 0:1], sums[:, 1:2]
        for t in range(width // 128):
            lanes = slice(t * 128, (t + 1) * 128)
            hat = (stagez[1, rows, lanes].astype(F32) - mu) * inv
            sg = dv_s[t, rows, :] * gain_own_p[:, lanes]
            in_grad_p[rows, lanes] = stagez[0, rows, lanes].astype(F32) + inv * (
                sg - one - hat * two
            )
        return 0

    lax.fori_loop(0, n_blocks, in_final, 0)
    spread_rest("qkv")
    for name in tensors:
        spread_next(name, 0)
    for name in tensors:
        finish(name)
    for i in range(6):
        weight_across(i).wait_send()
        weight_up(i).wait_send()
        for h in range(2):
            weight_share(i, h).wait_send()
    for i in range(n_full):
        swap_out(i).wait_send()
        for s in range(1, n_col):
            for h in range(2):
                full_on(i, s, h).wait_send()
    for n in range(2):
        for i in range(n_full if n == 0 else 0, n_blocks):
            for s in range(1, n_col):
                part_on(n, i, s).wait_send()


def local(
    block_input,
    segment_ids,
    positions,
    ln_gain,
    ln_bias,
    qkv_weight,
    qkv_bias,
    dense_weight,
    dense_bias,
    fc1_weight,
    fc1_bias,
    fc2_weight,
    fc2_bias,
    cotangent,
):
    n_col = lax.axis_size("col")
    n_dp = lax.axis_size("dp")
    n_bits = n_dp.bit_length() - 1
    tokens, width = block_input.shape
    full = width * n_col * 2
    half = full // 2
    qw = qkv_weight.shape[2] // 2
    hid = fc1_weight.shape[1] // 2
    pairs = qw // 128
    small_w = 3 * qw + hid + 3 * width
    vec = jnp.concatenate(
        [
            ln_gain.astype(F32),
            ln_bias.astype(F32),
            dense_bias + fc2_bias,
            qkv_bias.reshape(-1),
            fc1_bias.reshape(-1),
        ]
    )[None]
    lane = np.arange(128) % HEAD_DIM
    steps = (lane % (ROT_DIM // 2)).astype(np.float32)
    freq = np.exp(steps * np.float32(-2.0 * math.log(10000.0) / ROT_DIM), dtype=np.float32)
    freq = jnp.asarray(np.where(lane < ROT_DIM, freq, np.float32(0.0))[None])
    hbm = pl.BlockSpec(memory_space=pl.ANY)
    vmem = pl.BlockSpec(memory_space=pltpu.VMEM)
    dma = pltpu.SemaphoreType.DMA
    bits = max(n_bits, 1)
    sds = jax.ShapeDtypeStruct
    outs = (
        (vmem, sds((tokens, width), BF)),
        (vmem, sds((tokens, width), F32)),
        (vmem, sds((8, small_w), F32)),
        (hbm, sds((half, 2 * hid), BF)),
        (hbm, sds((2, hid, half), BF)),
        (hbm, sds((2, qw, half), BF)),
        (hbm, sds((3, half, 2 * qw), BF)),
        (hbm, sds((2, half, hid), BF)),
        (hbm, sds((2, qw, half), BF)),
        (hbm, sds((2, 3, half, qw), BF)),
        (hbm, sds((n_col - 1, tokens, width), BF)),
        (hbm, sds((n_col - 1, tokens, width), BF)),
        (hbm, sds((n_col - 1, 2, tokens, width), BF)),
    )
    v = pltpu.VMEM
    scratch = [
        v((tokens, full), BF),
        v((tokens, full), BF),
        v((16, full), F32),
        v((full, 3 * qw), BF),
        v((full, hid), BF),
        v((hid, full), BF),
        v((qw, full), BF),
        v((tokens, full), BF),
        v((tokens, hid), BF),
        v((tokens, hid), BF),
        v((pairs, tokens, 128), BF),
        v((pairs, tokens, 128), BF),
        v((pairs, tokens, 128), BF),
        v((pairs, tokens, 128), F32),
        v((pairs, tokens, 128), F32),
        v((BLOCK, tokens), F32),
        v((tokens, 128), F32),
        v((tokens, 128), F32),
        v((tokens, qw), BF),
        v((tokens, qw), BF),
        v((tokens, 3 * qw), BF),
        v((tokens, 128), F32),
        v((2, half, hid), BF),
        v((2, hid, half), BF),
        v((2, qw, half), BF),
        v((2, 3, half, qw), BF),
        v((half // 2, hid), BF),
        v((qw // 2, half), BF),
        v((3, half // 2, qw), BF),
        v((2, tokens, width), BF),
        v((n_col - 1, 2, BLOCK, width), BF),
        v((tokens, width), BF),
        v((16, width), F32),
        v((tokens, 128), F32),
        v((2, hid - (hid >> bits), half), BF),
        v((tokens, 1), F32),
        v((tokens, 1), F32),
        v((n_col + 1, 8, tokens), F32),
        v((8, small_w), F32),
        v((bits, 8, small_w), F32),
        dma((2, 3, n_col)),
        dma((2, n_col)),
        dma((1, 2, n_col)),
        dma((1, n_col)),
        dma((n_col,)),
        dma((n_col,)),
        dma((2, 3, n_col)),
        dma((2, n_col)),
        dma((1, 2, n_col)),
        dma((1, n_col)),
        dma((n_col,)),
        dma((n_col,)),
        dma((6,)),
        dma((6,)),
        dma((6,)),
        dma((6,)),
        dma((6, 2)),
        dma((6, 2)),
        dma((9,)),
        dma((4, 2, bits, n_col)),
        dma((4, 2, bits, n_col)),
        dma((4,)),
        dma((4,)),
        dma((4, bits)),
        dma((4, bits)),
        dma((4,)),
        dma((4,)),
        dma((2, tokens // BLOCK)),
        dma((2, tokens // BLOCK)),
        dma((2, tokens // BLOCK, n_col - 1)),
        dma((2, tokens // BLOCK, n_col - 1)),
        dma((tokens // BLOCK, n_col - 1, 2)),
        dma((tokens // BLOCK, n_col - 1, 2)),
        dma((tokens // BLOCK,)),
        dma((tokens // BLOCK,)),
        dma((n_col,)),
        dma((n_col,)),
        dma((bits,)),
        dma((bits,)),
        pltpu.SemaphoreType.REGULAR((2,)),
    ]
    res = pl.pallas_call(
        functools.partial(kernel, n_dp, n_col),
        out_shape=tuple(o[1] for o in outs),
        in_specs=[hbm] * 6 + [vmem] * 3,
        out_specs=tuple(o[0] for o in outs),
        scratch_shapes=scratch,
        compiler_params=pltpu.CompilerParams(
            collective_id=0,
            has_side_effects=True,
            vmem_limit_bytes=64 * 2**20,
            fuse_transposed_lhs_in_matmul=True,
        ),
        cost_estimate=pl.CostEstimate(
            flops=45 * 10**9, bytes_accessed=64 * 2**20, transcendentals=8 * 2**20
        ),
    )(
        block_input,
        cotangent,
        jnp.transpose(qkv_weight, (1, 0, 2)),
        fc1_weight,
        fc2_weight,
        dense_weight,
        vec,
        jnp.stack([segment_ids, positions]).astype(F32),
        freq,
    )
    y_out, in_grad, small, f1, f2, fd, fq = res[:7]
    small = small[0]
    n_mixed = 3 * qw
    base = n_mixed + hid
    bias_grad, gain_grad, shift_grad = (
        small[base + i * width : base + (i + 1) * width] for i in range(3)
    )
    return (
        y_out,
        in_grad,
        gain_grad,
        shift_grad,
        jnp.transpose(fq.astype(F32), (1, 0, 2)),
        small[:n_mixed].reshape(qkv_bias.shape),
        fd.reshape(dense_weight.shape).astype(F32),
        bias_grad,
        f1.astype(F32),
        small[n_mixed:base].reshape(fc1_bias.shape),
        f2.reshape(fc2_weight.shape).astype(F32),
        bias_grad,
    )


def solution(mesh):
    return jax.shard_map(
        local,
        mesh=mesh,
        in_specs=(
            P("dp", ("row", "col")),
            P("dp"),
            P("dp"),
            P(("row", "col")),
            P(("row", "col")),
            P("row", None, "col"),
            P(None, "col", "row", None),
            P("col", "row"),
            P(("row", "col")),
            P("row", "col"),
            P("col", "row", None),
            P("col", "row"),
            P(("row", "col")),
            P("dp", ("row", "col")),
        ),
        out_specs=(
            P("dp", ("row", "col")),
            P("dp", ("row", "col")),
            P(("row", "col")),
            P(("row", "col")),
            P("row", None, "col"),
            P(None, "col", "row", None),
            P("col", "row"),
            P(("row", "col")),
            P("row", "col"),
            P("col", "row", None),
            P("col", "row"),
            P(("row", "col")),
        ),
        check_vma=False,
    )
```

```python
import functools
import math

import jax
import jax.numpy as jnp
import numpy as np
from jax import lax
from jax.experimental import pallas as pl
from jax.experimental.pallas import tpu as pltpu
from jax.sharding import PartitionSpec as P

HEAD_DIM = 64
ROT_DIM = 32
NORM_EPSILON = 1e-05
MASKED_SCORE = -1e30
BLOCK = 256
MESH = pl.DeviceIdType.MESH
BF = jnp.bfloat16
F32 = jnp.float32
GELU_A = math.sqrt(2.0 / math.pi)
GELU_B = 0.044715
NN = (((1,), (0,)), ((), ()))
NT = (((1,), (1,)), ((), ()))
TN = (((0,), (0,)), ((), ()))


def dot(a, b, dims):
    return lax.dot_general(a, b, dims, preferred_element_type=F32)


def kernel(
    n_dp,
    n_col,
    x_p,
    cot_p,
    wq_p,
    w1_p,
    w2_p,
    wd_p,
    vec_p,
    qkv_bias_p,
    fc1_bias_p,
    token_p,
    freq_p,
    y_out_p,
    in_grad_p,
    small_p,
    f1_p,
    f2_p,
    fd_p,
    fq_p,
    rb1_p,
    rbd_p,
    rbq_p,
    rzo_p,
    rzn_p,
    rza_p,
    xf_p,
    cf_p,
    gf_p,
    wqf_p,
    w1f_p,
    w2f_p,
    wdf_p,
    normed_p,
    hidden_p,
    pg_p,
    q_p,
    k_p,
    v_p,
    dk_p,
    dv_p,
    bias_p,
    cos_p,
    sin_p,
    ctx_p,
    dctx_p,
    mg_p,
    lse_p,
    g1_p,
    g2_p,
    gd_p,
    gq_p,
    stage1_p,
    staged_p,
    stageq_p,
    stagez_p,
    stageo_p,
    xl_p,
    gb_p,
    places_p,
    rb2_p,
    mean_p,
    rstd_p,
    tot_p,
    small_v_p,
    small_r_p,
    x_send_p,
    x_recv_p,
    v_send_p,
    v_recv_p,
    vx_send_p,
    vx_recv_p,
    g_send_p,
    g_recv_p,
    c_send_p,
    c_recv_p,
    cx_send_p,
    cx_recv_p,
    w_send_p,
    w_recv_p,
    y_send_p,
    y_recv_p,
    s_send_p,
    s_recv_p,
    load_sem_p,
    rs_send_p,
    rs_recv_p,
    xs_send_p,
    xs_recv_p,
    ag_send_p,
    ag_recv_p,
    part_sem_p,
    stage_sem_p,
    ox_send_p,
    ox_recv_p,
    oz_send_p,
    oz_recv_p,
    za_send_p,
    za_recv_p,
    xo_send_p,
    xo_recv_p,
    tot_send_p,
    tot_recv_p,
    sm_send_p,
    sm_recv_p,
    free_sem_p,
):
    xf, cf, gf = xf_p, cf_p, gf_p
    wqf, w1f, w2f, wdf = wqf_p, w1f_p, w2f_p, wdf_p
    normed, hidden, pg = normed_p, hidden_p, pg_p
    q_s, k_s, v_s, dk_s, dv_s = q_p, k_p, v_p, dk_p, dv_p
    ctx, dctx, mg, lse = ctx_p, dctx_p, mg_p, lse_p
    cos_ref, sin_ref, bias_s = cos_p, sin_p, bias_p
    load_sem, stage_sem = load_sem_p, stage_sem_p

    d = lax.axis_index("dp")
    r = lax.axis_index("row")
    c = lax.axis_index("col")
    n_bits = n_dp.bit_length() - 1
    core = lax.rem(d, 2)
    sibling = d + 1 - 2 * core
    other = 1 - r
    has_right = c < n_col - 1
    has_left = c > 0
    right = jnp.minimum(c + 1, n_col - 1)
    left = jnp.maximum(c - 1, 0)
    tokens, width = x_p.shape
    full = width * n_col * 2
    half = full // 2
    heads_w = qw = ctx.shape[1]
    pairs = heads_w // 128
    n_blocks = tokens // BLOCK
    scale = HEAD_DIM**-0.5

    def to(dd, rr, cc):
        return dict(device_id=(dd, rr, cc), device_id_type=MESH)

    def bit(b):
        return lax.rem(lax.div(d, 1 << b), 2)

    def peer(b):
        return d + (1 - 2 * bit(b)) * (1 << b)

    def remote(src, dst, send, recv, dev):
        return pltpu.make_async_remote_copy(
            src_ref=src, dst_ref=dst, send_sem=send, recv_sem=recv, **dev
        )

    def at(start, size):
        return pl.ds(pl.multiple_of(start, math.gcd(size, 256)), size)

    across = to(d, other, c)

    barrier = pltpu.get_barrier_semaphore()
    pl.semaphore_signal(barrier, inc=1, **across)
    for s in range(1, n_col):
        pl.semaphore_signal(barrier, inc=1, **to(d, r, lax.rem(c + s, n_col)))
    for b in range(n_bits):
        pl.semaphore_signal(barrier, inc=1, **to(peer(b), r, c))
    pl.semaphore_wait(barrier, 1 + (n_col - 1) + n_bits)

    gain_own_p = vec_p.at[0:1, :]
    out_bias_p = vec_p.at[2:3, :]
    gb_p[0:8, :] = jnp.broadcast_to(vec_p[0:1, :], (8, width))
    gb_p[8:16, :] = jnp.broadcast_to(vec_p[1:2, :], (8, width))

    top = slice(0, tokens // 2)
    low = slice(tokens // 2, tokens)

    def block(ref, rr, j, rows=slice(None)):
        return ref.at[rows, at((rr * n_col + j) * width, width)]

    def hop(way, own, rr, j, lane, step):
        whole, mine_ref, send, recv, rows = way
        dst = block(whole, rr, j, rows)
        return remote(
            mine_ref if own else dst,
            dst,
            send.at[lane, step, j],
            recv.at[lane, j],
            to(d, r, right if step == 0 else left),
        )

    def over(way, own, j, send, recv):
        dst = block(way[0], r, j, way[4])
        return remote(way[1] if own else dst, dst, send, recv, across)

    def landed(dst, recv):
        return remote(dst, dst, recv, recv, across)

    def start_hop(cond, way, own, rr, j, lane, step):
        @pl.when(cond)
        def _():
            hop(way, own, rr, j, lane, step).start()

    def start_both(way, own, rr, lane):
        start_hop(has_right, way, own, rr, c, lane, 0)
        start_hop(has_left, way, own, rr, c, lane, 1)

    def advance(way, rr, lane, s, then=None):
        whole, _, _, recv, rows = way

        @pl.when(c >= s)
        def _():
            j = c - s
            landed(block(whole, rr, j, rows), recv.at[lane, j]).wait_recv()
            start_hop(has_right, way, False, rr, j, lane, 0)
            if then is not None:
                then(j)

        @pl.when(c + s < n_col)
        def _():
            j = c + s
            landed(block(whole, rr, j, rows), recv.at[lane, j]).wait_recv()
            start_hop(has_left, way, False, rr, j, lane, 1)
            if then is not None:
                then(j)

    def drain(way, rr, lane):
        for s in range(n_col):

            @pl.when((c >= s) & has_right)
            def _():
                hop(way, False, rr, jnp.maximum(c - s, 0), lane, 0).wait_send()

            @pl.when((c + s < n_col) & has_left)
            def _():
                j = jnp.minimum(c + s, n_col - 1)
                hop(way, False, rr, j, lane, 1).wait_send()

    def piece(i, k, rr):
        if i < 3:
            depth = wq_p.shape[1] // 4
            return (
                wq_p.at[i, at(k * depth, depth), at((1 - rr) * qw, qw)],
                wqf.at[at((rr * 4 + k) * depth, depth), i * qw : (i + 1) * qw],
            )
        if i == 3:
            depth, part = w1_p.shape[0] // 4, w1_p.shape[1] // 2
            return (
                w1_p.at[at(k * depth, depth), at((1 - rr) * part, part)],
                w1f.at[at((rr * 4 + k) * depth, depth), :],
            )
        src, dst = (w2_p, w2f) if i == 4 else (wd_p, wdf)
        depth, part = src.shape[0] // 8, src.shape[1]
        return (
            src.at[at(((1 - rr) * 4 + k) * depth, depth), :],
            dst.at[at(k * depth, depth), at(rr * part, part)],
        )

    w_send, w_recv, y_send, y_recv = w_send_p, w_recv_p, y_send_p, y_recv_p
    s_send, s_recv = s_send_p, s_recv_p
    upper = bit(1)
    quarter = (core + 2 * upper, core + 2 * (1 - upper))
    quarter_sib = (1 - core + 2 * upper, 1 - core + 2 * (1 - upper))

    def weight_across(i):
        src, dst = piece(i, quarter[0], r)
        return remote(src, dst, w_send.at[i], w_recv.at[i], across)

    def weight_up(i):
        dst = piece(i, quarter[0], other)[1]
        return remote(dst, dst, y_send.at[i], y_recv.at[i], to(peer(1), r, c))

    def weight_share(i, h):
        dst = piece(i, quarter[h], other)[1]
        return remote(dst, dst, s_send.at[i, h], s_recv.at[i, h], to(sibling, r, c))

    def weights_first(group):
        for i in group:
            landed(piece(i, quarter[0], other)[1], w_recv.at[i]).wait_recv()
            weight_up(i).start()
            weight_share(i, 0).start()

    def weights_second(group):
        for i in group:
            landed(piece(i, quarter[1], other)[1], y_recv.at[i]).wait_recv()
            weight_share(i, 1).start()

    def weights_wait(group):
        for i in group:
            for h in range(2):
                landed(piece(i, quarter_sib[h], other)[1], s_recv.at[i, h]).wait_recv()

    x_way = (xf, x_p.at[top, :], x_send_p, x_recv_p, top)
    x_low = (xf, x_p.at[low, :], v_send_p, v_recv_p, low)
    g_way = (gf, gb_p, g_send_p, g_recv_p, slice(None))
    c_way = (cf, cot_p, c_send_p, c_recv_p, slice(None))
    cx_send, cx_recv, vx_send, vx_recv = cx_send_p, cx_recv_p, vx_send_p, vx_recv_p
    g_over = over(g_way, True, c, g_send_p.at[1, 2, c], g_recv_p.at[1, c])
    x_over = over(x_way, True, c, x_send_p.at[1, 2, c], x_recv_p.at[1, c])

    def low_over(j, own=False):
        return over(x_low, own, j, vx_send.at[j], vx_recv.at[j])

    def cot_over(j, own=False):
        return over(c_way, own, j, cx_send.at[j], cx_recv.at[j])

    g_over.start()
    x_over.start()
    low_over(c, True).start()
    for way in (g_way, x_way, x_low):
        start_both(way, True, r, 0)

    own = [(x_p, block(xf, r, c)), (gb_p, block(gf, r, c)), (cot_p, block(cf, r, c))]
    depth = wq_p.shape[1]
    for s in range(3):
        own.append((wq_p.at[s, :, at(r * qw, qw)], wqf.at[at(r * depth, depth), s * qw : (s + 1) * qw]))
    depth, part = w1_p.shape[0], w1_p.shape[1] // 2
    own.append((w1_p.at[:, at(r * part, part)], w1f.at[at(r * depth, depth), :]))
    for src, dst in ((w2_p, w2f), (wd_p, wdf)):
        depth, part = src.shape[0] // 2, src.shape[1]
        own.append((src.at[at(r * depth, depth), :], dst.at[:, at(r * part, part)]))
    own = [pltpu.make_async_copy(a, b, load_sem.at[i]) for i, (a, b) in enumerate(own)]
    for copy in own:
        copy.start()

    def tables(i, _):
        rows = at(i * BLOCK, BLOCK)
        wide = jnp.concatenate([token_p[:, rows], jnp.zeros((126, BLOCK), F32)], axis=0)
        places_p[rows, :] = jnp.transpose(wide)
        angle = places_p[rows, 1:2] * freq_p[...]
        cos_ref[rows, :] = jnp.cos(angle)
        sin_ref[rows, :] = jnp.sin(angle)
        return 0

    for i in (3, 0, 1, 2):
        weight_across(i).start()
    for way in (g_way, x_way):
        landed(block(way[0], other, c, way[4]), way[3].at[1, c]).wait_recv()
        start_both(way, False, other, 1)

    def start_cot(s):
        start_hop(has_right & (c == s), c_way, True, r, c, 0, 0)
        start_hop(has_left & (c == n_col - 1 - s), c_way, True, r, c, 0, 1)

    start_cot(0)
    lax.fori_loop(0, n_blocks, tables, 0)
    for s in range(1, n_col):
        advance(g_way, r, 0, s)
        advance(x_way, r, 0, s)
        advance(x_low, r, 0, s, then=lambda j: low_over(j).start())
        advance(g_way, other, 1, s)
        advance(x_way, other, 1, s)
        start_cot(s)
        if s == 1:
            cot_over(c, True).start()
        if s == 2:
            weights_first((3,))
        if s == 3:
            for i in range(4, 6):
                weight_across(i).start()
            weights_first(range(3))
            weights_second((3,))

    def advance_cot(s):
        advance(c_way, r, 0, s, then=lambda j: cot_over(j).start())

    for copy in own:
        copy.wait()
    for s in range(n_col):
        landed(block(xf, other, s, low), vx_recv.at[s]).wait_recv()

    gain = gf[0:1, :]
    shift = gf[8:9, :]

    def norm_rows(i, _):
        rows = at(i * 64, 64)
        v = xf[rows, :].astype(F32)
        mu = jnp.sum(v, axis=1, keepdims=True) * (1.0 / full)
        v = v - mu
        inv = lax.rsqrt(jnp.sum(v * v, axis=1, keepdims=True) * (1.0 / full) + NORM_EPSILON)
        mean_p[rows, :] = mu
        rstd_p[rows, :] = inv
        normed[rows, :] = (v * inv * gain + shift).astype(BF)
        return 0


    lane_at = lax.broadcasted_iota(jnp.int32, (1, 128), 1)
    first = lane_at % HEAD_DIM < ROT_DIM // 2
    low_head = lane_at < HEAD_DIM

    def turn(v, cos, sin, sign):
        up = pltpu.roll(v, 128 - ROT_DIM // 2, 1)
        down = pltpu.roll(v, ROT_DIM // 2, 1)
        swapped = jnp.where(first, -up, down) * sin
        return v * cos + swapped if sign > 0 else v * cos - swapped

    def qkv_rows(i, _):
        rows = at(i * BLOCK, BLOCK)
        mixed = dot(normed[rows, :], wqf[...], NN)
        cos, sin = cos_ref[rows, :], sin_ref[rows, :]
        for s, dst in enumerate((q_s, k_s, v_s)):
            for t in range(pairs):
                lanes = slice(s * qw + t * 128, s * qw + (t + 1) * 128)
                v = mixed[:, lanes] + qkv_bias_p[s, 0, 0:1, t * 128 : (t + 1) * 128]
                dst[t, rows, :] = (turn(v, cos, sin, 1) if s < 2 else v).astype(BF)
        return 0


    def fc1_rows(i, _):
        rows = at(i * BLOCK, BLOCK)
        for h in range(2):
            cols = slice(h * 512, (h + 1) * 512)
            v = dot(normed[rows, :], w1f[:, cols], NN) + fc1_bias_p[0, 0:1, cols]
            th = jnp.tanh(GELU_A * (v + GELU_B * v * v * v))
            hidden[rows, cols] = (0.5 * v * (1.0 + th)).astype(BF)
            slope = 0.5 * (1.0 + th) + 0.5 * v * (1.0 - th * th) * (
                GELU_A * (1.0 + 3.0 * GELU_B * v * v)
            )
            pg[rows, cols] = slope.astype(BF)
        return 0

    def set_bias(i):
        keys = (i + 1) * BLOCK
        rows = slice(i * BLOCK, keys)
        row_at = lax.broadcasted_iota(jnp.int32, (BLOCK, keys), 0) + i * BLOCK
        key_at = lax.broadcasted_iota(jnp.int32, (BLOCK, keys), 1)
        allowed = (places_p[rows, 0:1] == token_p[0:1, :keys]) & (row_at >= key_at)
        bias_s[:, :keys] = jnp.where(allowed, 0.0, MASKED_SCORE)

    def mine(h, v):
        return jnp.where(low_head if h == 0 else ~low_head, v, jnp.zeros_like(v))

    def forward_block(i):
        keys = (i + 1) * BLOCK
        rows = slice(i * BLOCK, keys)
        set_bias(i)

        def pair(t, _):
            q, k, v = q_s[t, rows, :], k_s[t, :keys, :], v_s[t, :keys, :]
            outs = []
            logs = lse[rows, :]
            for h in range(2):
                s = dot(mine(h, q), k, NT) * scale + bias_s[:, :keys]
                top = jnp.max(s, axis=1, keepdims=True)
                e = jnp.exp(s - top)
                total = jnp.sum(e, axis=1, keepdims=True)
                low = (e * (1.0 / total)).astype(BF)
                outs.append(dot(low, v, NN))
                logs = jnp.where(lane_at == 2 * t + h, top + jnp.log(total), logs)
            lse[rows, :] = logs
            ctx[rows, at(t * 128, 128)] = jnp.where(low_head, outs[0], outs[1]).astype(BF)
            return 0

        lax.fori_loop(0, pairs, pair, 0)

    rs_send, rs_recv, xs_send, xs_recv = rs_send_p, rs_recv_p, xs_send_p, xs_recv_p
    ag_send, ag_recv, part_sem = ag_send_p, ag_recv_p, part_sem_p
    g1, g2, gd, gq = g1_p, g2_p, gd_p, gq_p
    tensors = dict(
        fc1=(0, g1, rb1_p, stage1_p, half),
        fc2=(1, g2, rb2_p, None, hidden.shape[1]),
        dense=(2, gd, rbd_p, staged_p, heads_w),
        qkv=(3, gq, rbq_p, stageq_p, half),
    )
    results = dict(fc1=f1_p, fc2=f2_p, dense=fd_p, qkv=fq_p)
    mine_at, theirs_at = r * half, other * half
    starts = (mine_at, theirs_at)

    def slab(ref, p, rows):
        return ref.at[p, :, rows, :] if len(ref.shape) == 4 else ref.at[p, rows, :]

    def offset(rows, upto):
        off = 0
        for b in range(upto):
            off = off + bit(b) * (rows >> (b + 1))
        return off

    def landing(rows, b):
        return slice(rows - (rows >> b), rows - (rows >> (b + 1)))

    def nth(k):
        j = c
        for here in range(n_col):
            turn_k = sorted(range(n_col), key=lambda v: (abs(v - here), v))[k]
            j = jnp.where(c == here, turn_k, j)
        return j

    def sum_copy(name, p, b, k=0):
        n, g, rb, _, rows = tensors[name]
        size = rows >> (b + 1)
        src = slab(g, p, at(offset(rows, b) + (1 - bit(b)) * size, size))
        dst = slab(rb, p, landing(rows, b))
        if name == "fc2":
            cols = at(nth(k) * width, width)
            src, dst = src.at[:, cols], dst.at[:, cols]
        return remote(src, dst, rs_send.at[n, p, b, k], rs_recv.at[n, p, b, k], to(peer(b), r, c))

    def place(name, rr, off, size):
        if name == "fc1":
            return f1_p.at[at(off, size), at(rr * hidden.shape[1], hidden.shape[1])]
        if name == "qkv":
            return fq_p.at[:, at(off, size), at(rr * qw, qw)]
        return results[name].at[rr, at(off, size), :]

    def kept(name, p):
        _, g, _, _, rows = tensors[name]
        size = rows >> n_bits
        off = offset(rows, n_bits)
        return slab(g, p, at(off, size)), off, size

    def part_copy(name):
        src, off, size = kept(name, 0)
        return pltpu.make_async_copy(src, place(name, r, off, size), part_sem.at[tensors[name][0]])

    def swap_copy(name):
        src, off, size = kept(name, 1)
        n = tensors[name][0]
        return remote(src, place(name, r, off, size), xs_send.at[n], xs_recv.at[n], across)

    def fc2_next(p, b, k):
        _, g, rb, _, rows = tensors["fc2"]
        size = rows >> (b + 1)
        off = offset(rows, b + 1)
        cols = at(nth(k) * width, width)
        sum_copy("fc2", p, b, k).wait_recv()
        chunk = min(size, 128)

        def add(i, _):
            there = (p, at(off + i * chunk, chunk), cols)
            here = (p, at(rows - (rows >> b) + i * chunk, chunk), cols)
            g[there] = (g[there].astype(F32) + rb[here].astype(F32)).astype(BF)
            return 0

        lax.fori_loop(0, size // chunk, add, 0)
        if b + 1 < n_bits:
            sum_copy("fc2", p, b + 1, k).start()

    def sum_next(name, p, b):
        n, g, rb, stage, rows = tensors[name]
        size = rows >> (b + 1)
        off = offset(rows, b + 1)
        sum_copy(name, p, b).wait_recv()
        four = len(g.shape) == 4
        chunk = min(size, 128)
        dst = stage.at[:, :size, :] if four else stage.at[:size, :]
        copy = pltpu.make_async_copy(slab(rb, p, landing(rows, b)), dst, stage_sem.at[0])
        copy.start()
        copy.wait()

        def add(i, _):
            if four:
                there = (p, slice(None), at(off + i * chunk, chunk), slice(None))
                here = (slice(None), at(i * chunk, chunk), slice(None))
            else:
                there = (p, at(off + i * chunk, chunk), slice(None))
                here = (at(i * chunk, chunk), slice(None))
            g[there] = (g[there].astype(F32) + stage[here].astype(F32)).astype(BF)
            return 0

        lax.fori_loop(0, size // chunk, add, 0)
        if b + 1 < n_bits:
            sum_copy(name, p, b + 1).start()
        elif p == 0:
            part_copy(name).start()
        else:
            swap_copy(name).start()

    def fc2_rest(p):
        for b in range(1, n_bits):
            for k in range(n_col):
                fc2_next(p, b, k)
        if p == 0:
            part_copy("fc2").start()
        else:
            swap_copy("fc2").start()

    def sum_rest(name, p):
        for b in range(1, n_bits):
            sum_next(name, p, b)

    def spread_copy(name, p, b):
        n, rows = tensors[name][0], tensors[name][4]
        ref = place(name, r if p == 0 else other, offset(rows, b + 1), rows >> (b + 1))
        return remote(ref, ref, ag_send_p.at[n, p, b], ag_recv_p.at[n, p, b], to(peer(b), r, c))

    def spread_landed(name, p, b):
        n, rows = tensors[name][0], tensors[name][4]
        size = rows >> (b + 1)
        off = offset(rows, b) + (1 - bit(b)) * size
        return landed(place(name, r if p == 0 else other, off, size), ag_recv_p.at[n, p, b])

    def spread_first(name, p):
        if p == 0:
            part_copy(name).wait()
        else:
            _, off, size = kept(name, 1)
            landed(place(name, other, off, size), xs_recv_p.at[tensors[name][0]]).wait_recv()
        spread_copy(name, p, n_bits - 1).start()

    def spread_next(name, p, b):
        spread_landed(name, p, b).wait_recv()
        if b > 0:
            spread_copy(name, p, b - 1).start()

    def spread_rest(name, p):
        for b in reversed(range(1, n_bits)):
            spread_next(name, p, b)

    def finish(name):
        for b in range(n_bits):
            for p in range(2):
                for k in range(n_col if name == "fc2" else 1):
                    sum_copy(name, p, b, k).wait_send()
                spread_copy(name, p, b).wait_send()
        swap_copy(name).wait_send()

    def fc2_grad(p, k):
        col = nth(k) * width

        def body(i, _):
            cols = at(i * BLOCK, BLOCK)
            g2[p, cols, at(col, width)] = dot(
                hidden[:, cols], cf[:, at(starts[p] + col, width)], TN
            ).astype(BF)
            return 0

        lax.fori_loop(0, hidden.shape[1] // BLOCK, body, 0)
        sum_copy("fc2", p, 0, k).start()

    def fc1_grad(p):
        def body(i, _):
            g1[p, at(i * BLOCK, BLOCK), :] = dot(
                normed[:, at(starts[p] + i * BLOCK, BLOCK)], pg[...], TN
            ).astype(BF)
            return 0

        lax.fori_loop(0, half // BLOCK, body, 0)
        sum_copy("fc1", p, 0).start()

    def dense_grad(p):
        gd[p] = dot(ctx[...], cf[:, at(starts[p], half)], TN).astype(BF)
        sum_copy("dense", p, 0).start()

    def qkv_grad(p):
        def body(i, _):
            v = dot(normed[:, at(starts[p] + i * BLOCK, BLOCK)], mg[...], TN).astype(BF)
            for s in range(3):
                gq[p, s, at(i * BLOCK, BLOCK), :] = v[:, s * qw : (s + 1) * qw]
            return 0

        lax.fori_loop(0, half // BLOCK, body, 0)
        sum_copy("qkv", p, 0).start()

    ox_send, ox_recv, oz_send, oz_recv = ox_send_p, ox_recv_p, oz_send_p, oz_recv_p
    free_sem = free_sem_p
    outputs = ((xf, rzo_p), (cf, rzn_p))

    def out_part(n, rows, start):
        if n == 0:
            return dot(ctx[rows, :], wdf[:, at(start, half)], NN) + dot(
                hidden[rows, :], w2f[:, at(start, half)], NN
            )
        return dot(mg[rows, :], wqf[at(start, half), :], NT) + dot(
            pg[rows, :], w1f[at(start, half), :], NT
        )

    def part_over(n, i):
        buf = outputs[n][0]
        rows = slice(i * BLOCK, (i + 1) * BLOCK)
        return remote(
            buf.at[rows, :half], buf.at[rows, half:], ox_send.at[n, i], ox_recv.at[n, i], across
        )

    def send_theirs(n, i):
        rows = slice(i * BLOCK, (i + 1) * BLOCK)
        outputs[n][0][rows, :half] = out_part(n, rows, theirs_at).astype(BF)
        part_over(n, i).start()

    def part_on(n, i, s):
        buf, landing_z = outputs[n]
        rows = slice(i * BLOCK, (i + 1) * BLOCK)
        j = lax.rem(c + s, n_col)
        return remote(
            buf.at[rows, at(j * width, width)],
            landing_z.at[s - 1, rows, :],
            oz_send.at[n, i, s - 1],
            oz_recv.at[n, i, s - 1],
            to(d, r, j),
        )

    def scatter(n, i):
        buf = outputs[n][0]
        rows = slice(i * BLOCK, (i + 1) * BLOCK)
        part_over(n, i).wait()
        v = out_part(n, rows, mine_at) + buf[rows, half:].astype(F32)
        bias_s[:, :half] = v
        buf[rows, :half] = v.astype(BF)
        for t in range(width // 128):
            own_part = bias_s[:, at(c * width + t * 128, 128)]
            if n == 0:
                in_grad_p[rows, t * 128 : (t + 1) * 128] = own_part
            else:
                dv_s[t, rows, :] = own_part
        for s in range(1, n_col):
            part_on(n, i, s).start()

    stagez, stageo = stagez_p, stageo_p

    def full_on(i, s, h):
        rows = slice(i * BLOCK, (i + 1) * BLOCK)
        j = lax.rem(c + s, n_col)
        return remote(
            xf.at[rows, at(starts[h] + j * width, width)],
            rza_p.at[s - 1, h, rows, :],
            za_send_p.at[i, s - 1, h],
            za_recv_p.at[i, s - 1, h],
            to(d, r, j),
        )

    def out_full(i):
        rows = slice(i * BLOCK, (i + 1) * BLOCK)
        for start in starts:
            xf[rows, at(start, half)] = out_part(0, rows, start).astype(BF)
        for s in range(1, n_col):
            for h in range(2):
                full_on(i, s, h).start()

    def swap_out(i):
        rows = slice(i * BLOCK, (i + 1) * BLOCK)
        return remote(
            xf.at[rows, at(theirs_at + c * width, width)],
            xl_p.at[rows, :],
            xo_send_p.at[i],
            xo_recv_p.at[i],
            across,
        )

    def collect_full(i):
        rows = slice(i * BLOCK, (i + 1) * BLOCK)
        for s in range(1, n_col):
            for h in range(2):
                full_on(i, s, h).wait_recv()
        load = pltpu.make_async_copy(rza_p.at[:, :, rows, :], stageo, stage_sem.at[1])
        load.start()
        load.wait()
        for h, start in enumerate(starts):
            own = at(start + c * width, width)
            v = xf[rows, own].astype(F32)
            for s in range(n_col - 1):
                v = v + stageo[s, h].astype(F32)
            if h == 0:
                in_grad_p[rows, :] = v
            else:
                xf[rows, own] = v.astype(BF)
        swap_out(i).start()

    def collect_half(n, i):
        rows = slice(i * BLOCK, (i + 1) * BLOCK)
        for s in range(1, n_col):
            part_on(n, i, s).wait_recv()
        landing_z = outputs[n][1]
        load = pltpu.make_async_copy(landing_z.at[:, rows, :], stageo.at[:, 0], stage_sem.at[1])
        load.start()
        load.wait()
        for t in range(width // 128):
            lanes = slice(t * 128, (t + 1) * 128)
            v = stageo[0, 0, :, lanes].astype(F32)
            for s in range(1, n_col - 1):
                v = v + stageo[s, 0, :, lanes].astype(F32)
            if n == 0:
                in_grad_p[rows, lanes] += v
            else:
                dv_s[t, rows, :] += v

    def backward_block(i):
        keys = (i + 1) * BLOCK
        rows = slice(i * BLOCK, keys)
        set_bias(i)

        def pair(t, _):
            lanes = at(t * 128, 128)
            q, k, v = q_s[t, rows, :], k_s[t, :keys, :], v_s[t, :keys, :]
            grad = dctx[rows, lanes]
            query_grads = []
            for h in range(2):
                qh, gh = mine(h, q), mine(h, grad)
                log_total = jnp.sum(
                    jnp.where(lane_at == 2 * t + h, lse[rows, :], 0.0), axis=1, keepdims=True
                )
                p = jnp.exp(dot(qh, k, NT) * scale + bias_s[:, :keys] - log_total)
                dp = dot(gh, v, NT)
                dv_s[t, :keys, :] += dot(p.astype(BF), gh, TN)
                centre = jnp.sum(p * dp, axis=1, keepdims=True)
                ds = (p * (dp - centre) * scale).astype(BF)
                query_grads.append(dot(ds, k, NN))
                dk_s[t, :keys, :] += dot(ds, qh, TN)
            dq = jnp.where(low_head, query_grads[0], query_grads[1])
            mg[rows, lanes] = turn(dq, cos_ref[rows, :], sin_ref[rows, :], -1).astype(BF)
            return 0

        lax.fori_loop(0, pairs, pair, 0)

    def grad_rows(i, _):
        rows = at(i * BLOCK, BLOCK)
        dctx[rows, :] = dot(cf[rows, :], wdf[...], NT).astype(BF)
        for h in range(2):
            cols = slice(h * 512, (h + 1) * 512)
            v = dot(cf[rows, :], w2f[cols, :], NT)
            pg[rows, cols] = (v * pg[rows, cols].astype(F32)).astype(BF)
        return 0

    def theirs_came(k):
        j = nth(k)
        landed(block(cf, other, j), cx_recv.at[j]).wait_recv()

    def finish_mixed(i):
        rows = slice(i * BLOCK, (i + 1) * BLOCK)
        for t in range(pairs):
            lanes = slice(qw + t * 128, qw + (t + 1) * 128)
            mg[rows, lanes] = turn(dk_s[t, rows, :], cos_ref[rows, :], sin_ref[rows, :], -1).astype(BF)
            lanes = slice(2 * qw + t * 128, 2 * qw + (t + 1) * 128)
            mg[rows, lanes] = dv_s[t, rows, :].astype(BF)

    tot, small_v, small_r = tot_p, small_v_p, small_r_p
    n_mixed, n_pre = mg.shape[1], pg.shape[1]
    base = n_mixed + n_pre

    def column_sums(i, _):
        rows = at(i * BLOCK, BLOCK)
        for ref, lo, size in ((mg, 0, n_mixed), (pg, n_mixed, n_pre), (stagez.at[0], base, width)):
            small_v[0:1, lo : lo + size] += jnp.sum(ref[rows, :].astype(F32), axis=0, keepdims=True)
        return 0

    def collect_norm(i):
        collect_half(1, i)
        rows = slice(i * BLOCK, (i + 1) * BLOCK)
        mu, inv = mean_p[rows, :], rstd_p[rows, :]
        one = jnp.zeros((BLOCK, 1), F32)
        two = jnp.zeros((BLOCK, 1), F32)
        for t in range(width // 128):
            lanes = slice(t * 128, (t + 1) * 128)
            g = dv_s[t, rows, :]
            hat = (stagez[1, rows, lanes].astype(F32) - mu) * inv
            sg = g * gain_own_p[:, lanes]
            one = one + jnp.sum(sg, axis=1, keepdims=True)
            two = two + jnp.sum(sg * hat, axis=1, keepdims=True)
            lo = base + width + t * 128
            small_v[0:1, lo : lo + 128] += jnp.sum(g * hat, axis=0, keepdims=True)
            lo = base + 2 * width + t * 128
            small_v[0:1, lo : lo + 128] += jnp.sum(g, axis=0, keepdims=True)
        packed = jnp.where(lane_at == 0, one, jnp.where(lane_at == 1, two, 0.0))
        tot[0, :, rows] = jnp.transpose(packed)[0:8, :]

    def small_copy(b):
        return remote(small_v, small_r.at[b], sm_send_p.at[b], sm_recv_p.at[b], to(peer(b), r, c))

    lax.fori_loop(0, tokens // 64, norm_rows, 0)
    advance_cot(1)
    weights_second(range(3))
    weights_wait((3,))
    lax.fori_loop(0, n_blocks, fc1_rows, 0)
    fc2_grad(0, 0)
    theirs_came(0)
    fc2_grad(1, 0)
    fc2_grad(0, 1)
    weights_wait(range(3))
    lax.fori_loop(0, n_blocks, qkv_rows, 0)
    advance_cot(2)
    weights_first(range(4, 6))
    for p, k in ((0, 0), (1, 0), (0, 1)):
        fc2_next(p, 0, k)
    fc2_grad(0, 2)
    lse[...] = jnp.zeros_like(lse)
    for i in range(n_blocks):
        if i == n_blocks - 2:
            theirs_came(1)
            fc2_grad(1, 1)
            fc2_next(0, 0, 2)
            weights_second(range(4, 6))
        if i == n_blocks - 1:
            advance_cot(3)
            fc2_grad(0, 3)
            fc2_next(1, 0, 1)
        forward_block(i)
    dense_grad(0)
    fc2_next(0, 0, 3)
    weights_wait(range(4, 6))
    for way in (g_way, x_way):
        drain(way, r, 0)
        drain(way, other, 1)
    drain(x_low, r, 0)
    for s in range(n_col):
        low_over(s).wait_send()
    g_over.wait_send()
    x_over.wait_send()
    pl.semaphore_signal(free_sem.at[0], inc=1, **across)
    n_full = n_blocks // 2
    for i in range(n_full):
        out_full(i)
        if i == 0:
            sum_next("dense", 0, 0)
    pl.semaphore_wait(free_sem.at[0], 1)
    for i in range(n_full, n_blocks):
        send_theirs(0, i)
    theirs_came(2)
    fc2_grad(1, 2)
    fc2_rest(0)
    spread_first("fc2", 0)
    fc2_next(1, 0, 2)
    theirs_came(3)
    fc2_grad(1, 3)
    lax.fori_loop(0, n_blocks, grad_rows, 0)
    dense_grad(1)
    fc2_next(1, 0, 3)
    fc1_grad(1)
    sum_rest("dense", 0)
    spread_first("dense", 0)
    sum_next("dense", 1, 0)
    drain(c_way, r, 0)
    for s in range(n_col):
        cot_over(s).wait_send()
    pl.semaphore_signal(free_sem.at[1], inc=1, **across)
    sum_next("fc1", 1, 0)
    fc1_grad(0)
    fc2_rest(1)
    scatter(0, n_full)
    sum_next("fc1", 0, 0)
    sum_rest("dense", 1)
    dk_s[...] = jnp.zeros_like(dk_s)
    dv_s[...] = jnp.zeros_like(dv_s)
    pl.semaphore_wait(free_sem.at[1], 1)
    for i in reversed(range(n_blocks)):
        backward_block(i)
        finish_mixed(i)
        send_theirs(1, i)
        if i == n_blocks - 1:
            for m in range(n_full + 1, n_blocks):
                scatter(0, m)
            spread_first("fc2", 1)
        if i == n_blocks // 2:
            for p in (1, 0):
                sum_rest("fc1", p)
            spread_first("fc1", 0)
    for p in (1, 0):
        qkv_grad(p)
    loads = [
        pltpu.make_async_copy(ref, stagez.at[m], stage_sem.at[2 + m])
        for m, ref in enumerate((cot_p, x_p))
    ]
    for load in loads:
        load.start()
    small_v[...] = jnp.zeros_like(small_v)
    scatter(1, n_blocks - 1)
    sum_next("qkv", 1, 0)
    scatter(1, n_blocks - 2)
    sum_next("qkv", 0, 0)
    spread_first("dense", 1)
    for load in loads:
        load.wait()
    lax.fori_loop(0, n_blocks, column_sums, 0)
    spread_first("fc1", 1)
    sum_rest("qkv", 1)
    for i in range(n_full):
        collect_full(i)
    for i in reversed(range(1, n_blocks - 2)):
        scatter(1, i)
    sum_rest("qkv", 0)
    spread_first("qkv", 0)
    for name, p in (("fc2", 0), ("dense", 0), ("fc2", 1)):
        spread_rest(name, p)
    for i in range(n_full, n_blocks):
        collect_half(0, i)
    scatter(1, 0)
    spread_rest("fc1", 0)
    spread_rest("dense", 1)
    collect_norm(n_blocks - 1)
    spread_first("qkv", 1)
    for i in reversed(range(1, n_blocks - 1)):
        collect_norm(i)
    spread_rest("fc1", 1)
    collect_norm(0)
    swap = remote(tot.at[0], tot.at[1], tot_send_p.at[0], tot_recv_p.at[0], across)
    swap.start()
    small_copy(0).start()
    swap.wait()
    tot[0] = tot[0] + tot[1]
    tot_copies = [
        remote(
            tot.at[0],
            tot.at[1 + s],
            tot_send_p.at[s],
            tot_recv_p.at[s],
            to(d, r, lax.rem(c + s, n_col)),
        )
        for s in range(1, n_col)
    ]
    for copy in tot_copies:
        copy.start()
    spread_rest("qkv", 0)
    for b in range(n_bits):
        small_copy(b).wait()
        small_v[...] = small_v[...] + small_r[b]
        if b + 1 < n_bits:
            small_copy(b + 1).start()
    small_p[...] = small_v[...]
    for i in range(n_full):
        swap_out(i).wait_recv()
    for i in range(n_blocks):
        rows = slice(i * BLOCK, (i + 1) * BLOCK)
        v = stagez[1, rows, :].astype(F32) + in_grad_p[rows, :] + out_bias_p[...]
        if i < n_full:
            v = v + xl_p[rows, :].astype(F32)
        y_out_p[rows, :] = v.astype(BF)
    spread_rest("qkv", 1)
    for copy in tot_copies:
        copy.wait()
    tot[1] = tot[0]
    for s in range(1, n_col):
        tot[1] = tot[1] + tot[1 + s]

    def in_final(i, _):
        rows = at(i * BLOCK, BLOCK)
        mu, inv = mean_p[rows, :], rstd_p[rows, :]
        sums = jnp.transpose(
            jnp.concatenate([tot[1, :, rows], jnp.zeros((120, BLOCK), F32)], axis=0)
        ) * (1.0 / full)
        one, two = sums[:, 0:1], sums[:, 1:2]
        for t in range(width // 128):
            lanes = slice(t * 128, (t + 1) * 128)
            hat = (stagez[1, rows, lanes].astype(F32) - mu) * inv
            sg = dv_s[t, rows, :] * gain_own_p[:, lanes]
            in_grad_p[rows, lanes] = stagez[0, rows, lanes].astype(F32) + inv * (
                sg - one - hat * two
            )
        return 0

    lax.fori_loop(0, n_blocks, in_final, 0)
    for name in tensors:
        for p in range(2):
            spread_next(name, p, 0)
    for name in tensors:
        finish(name)
    for i in range(6):
        weight_across(i).wait_send()
        weight_up(i).wait_send()
        for h in range(2):
            weight_share(i, h).wait_send()
    for i in range(n_full):
        swap_out(i).wait_send()
        for s in range(1, n_col):
            for h in range(2):
                full_on(i, s, h).wait_send()
    for n in range(2):
        for i in range(n_full if n == 0 else 0, n_blocks):
            for s in range(1, n_col):
                part_on(n, i, s).wait_send()


def widen_kernel(widths, *refs):
    n_wide = 6
    for src, dst in zip(refs[:n_wide], refs[n_wide + 1 : 2 * n_wide + 1]):
        dst[...] = src[...].astype(dst.dtype)
    small = refs[n_wide]
    qkv_ref, fc1_ref, bias_a, bias_b, gain_ref, shift_ref = refs[2 * n_wide + 1 :]
    qw, hid, width = widths

    @pl.when(pl.program_id(0) == 0)
    def _():
        for s in range(3):
            qkv_ref[s, 0, 0:1, :] = small[0:1, s * qw : (s + 1) * qw]
        at = 3 * qw
        fc1_ref[0, 0:1, :] = small[0:1, at : at + hid]
        at = at + hid
        for i, dsts in enumerate(((bias_a, bias_b), (gain_ref,), (shift_ref,))):
            for dst in dsts:
                dst[...] = small[0, at + i * width : at + (i + 1) * width]


def widen(arrays, small, widths):
    steps = 4
    qw, hid, width = widths

    def spec(shape):
        block = shape[:-2] + (shape[-2] // steps, shape[-1])
        lead = len(shape) - 2
        return pl.BlockSpec(block, lambda i: (0,) * lead + (i, 0))

    def whole(shape):
        return pl.BlockSpec(shape, lambda i: (0,) * len(shape))

    wide = [jax.ShapeDtypeStruct(a.shape, t) for a, t in arrays]
    shapes = [(3, 1, 1, qw), (1, 1, hid)] + [(width,)] * 4
    specs = [spec(a.shape) for a, _ in arrays]
    return pl.pallas_call(
        functools.partial(widen_kernel, widths),
        grid=(steps,),
        out_shape=wide + [jax.ShapeDtypeStruct(z, F32) for z in shapes],
        in_specs=specs + [whole(small.shape)],
        out_specs=specs + [whole(z) for z in shapes],
        compiler_params=pltpu.CompilerParams(vmem_limit_bytes=64 * 2**20),
        cost_estimate=pl.CostEstimate(
            flops=0, bytes_accessed=40 * 2**20, transcendentals=0
        ),
    )(*[a for a, _ in arrays], small)


def local(
    block_input,
    segment_ids,
    positions,
    ln_gain,
    ln_bias,
    qkv_weight,
    qkv_bias,
    dense_weight,
    dense_bias,
    fc1_weight,
    fc1_bias,
    fc2_weight,
    fc2_bias,
    cotangent,
):
    n_col = lax.axis_size("col")
    n_dp = lax.axis_size("dp")
    n_bits = n_dp.bit_length() - 1
    tokens, width = block_input.shape
    full = width * n_col * 2
    half = full // 2
    qw = qkv_weight.shape[2] // 2
    hid = fc1_weight.shape[1] // 2
    pairs = qw // 128
    small_w = 3 * qw + hid + 3 * width
    row = lax.broadcasted_iota(jnp.int32, (8, width), 0)
    vec = jnp.where(
        row == 0,
        ln_gain.astype(F32)[None],
        jnp.where(row == 1, ln_bias.astype(F32)[None], (dense_bias + fc2_bias)[None]),
    )
    lane = np.arange(128) % HEAD_DIM
    steps = (lane % (ROT_DIM // 2)).astype(np.float32)
    freq = np.exp(steps * np.float32(-2.0 * math.log(10000.0) / ROT_DIM), dtype=np.float32)
    freq = jnp.asarray(np.where(lane < ROT_DIM, freq, np.float32(0.0))[None])
    hbm = pl.BlockSpec(memory_space=pl.ANY)
    vmem = pl.BlockSpec(memory_space=pltpu.VMEM)
    dma = pltpu.SemaphoreType.DMA
    bits = max(n_bits, 1)
    sds = jax.ShapeDtypeStruct
    outs = (
        (vmem, sds((tokens, width), BF)),
        (vmem, sds((tokens, width), F32)),
        (vmem, sds((8, small_w), F32)),
        (hbm, sds((half, 2 * hid), BF)),
        (hbm, sds((2, hid, half), BF)),
        (hbm, sds((2, qw, half), BF)),
        (hbm, sds((3, half, 2 * qw), BF)),
        (hbm, sds((2, half, hid), BF)),
        (hbm, sds((2, qw, half), BF)),
        (hbm, sds((2, 3, half, qw), BF)),
        (hbm, sds((n_col - 1, tokens, width), BF)),
        (hbm, sds((n_col - 1, tokens, width), BF)),
        (hbm, sds((n_col - 1, 2, tokens, width), BF)),
    )
    v = pltpu.VMEM
    scratch = [
        v((tokens, full), BF),
        v((tokens, full), BF),
        v((16, full), F32),
        v((full, 3 * qw), BF),
        v((full, hid), BF),
        v((hid, full), BF),
        v((qw, full), BF),
        v((tokens, full), BF),
        v((tokens, hid), BF),
        v((tokens, hid), BF),
        v((pairs, tokens, 128), BF),
        v((pairs, tokens, 128), BF),
        v((pairs, tokens, 128), BF),
        v((pairs, tokens, 128), F32),
        v((pairs, tokens, 128), F32),
        v((BLOCK, tokens), F32),
        v((tokens, 128), F32),
        v((tokens, 128), F32),
        v((tokens, qw), BF),
        v((tokens, qw), BF),
        v((tokens, 3 * qw), BF),
        v((tokens, 128), F32),
        v((2, half, hid), BF),
        v((2, hid, half), BF),
        v((2, qw, half), BF),
        v((2, 3, half, qw), BF),
        v((half // 2, hid), BF),
        v((qw // 2, half), BF),
        v((3, half // 2, qw), BF),
        v((2, tokens, width), BF),
        v((n_col - 1, 2, BLOCK, width), BF),
        v((tokens, width), BF),
        v((16, width), F32),
        v((tokens, 128), F32),
        v((2, hid - (hid >> bits), half), BF),
        v((tokens, 1), F32),
        v((tokens, 1), F32),
        v((n_col + 1, 8, tokens), F32),
        v((8, small_w), F32),
        v((bits, 8, small_w), F32),
        dma((2, 3, n_col)),
        dma((2, n_col)),
        dma((1, 2, n_col)),
        dma((1, n_col)),
        dma((n_col,)),
        dma((n_col,)),
        dma((2, 3, n_col)),
        dma((2, n_col)),
        dma((1, 2, n_col)),
        dma((1, n_col)),
        dma((n_col,)),
        dma((n_col,)),
        dma((6,)),
        dma((6,)),
        dma((6,)),
        dma((6,)),
        dma((6, 2)),
        dma((6, 2)),
        dma((9,)),
        dma((4, 2, bits, n_col)),
        dma((4, 2, bits, n_col)),
        dma((4,)),
        dma((4,)),
        dma((4, 2, bits)),
        dma((4, 2, bits)),
        dma((4,)),
        dma((4,)),
        dma((2, tokens // BLOCK)),
        dma((2, tokens // BLOCK)),
        dma((2, tokens // BLOCK, n_col - 1)),
        dma((2, tokens // BLOCK, n_col - 1)),
        dma((tokens // BLOCK, n_col - 1, 2)),
        dma((tokens // BLOCK, n_col - 1, 2)),
        dma((tokens // BLOCK,)),
        dma((tokens // BLOCK,)),
        dma((n_col,)),
        dma((n_col,)),
        dma((bits,)),
        dma((bits,)),
        pltpu.SemaphoreType.REGULAR((2,)),
    ]
    res = pl.pallas_call(
        functools.partial(kernel, n_dp, n_col),
        out_shape=tuple(o[1] for o in outs),
        in_specs=[hbm] * 6 + [vmem] * 5,
        out_specs=tuple(o[0] for o in outs),
        scratch_shapes=scratch,
        compiler_params=pltpu.CompilerParams(
            collective_id=0,
            has_side_effects=True,
            vmem_limit_bytes=64 * 2**20,
            fuse_transposed_lhs_in_matmul=True,
        ),
        cost_estimate=pl.CostEstimate(
            flops=45 * 10**9, bytes_accessed=64 * 2**20, transcendentals=8 * 2**20
        ),
    )(
        block_input,
        cotangent,
        jnp.transpose(qkv_weight, (1, 0, 2)),
        fc1_weight,
        fc2_weight,
        dense_weight,
        vec,
        qkv_bias,
        fc1_bias,
        jnp.where(
            lax.broadcasted_iota(jnp.int32, (2, tokens), 0) == 0, segment_ids[None], positions[None]
        ).astype(F32),
        freq,
    )
    y_out, in_grad, small, f1, f2, fd, fq = res[:7]
    res = widen(
        ((f1, F32), (f2, F32), (fd, F32), (fq, F32), (y_out, BF), (in_grad, F32)), small, (qw, hid, width)
    )
    f1, f2, fd, fq, y_out, in_grad, qkv_b, fc1_b, bias_a, bias_b, gain_grad, shift_grad = res
    return (
        y_out,
        in_grad,
        gain_grad,
        shift_grad,
        jnp.transpose(fq, (1, 0, 2)),
        qkv_b,
        fd.reshape(dense_weight.shape),
        bias_a,
        f1,
        fc1_b,
        f2.reshape(fc2_weight.shape),
        bias_b,
    )


def solution(mesh):
    return jax.shard_map(
        local,
        mesh=mesh,
        in_specs=(
            P("dp", ("row", "col")),
            P("dp"),
            P("dp"),
            P(("row", "col")),
            P(("row", "col")),
            P("row", None, "col"),
            P(None, "col", "row", None),
            P("col", "row"),
            P(("row", "col")),
            P("row", "col"),
            P("col", "row", None),
            P("col", "row"),
            P(("row", "col")),
            P("dp", ("row", "col")),
        ),
        out_specs=(
            P("dp", ("row", "col")),
            P("dp", ("row", "col")),
            P(("row", "col")),
            P(("row", "col")),
            P("row", None, "col"),
            P(None, "col", "row", None),
            P("col", "row"),
            P(("row", "col")),
            P("row", "col"),
            P("col", "row", None),
            P("col", "row"),
            P(("row", "col")),
        ),
        check_vma=False,
    )
```

```python
import functools
import math

import jax
import jax.numpy as jnp
import numpy as np
from jax import lax
from jax.experimental import pallas as pl
from jax.experimental.pallas import tpu as pltpu
from jax.sharding import PartitionSpec as P

HEAD_DIM = 64
ROT_DIM = 32
NORM_EPSILON = 1e-05
MASKED_SCORE = -1e30
BLOCK = 256
MESH = pl.DeviceIdType.MESH
BF = jnp.bfloat16
F32 = jnp.float32
GELU_A = math.sqrt(2.0 / math.pi)
GELU_B = 0.044715
NN = (((1,), (0,)), ((), ()))
NT = (((1,), (1,)), ((), ()))
TN = (((0,), (0,)), ((), ()))


def dot(a, b, dims):
    return lax.dot_general(a, b, dims, preferred_element_type=F32)


def kernel(
    n_dp,
    n_col,
    x_p,
    cot_p,
    wq_p,
    w1_p,
    w2_p,
    wd_p,
    gain_1d_p,
    shift_1d_p,
    dense_1d_p,
    fc2_1d_p,
    qkv_bias_p,
    fc1_bias_p,
    seg_1d_p,
    pos_1d_p,
    freq_p,
    y_out_p,
    in_grad_p,
    small_p,
    f1_p,
    f2_p,
    fd_p,
    fq_p,
    rb1_p,
    rbd_p,
    rbq_p,
    rzo_p,
    rzn_p,
    rza_p,
    xf_p,
    cf_p,
    gf_p,
    wqf_p,
    w1f_p,
    w2f_p,
    wdf_p,
    normed_p,
    hidden_p,
    pg_p,
    q_p,
    k_p,
    v_p,
    dk_p,
    dv_p,
    bias_p,
    cos_p,
    sin_p,
    ctx_p,
    dctx_p,
    mg_p,
    lse_p,
    g1_p,
    g2_p,
    gd_p,
    gq_p,
    stage1_p,
    staged_p,
    stageq_p,
    stagez_p,
    stageo_p,
    xl_p,
    gb_p,
    vec_p,
    token_p,
    places_p,
    rb2_p,
    mean_p,
    rstd_p,
    tot_p,
    small_v_p,
    small_r_p,
    x_send_p,
    x_recv_p,
    v_send_p,
    v_recv_p,
    vx_send_p,
    vx_recv_p,
    g_send_p,
    g_recv_p,
    c_send_p,
    c_recv_p,
    cx_send_p,
    cx_recv_p,
    w_send_p,
    w_recv_p,
    y_send_p,
    y_recv_p,
    s_send_p,
    s_recv_p,
    load_sem_p,
    rs_send_p,
    rs_recv_p,
    xs_send_p,
    xs_recv_p,
    ag_send_p,
    ag_recv_p,
    part_sem_p,
    stage_sem_p,
    ox_send_p,
    ox_recv_p,
    oz_send_p,
    oz_recv_p,
    za_send_p,
    za_recv_p,
    xo_send_p,
    xo_recv_p,
    tot_send_p,
    tot_recv_p,
    sm_send_p,
    sm_recv_p,
    free_sem_p,
):
    xf, cf, gf = xf_p, cf_p, gf_p
    wqf, w1f, w2f, wdf = wqf_p, w1f_p, w2f_p, wdf_p
    normed, hidden, pg = normed_p, hidden_p, pg_p
    q_s, k_s, v_s, dk_s, dv_s = q_p, k_p, v_p, dk_p, dv_p
    ctx, dctx, mg, lse = ctx_p, dctx_p, mg_p, lse_p
    cos_ref, sin_ref, bias_s = cos_p, sin_p, bias_p
    load_sem, stage_sem = load_sem_p, stage_sem_p

    d = lax.axis_index("dp")
    r = lax.axis_index("row")
    c = lax.axis_index("col")
    n_bits = n_dp.bit_length() - 1
    core = lax.rem(d, 2)
    sibling = d + 1 - 2 * core
    other = 1 - r
    has_right = c < n_col - 1
    has_left = c > 0
    right = jnp.minimum(c + 1, n_col - 1)
    left = jnp.maximum(c - 1, 0)
    tokens, width = x_p.shape
    full = width * n_col * 2
    half = full // 2
    heads_w = qw = ctx.shape[1]
    pairs = heads_w // 128
    n_blocks = tokens // BLOCK
    scale = HEAD_DIM**-0.5

    def to(dd, rr, cc):
        return dict(device_id=(dd, rr, cc), device_id_type=MESH)

    def bit(b):
        return lax.rem(lax.div(d, 1 << b), 2)

    def peer(b):
        return d + (1 - 2 * bit(b)) * (1 << b)

    def remote(src, dst, send, recv, dev):
        return pltpu.make_async_remote_copy(
            src_ref=src, dst_ref=dst, send_sem=send, recv_sem=recv, **dev
        )

    def at(start, size):
        return pl.ds(pl.multiple_of(start, math.gcd(size, 256)), size)

    across = to(d, other, c)

    barrier = pltpu.get_barrier_semaphore()
    pl.semaphore_signal(barrier, inc=1, **across)
    for s in range(1, n_col):
        pl.semaphore_signal(barrier, inc=1, **to(d, r, lax.rem(c + s, n_col)))
    for b in range(n_bits):
        pl.semaphore_signal(barrier, inc=1, **to(peer(b), r, c))

    own_gain = gain_1d_p[...].astype(F32).reshape(1, width)
    vec_p[0:1, :] = own_gain
    vec_p[1:2, :] = dense_1d_p[...].reshape(1, width) + fc2_1d_p[...].reshape(1, width)
    gain_own_p = vec_p.at[0:1, :]
    out_bias_p = vec_p.at[1:2, :]
    gb_p[0:8, :] = jnp.broadcast_to(own_gain, (8, width))
    gb_p[8:16, :] = jnp.broadcast_to(shift_1d_p[...].astype(F32).reshape(1, width), (8, width))
    token_p[0:1, :] = seg_1d_p[...].astype(F32).reshape(1, tokens)
    token_p[1:2, :] = pos_1d_p[...].astype(F32).reshape(1, tokens)

    top = slice(0, tokens // 2)
    low = slice(tokens // 2, tokens)

    def block(ref, rr, j, rows=slice(None)):
        return ref.at[rows, at((rr * n_col + j) * width, width)]

    def hop(way, own, rr, j, lane, step):
        whole, mine_ref, send, recv, rows = way
        dst = block(whole, rr, j, rows)
        return remote(
            mine_ref if own else dst,
            dst,
            send.at[lane, step, j],
            recv.at[lane, j],
            to(d, r, right if step == 0 else left),
        )

    def over(way, own, j, send, recv):
        dst = block(way[0], r, j, way[4])
        return remote(way[1] if own else dst, dst, send, recv, across)

    def landed(dst, recv):
        return remote(dst, dst, recv, recv, across)

    def start_hop(cond, way, own, rr, j, lane, step):
        @pl.when(cond)
        def _():
            hop(way, own, rr, j, lane, step).start()

    def start_both(way, own, rr, lane):
        start_hop(has_right, way, own, rr, c, lane, 0)
        start_hop(has_left, way, own, rr, c, lane, 1)

    def advance(way, rr, lane, s, then=None):
        whole, _, _, recv, rows = way

        @pl.when(c >= s)
        def _():
            j = c - s
            landed(block(whole, rr, j, rows), recv.at[lane, j]).wait_recv()
            start_hop(has_right, way, False, rr, j, lane, 0)
            if then is not None:
                then(j)

        @pl.when(c + s < n_col)
        def _():
            j = c + s
            landed(block(whole, rr, j, rows), recv.at[lane, j]).wait_recv()
            start_hop(has_left, way, False, rr, j, lane, 1)
            if then is not None:
                then(j)

    def drain(way, rr, lane):
        for s in range(n_col):

            @pl.when((c >= s) & has_right)
            def _():
                hop(way, False, rr, jnp.maximum(c - s, 0), lane, 0).wait_send()

            @pl.when((c + s < n_col) & has_left)
            def _():
                j = jnp.minimum(c + s, n_col - 1)
                hop(way, False, rr, j, lane, 1).wait_send()

    def piece(i, k, rr):
        if i < 3:
            depth = wq_p.shape[1] // 4
            return (
                wq_p.at[i, at(k * depth, depth), at((1 - rr) * qw, qw)],
                wqf.at[at((rr * 4 + k) * depth, depth), i * qw : (i + 1) * qw],
            )
        if i == 3:
            depth, part = w1_p.shape[0] // 4, w1_p.shape[1] // 2
            return (
                w1_p.at[at(k * depth, depth), at((1 - rr) * part, part)],
                w1f.at[at((rr * 4 + k) * depth, depth), :],
            )
        src, dst = (w2_p, w2f) if i == 4 else (wd_p, wdf)
        depth, part = src.shape[0] // 8, src.shape[1]
        return (
            src.at[at(((1 - rr) * 4 + k) * depth, depth), :],
            dst.at[at(k * depth, depth), at(rr * part, part)],
        )

    w_send, w_recv, y_send, y_recv = w_send_p, w_recv_p, y_send_p, y_recv_p
    s_send, s_recv = s_send_p, s_recv_p
    upper = bit(1)
    quarter = (core + 2 * upper, core + 2 * (1 - upper))
    quarter_sib = (1 - core + 2 * upper, 1 - core + 2 * (1 - upper))

    def weight_across(i):
        src, dst = piece(i, quarter[0], r)
        return remote(src, dst, w_send.at[i], w_recv.at[i], across)

    def weight_up(i):
        dst = piece(i, quarter[0], other)[1]
        return remote(dst, dst, y_send.at[i], y_recv.at[i], to(peer(1), r, c))

    def weight_share(i, h):
        dst = piece(i, quarter[h], other)[1]
        return remote(dst, dst, s_send.at[i, h], s_recv.at[i, h], to(sibling, r, c))

    def weights_first(group):
        for i in group:
            landed(piece(i, quarter[0], other)[1], w_recv.at[i]).wait_recv()
            weight_up(i).start()
            weight_share(i, 0).start()

    def weights_second(group):
        for i in group:
            landed(piece(i, quarter[1], other)[1], y_recv.at[i]).wait_recv()
            weight_share(i, 1).start()

    def weights_wait(group):
        for i in group:
            for h in range(2):
                landed(piece(i, quarter_sib[h], other)[1], s_recv.at[i, h]).wait_recv()

    x_way = (xf, x_p.at[top, :], x_send_p, x_recv_p, top)
    x_low = (xf, x_p.at[low, :], v_send_p, v_recv_p, low)
    g_way = (gf, gb_p, g_send_p, g_recv_p, slice(None))
    c_way = (cf, cot_p, c_send_p, c_recv_p, slice(None))
    cx_send, cx_recv, vx_send, vx_recv = cx_send_p, cx_recv_p, vx_send_p, vx_recv_p
    g_over = over(g_way, True, c, g_send_p.at[1, 2, c], g_recv_p.at[1, c])
    x_over = over(x_way, True, c, x_send_p.at[1, 2, c], x_recv_p.at[1, c])

    def low_over(j, own=False):
        return over(x_low, own, j, vx_send.at[j], vx_recv.at[j])

    def cot_over(j, own=False):
        return over(c_way, own, j, cx_send.at[j], cx_recv.at[j])

    own = [(x_p, block(xf, r, c)), (gb_p, block(gf, r, c)), (cot_p, block(cf, r, c))]
    depth = wq_p.shape[1]
    for s in range(3):
        own.append((wq_p.at[s, :, at(r * qw, qw)], wqf.at[at(r * depth, depth), s * qw : (s + 1) * qw]))
    depth, part = w1_p.shape[0], w1_p.shape[1] // 2
    own.append((w1_p.at[:, at(r * part, part)], w1f.at[at(r * depth, depth), :]))
    for src, dst in ((w2_p, w2f), (wd_p, wdf)):
        depth, part = src.shape[0] // 2, src.shape[1]
        own.append((src.at[at(r * depth, depth), :], dst.at[:, at(r * part, part)]))
    own = [pltpu.make_async_copy(a, b, load_sem.at[i]) for i, (a, b) in enumerate(own)]
    for copy in own:
        copy.start()

    pl.semaphore_wait(barrier, 1 + (n_col - 1) + n_bits)
    g_over.start()
    x_over.start()
    low_over(c, True).start()
    for way in (g_way, x_way, x_low):
        start_both(way, True, r, 0)

    def tables(i, _):
        rows = at(i * BLOCK, BLOCK)
        wide = jnp.concatenate([token_p[:, rows], jnp.zeros((126, BLOCK), F32)], axis=0)
        places_p[rows, :] = jnp.transpose(wide)
        angle = places_p[rows, 1:2] * freq_p[...]
        cos_ref[rows, :] = jnp.cos(angle)
        sin_ref[rows, :] = jnp.sin(angle)
        return 0

    for i in (3, 0, 1, 2):
        weight_across(i).start()
    for way in (g_way, x_way):
        landed(block(way[0], other, c, way[4]), way[3].at[1, c]).wait_recv()
        start_both(way, False, other, 1)

    def start_cot(s):
        start_hop(has_right & (c == s), c_way, True, r, c, 0, 0)
        start_hop(has_left & (c == n_col - 1 - s), c_way, True, r, c, 0, 1)

    start_cot(0)
    lax.fori_loop(0, n_blocks, tables, 0)
    for s in range(1, n_col):
        advance(g_way, r, 0, s)
        advance(x_way, r, 0, s)
        advance(x_low, r, 0, s, then=lambda j: low_over(j).start())
        advance(g_way, other, 1, s)
        advance(x_way, other, 1, s)
        start_cot(s)
        if s == 1:
            cot_over(c, True).start()
        if s == 2:
            weights_first((3,))
        if s == 3:
            for i in range(4, 6):
                weight_across(i).start()
            weights_first(range(3))
            weights_second((3,))

    def advance_cot(s):
        advance(c_way, r, 0, s, then=lambda j: cot_over(j).start())

    for copy in own:
        copy.wait()
    for s in range(n_col):
        landed(block(xf, other, s, low), vx_recv.at[s]).wait_recv()

    gain = gf[0:1, :]
    shift = gf[8:9, :]

    def norm_rows(i, _):
        rows = at(i * 64, 64)
        v = xf[rows, :].astype(F32)
        mu = jnp.sum(v, axis=1, keepdims=True) * (1.0 / full)
        v = v - mu
        inv = lax.rsqrt(jnp.sum(v * v, axis=1, keepdims=True) * (1.0 / full) + NORM_EPSILON)
        mean_p[rows, :] = mu
        rstd_p[rows, :] = inv
        normed[rows, :] = (v * inv * gain + shift).astype(BF)
        return 0


    lane_at = lax.broadcasted_iota(jnp.int32, (1, 128), 1)
    first = lane_at % HEAD_DIM < ROT_DIM // 2
    low_head = lane_at < HEAD_DIM

    def turn(v, cos, sin, sign):
        up = pltpu.roll(v, 128 - ROT_DIM // 2, 1)
        down = pltpu.roll(v, ROT_DIM // 2, 1)
        swapped = jnp.where(first, -up, down) * sin
        return v * cos + swapped if sign > 0 else v * cos - swapped

    def qkv_rows(i, _):
        rows = at(i * BLOCK, BLOCK)
        mixed = dot(normed[rows, :], wqf[...], NN)
        cos, sin = cos_ref[rows, :], sin_ref[rows, :]
        for s, dst in enumerate((q_s, k_s, v_s)):
            for t in range(pairs):
                lanes = slice(s * qw + t * 128, s * qw + (t + 1) * 128)
                v = mixed[:, lanes] + qkv_bias_p[s, 0, 0:1, t * 128 : (t + 1) * 128]
                dst[t, rows, :] = (turn(v, cos, sin, 1) if s < 2 else v).astype(BF)
        return 0


    def fc1_rows(i, _):
        rows = at(i * BLOCK, BLOCK)
        for h in range(2):
            cols = slice(h * 512, (h + 1) * 512)
            v = dot(normed[rows, :], w1f[:, cols], NN) + fc1_bias_p[0, 0:1, cols]
            th = jnp.tanh(GELU_A * (v + GELU_B * v * v * v))
            hidden[rows, cols] = (0.5 * v * (1.0 + th)).astype(BF)
            slope = 0.5 * (1.0 + th) + 0.5 * v * (1.0 - th * th) * (
                GELU_A * (1.0 + 3.0 * GELU_B * v * v)
            )
            pg[rows, cols] = slope.astype(BF)
        return 0

    def set_bias(i):
        keys = (i + 1) * BLOCK
        rows = slice(i * BLOCK, keys)
        row_at = lax.broadcasted_iota(jnp.int32, (BLOCK, keys), 0) + i * BLOCK
        key_at = lax.broadcasted_iota(jnp.int32, (BLOCK, keys), 1)
        allowed = (places_p[rows, 0:1] == token_p[0:1, :keys]) & (row_at >= key_at)
        bias_s[:, :keys] = jnp.where(allowed, 0.0, MASKED_SCORE)

    def mine(h, v):
        return jnp.where(low_head if h == 0 else ~low_head, v, jnp.zeros_like(v))

    def forward_block(i):
        keys = (i + 1) * BLOCK
        rows = slice(i * BLOCK, keys)
        set_bias(i)

        def pair(t, _):
            q, k, v = q_s[t, rows, :], k_s[t, :keys, :], v_s[t, :keys, :]
            outs = []
            logs = lse[rows, :]
            for h in range(2):
                s = dot(mine(h, q), k, NT) * scale + bias_s[:, :keys]
                top = jnp.max(s, axis=1, keepdims=True)
                e = jnp.exp(s - top)
                total = jnp.sum(e, axis=1, keepdims=True)
                low = (e * (1.0 / total)).astype(BF)
                outs.append(dot(low, v, NN))
                logs = jnp.where(lane_at == 2 * t + h, top + jnp.log(total), logs)
            lse[rows, :] = logs
            ctx[rows, at(t * 128, 128)] = jnp.where(low_head, outs[0], outs[1]).astype(BF)
            return 0

        lax.fori_loop(0, pairs, pair, 0)

    rs_send, rs_recv, xs_send, xs_recv = rs_send_p, rs_recv_p, xs_send_p, xs_recv_p
    ag_send, ag_recv, part_sem = ag_send_p, ag_recv_p, part_sem_p
    g1, g2, gd, gq = g1_p, g2_p, gd_p, gq_p
    tensors = dict(
        fc1=(0, g1, rb1_p, stage1_p, half),
        fc2=(1, g2, rb2_p, None, hidden.shape[1]),
        dense=(2, gd, rbd_p, staged_p, heads_w),
        qkv=(3, gq, rbq_p, stageq_p, half),
    )
    results = dict(fc1=f1_p, fc2=f2_p, dense=fd_p, qkv=fq_p)
    mine_at, theirs_at = r * half, other * half
    starts = (mine_at, theirs_at)

    def slab(ref, p, rows):
        return ref.at[p, :, rows, :] if len(ref.shape) == 4 else ref.at[p, rows, :]

    def offset(rows, upto):
        off = 0
        for b in range(upto):
            off = off + bit(b) * (rows >> (b + 1))
        return off

    def landing(rows, b):
        return slice(rows - (rows >> b), rows - (rows >> (b + 1)))

    def nth(k):
        j = c
        for here in range(n_col):
            turn_k = sorted(range(n_col), key=lambda v: (abs(v - here), v))[k]
            j = jnp.where(c == here, turn_k, j)
        return j

    def sum_copy(name, p, b, k=0):
        n, g, rb, _, rows = tensors[name]
        size = rows >> (b + 1)
        src = slab(g, p, at(offset(rows, b) + (1 - bit(b)) * size, size))
        dst = slab(rb, p, landing(rows, b))
        if name == "fc2":
            cols = at(nth(k) * width, width)
            src, dst = src.at[:, cols], dst.at[:, cols]
        return remote(src, dst, rs_send.at[n, p, b, k], rs_recv.at[n, p, b, k], to(peer(b), r, c))

    def place(name, rr, off, size):
        if name == "fc1":
            return f1_p.at[at(off, size), at(rr * hidden.shape[1], hidden.shape[1])]
        if name == "qkv":
            return fq_p.at[:, at(off, size), at(rr * qw, qw)]
        return results[name].at[rr, at(off, size), :]

    def kept(name, p):
        _, g, _, _, rows = tensors[name]
        size = rows >> n_bits
        off = offset(rows, n_bits)
        return slab(g, p, at(off, size)), off, size

    def part_copy(name):
        src, off, size = kept(name, 0)
        return pltpu.make_async_copy(src, place(name, r, off, size), part_sem.at[tensors[name][0]])

    def swap_copy(name):
        src, off, size = kept(name, 1)
        n = tensors[name][0]
        return remote(src, place(name, r, off, size), xs_send.at[n], xs_recv.at[n], across)

    def fc2_next(p, b, k):
        _, g, rb, _, rows = tensors["fc2"]
        size = rows >> (b + 1)
        off = offset(rows, b + 1)
        cols = at(nth(k) * width, width)
        sum_copy("fc2", p, b, k).wait_recv()
        chunk = min(size, 128)

        def add(i, _):
            there = (p, at(off + i * chunk, chunk), cols)
            here = (p, at(rows - (rows >> b) + i * chunk, chunk), cols)
            g[there] = (g[there].astype(F32) + rb[here].astype(F32)).astype(BF)
            return 0

        lax.fori_loop(0, size // chunk, add, 0)
        if b + 1 < n_bits:
            sum_copy("fc2", p, b + 1, k).start()

    def sum_next(name, p, b):
        n, g, rb, stage, rows = tensors[name]
        size = rows >> (b + 1)
        off = offset(rows, b + 1)
        sum_copy(name, p, b).wait_recv()
        four = len(g.shape) == 4
        chunk = min(size, 128)
        dst = stage.at[:, :size, :] if four else stage.at[:size, :]
        copy = pltpu.make_async_copy(slab(rb, p, landing(rows, b)), dst, stage_sem.at[0])
        copy.start()
        copy.wait()

        def add(i, _):
            if four:
                there = (p, slice(None), at(off + i * chunk, chunk), slice(None))
                here = (slice(None), at(i * chunk, chunk), slice(None))
            else:
                there = (p, at(off + i * chunk, chunk), slice(None))
                here = (at(i * chunk, chunk), slice(None))
            g[there] = (g[there].astype(F32) + stage[here].astype(F32)).astype(BF)
            return 0

        lax.fori_loop(0, size // chunk, add, 0)
        if b + 1 < n_bits:
            sum_copy(name, p, b + 1).start()
        elif p == 0:
            part_copy(name).start()
        else:
            swap_copy(name).start()

    def fc2_rest(p):
        for b in range(1, n_bits):
            for k in range(n_col):
                fc2_next(p, b, k)
        if p == 0:
            part_copy("fc2").start()
        else:
            swap_copy("fc2").start()

    def sum_rest(name, p):
        for b in range(1, n_bits):
            sum_next(name, p, b)

    def spread_copy(name, p, b):
        n, rows = tensors[name][0], tensors[name][4]
        ref = place(name, r if p == 0 else other, offset(rows, b + 1), rows >> (b + 1))
        return remote(ref, ref, ag_send_p.at[n, p, b], ag_recv_p.at[n, p, b], to(peer(b), r, c))

    def spread_landed(name, p, b):
        n, rows = tensors[name][0], tensors[name][4]
        size = rows >> (b + 1)
        off = offset(rows, b) + (1 - bit(b)) * size
        return landed(place(name, r if p == 0 else other, off, size), ag_recv_p.at[n, p, b])

    def spread_first(name, p):
        if p == 0:
            part_copy(name).wait()
        else:
            _, off, size = kept(name, 1)
            landed(place(name, other, off, size), xs_recv_p.at[tensors[name][0]]).wait_recv()
        spread_copy(name, p, n_bits - 1).start()

    def spread_next(name, p, b):
        spread_landed(name, p, b).wait_recv()
        if b > 0:
            spread_copy(name, p, b - 1).start()

    def spread_rest(name, p):
        for b in reversed(range(1, n_bits)):
            spread_next(name, p, b)

    def finish(name):
        for b in range(n_bits):
            for p in range(2):
                for k in range(n_col if name == "fc2" else 1):
                    sum_copy(name, p, b, k).wait_send()
                spread_copy(name, p, b).wait_send()
        swap_copy(name).wait_send()

    def fc2_grad(p, k):
        col = nth(k) * width

        def body(i, _):
            cols = at(i * BLOCK, BLOCK)
            g2[p, cols, at(col, width)] = dot(
                hidden[:, cols], cf[:, at(starts[p] + col, width)], TN
            ).astype(BF)
            return 0

        lax.fori_loop(0, hidden.shape[1] // BLOCK, body, 0)
        sum_copy("fc2", p, 0, k).start()

    def fc1_grad(p):
        def body(i, _):
            g1[p, at(i * BLOCK, BLOCK), :] = dot(
                normed[:, at(starts[p] + i * BLOCK, BLOCK)], pg[...], TN
            ).astype(BF)
            return 0

        lax.fori_loop(0, half // BLOCK, body, 0)
        sum_copy("fc1", p, 0).start()

    def dense_grad(p):
        gd[p] = dot(ctx[...], cf[:, at(starts[p], half)], TN).astype(BF)
        sum_copy("dense", p, 0).start()

    def qkv_grad(p):
        def body(i, _):
            v = dot(normed[:, at(starts[p] + i * BLOCK, BLOCK)], mg[...], TN).astype(BF)
            for s in range(3):
                gq[p, s, at(i * BLOCK, BLOCK), :] = v[:, s * qw : (s + 1) * qw]
            return 0

        lax.fori_loop(0, half // BLOCK, body, 0)
        sum_copy("qkv", p, 0).start()

    ox_send, ox_recv, oz_send, oz_recv = ox_send_p, ox_recv_p, oz_send_p, oz_recv_p
    free_sem = free_sem_p
    outputs = ((xf, rzo_p), (cf, rzn_p))

    def out_part(n, rows, start):
        if n == 0:
            return dot(ctx[rows, :], wdf[:, at(start, half)], NN) + dot(
                hidden[rows, :], w2f[:, at(start, half)], NN
            )
        return dot(mg[rows, :], wqf[at(start, half), :], NT) + dot(
            pg[rows, :], w1f[at(start, half), :], NT
        )

    def part_over(n, i):
        buf = outputs[n][0]
        rows = slice(i * BLOCK, (i + 1) * BLOCK)
        return remote(
            buf.at[rows, :half], buf.at[rows, half:], ox_send.at[n, i], ox_recv.at[n, i], across
        )

    def send_theirs(n, i):
        rows = slice(i * BLOCK, (i + 1) * BLOCK)
        outputs[n][0][rows, :half] = out_part(n, rows, theirs_at).astype(BF)
        part_over(n, i).start()

    def part_on(n, i, s):
        buf, landing_z = outputs[n]
        rows = slice(i * BLOCK, (i + 1) * BLOCK)
        j = lax.rem(c + s, n_col)
        return remote(
            buf.at[rows, at(j * width, width)],
            landing_z.at[s - 1, rows, :],
            oz_send.at[n, i, s - 1],
            oz_recv.at[n, i, s - 1],
            to(d, r, j),
        )

    def scatter(n, i):
        buf = outputs[n][0]
        rows = slice(i * BLOCK, (i + 1) * BLOCK)
        part_over(n, i).wait()
        v = out_part(n, rows, mine_at) + buf[rows, half:].astype(F32)
        bias_s[:, :half] = v
        buf[rows, :half] = v.astype(BF)
        for t in range(width // 128):
            own_part = bias_s[:, at(c * width + t * 128, 128)]
            if n == 0:
                in_grad_p[rows, t * 128 : (t + 1) * 128] = own_part
            else:
                dv_s[t, rows, :] = own_part
        for s in range(1, n_col):
            part_on(n, i, s).start()

    stagez, stageo = stagez_p, stageo_p

    def full_on(i, s, h):
        rows = slice(i * BLOCK, (i + 1) * BLOCK)
        j = lax.rem(c + s, n_col)
        return remote(
            xf.at[rows, at(starts[h] + j * width, width)],
            rza_p.at[s - 1, h, rows, :],
            za_send_p.at[i, s - 1, h],
            za_recv_p.at[i, s - 1, h],
            to(d, r, j),
        )

    def out_full(i):
        rows = slice(i * BLOCK, (i + 1) * BLOCK)
        for start in starts:
            xf[rows, at(start, half)] = out_part(0, rows, start).astype(BF)
        for s in range(1, n_col):
            for h in range(2):
                full_on(i, s, h).start()

    def swap_out(i):
        rows = slice(i * BLOCK, (i + 1) * BLOCK)
        return remote(
            xf.at[rows, at(theirs_at + c * width, width)],
            xl_p.at[rows, :],
            xo_send_p.at[i],
            xo_recv_p.at[i],
            across,
        )

    def collect_full(i):
        rows = slice(i * BLOCK, (i + 1) * BLOCK)
        for s in range(1, n_col):
            for h in range(2):
                full_on(i, s, h).wait_recv()
        load = pltpu.make_async_copy(rza_p.at[:, :, rows, :], stageo, stage_sem.at[1])
        load.start()
        load.wait()
        for h, start in enumerate(starts):
            own = at(start + c * width, width)
            v = xf[rows, own].astype(F32)
            for s in range(n_col - 1):
                v = v + stageo[s, h].astype(F32)
            if h == 0:
                in_grad_p[rows, :] = v
            else:
                xf[rows, own] = v.astype(BF)
        swap_out(i).start()

    def collect_half(n, i):
        rows = slice(i * BLOCK, (i + 1) * BLOCK)
        for s in range(1, n_col):
            part_on(n, i, s).wait_recv()
        landing_z = outputs[n][1]
        load = pltpu.make_async_copy(landing_z.at[:, rows, :], stageo.at[:, 0], stage_sem.at[1])
        load.start()
        load.wait()
        for t in range(width // 128):
            lanes = slice(t * 128, (t + 1) * 128)
            v = stageo[0, 0, :, lanes].astype(F32)
            for s in range(1, n_col - 1):
                v = v + stageo[s, 0, :, lanes].astype(F32)
            if n == 0:
                in_grad_p[rows, lanes] += v
            else:
                dv_s[t, rows, :] += v

    def backward_block(i):
        keys = (i + 1) * BLOCK
        rows = slice(i * BLOCK, keys)
        set_bias(i)

        def pair(t, _):
            lanes = at(t * 128, 128)
            q, k, v = q_s[t, rows, :], k_s[t, :keys, :], v_s[t, :keys, :]
            grad = dctx[rows, lanes]
            query_grads = []
            for h in range(2):
                qh, gh = mine(h, q), mine(h, grad)
                log_total = jnp.sum(
                    jnp.where(lane_at == 2 * t + h, lse[rows, :], 0.0), axis=1, keepdims=True
                )
                p = jnp.exp(dot(qh, k, NT) * scale + bias_s[:, :keys] - log_total)
                dp = dot(gh, v, NT)
                dv_s[t, :keys, :] += dot(p.astype(BF), gh, TN)
                centre = jnp.sum(p * dp, axis=1, keepdims=True)
                ds = (p * (dp - centre) * scale).astype(BF)
                query_grads.append(dot(ds, k, NN))
                dk_s[t, :keys, :] += dot(ds, qh, TN)
            dq = jnp.where(low_head, query_grads[0], query_grads[1])
            mg[rows, lanes] = turn(dq, cos_ref[rows, :], sin_ref[rows, :], -1).astype(BF)
            return 0

        lax.fori_loop(0, pairs, pair, 0)

    def grad_rows(i, _):
        rows = at(i * BLOCK, BLOCK)
        dctx[rows, :] = dot(cf[rows, :], wdf[...], NT).astype(BF)
        for h in range(2):
            cols = slice(h * 512, (h + 1) * 512)
            v = dot(cf[rows, :], w2f[cols, :], NT)
            pg[rows, cols] = (v * pg[rows, cols].astype(F32)).astype(BF)
        return 0

    def theirs_came(k):
        j = nth(k)
        landed(block(cf, other, j), cx_recv.at[j]).wait_recv()

    def finish_mixed(i):
        rows = slice(i * BLOCK, (i + 1) * BLOCK)
        for t in range(pairs):
            lanes = slice(qw + t * 128, qw + (t + 1) * 128)
            mg[rows, lanes] = turn(dk_s[t, rows, :], cos_ref[rows, :], sin_ref[rows, :], -1).astype(BF)
            lanes = slice(2 * qw + t * 128, 2 * qw + (t + 1) * 128)
            mg[rows, lanes] = dv_s[t, rows, :].astype(BF)

    tot, small_v, small_r = tot_p, small_v_p, small_r_p
    n_mixed, n_pre = mg.shape[1], pg.shape[1]
    base = n_mixed + n_pre

    def column_sums(i, _):
        rows = at(i * BLOCK, BLOCK)
        for ref, lo, size in ((mg, 0, n_mixed), (pg, n_mixed, n_pre), (stagez.at[0], base, width)):
            small_v[0:1, lo : lo + size] += jnp.sum(ref[rows, :].astype(F32), axis=0, keepdims=True)
        return 0

    def collect_norm(i):
        collect_half(1, i)
        rows = slice(i * BLOCK, (i + 1) * BLOCK)
        mu, inv = mean_p[rows, :], rstd_p[rows, :]
        one = jnp.zeros((BLOCK, 1), F32)
        two = jnp.zeros((BLOCK, 1), F32)
        for t in range(width // 128):
            lanes = slice(t * 128, (t + 1) * 128)
            g = dv_s[t, rows, :]
            hat = (stagez[1, rows, lanes].astype(F32) - mu) * inv
            sg = g * gain_own_p[:, lanes]
            one = one + jnp.sum(sg, axis=1, keepdims=True)
            two = two + jnp.sum(sg * hat, axis=1, keepdims=True)
            lo = base + width + t * 128
            small_v[0:1, lo : lo + 128] += jnp.sum(g * hat, axis=0, keepdims=True)
            lo = base + 2 * width + t * 128
            small_v[0:1, lo : lo + 128] += jnp.sum(g, axis=0, keepdims=True)
        packed = jnp.where(lane_at == 0, one, jnp.where(lane_at == 1, two, 0.0))
        tot[0, :, rows] = jnp.transpose(packed)[0:8, :]

    def small_copy(b):
        return remote(small_v, small_r.at[b], sm_send_p.at[b], sm_recv_p.at[b], to(peer(b), r, c))

    lax.fori_loop(0, tokens // 64, norm_rows, 0)
    advance_cot(1)
    weights_second(range(3))
    weights_wait((3,))
    lax.fori_loop(0, n_blocks, fc1_rows, 0)
    fc2_grad(0, 0)
    theirs_came(0)
    fc2_grad(1, 0)
    fc2_grad(0, 1)
    weights_wait(range(3))
    lax.fori_loop(0, n_blocks, qkv_rows, 0)
    advance_cot(2)
    weights_first(range(4, 6))
    for p, k in ((0, 0), (1, 0), (0, 1)):
        fc2_next(p, 0, k)
    fc2_grad(0, 2)
    lse[...] = jnp.zeros_like(lse)
    for i in range(n_blocks):
        if i == n_blocks - 2:
            theirs_came(1)
            fc2_grad(1, 1)
            fc2_next(0, 0, 2)
            weights_second(range(4, 6))
        if i == n_blocks - 1:
            advance_cot(3)
            fc2_grad(0, 3)
            fc2_next(1, 0, 1)
        forward_block(i)
    dense_grad(0)
    fc2_next(0, 0, 3)
    weights_wait(range(4, 6))
    for way in (g_way, x_way):
        drain(way, r, 0)
        drain(way, other, 1)
    drain(x_low, r, 0)
    for s in range(n_col):
        low_over(s).wait_send()
    g_over.wait_send()
    x_over.wait_send()
    pl.semaphore_signal(free_sem.at[0], inc=1, **across)
    n_full = n_blocks // 2
    for i in range(n_full):
        out_full(i)
        if i == 0:
            sum_next("dense", 0, 0)
    pl.semaphore_wait(free_sem.at[0], 1)
    for i in range(n_full, n_blocks):
        send_theirs(0, i)
    theirs_came(2)
    fc2_grad(1, 2)
    fc2_rest(0)
    spread_first("fc2", 0)
    fc2_next(1, 0, 2)
    theirs_came(3)
    fc2_grad(1, 3)
    lax.fori_loop(0, n_blocks, grad_rows, 0)
    dense_grad(1)
    fc2_next(1, 0, 3)
    fc1_grad(1)
    sum_rest("dense", 0)
    spread_first("dense", 0)
    sum_next("dense", 1, 0)
    drain(c_way, r, 0)
    for s in range(n_col):
        cot_over(s).wait_send()
    pl.semaphore_signal(free_sem.at[1], inc=1, **across)
    sum_next("fc1", 1, 0)
    fc1_grad(0)
    fc2_rest(1)
    scatter(0, n_full)
    sum_next("fc1", 0, 0)
    sum_rest("dense", 1)
    dk_s[...] = jnp.zeros_like(dk_s)
    dv_s[...] = jnp.zeros_like(dv_s)
    pl.semaphore_wait(free_sem.at[1], 1)
    for i in reversed(range(n_blocks)):
        backward_block(i)
        finish_mixed(i)
        send_theirs(1, i)
        if i == n_blocks - 1:
            for m in range(n_full + 1, n_blocks):
                scatter(0, m)
            spread_first("fc2", 1)
        if i == n_blocks // 2:
            for p in (1, 0):
                sum_rest("fc1", p)
            spread_first("fc1", 0)
    for p in (1, 0):
        qkv_grad(p)
    loads = [
        pltpu.make_async_copy(ref, stagez.at[m], stage_sem.at[2 + m])
        for m, ref in enumerate((cot_p, x_p))
    ]
    for load in loads:
        load.start()
    small_v[...] = jnp.zeros_like(small_v)
    scatter(1, n_blocks - 1)
    sum_next("qkv", 1, 0)
    scatter(1, n_blocks - 2)
    sum_next("qkv", 0, 0)
    spread_first("dense", 1)
    for load in loads:
        load.wait()
    lax.fori_loop(0, n_blocks, column_sums, 0)
    spread_first("fc1", 1)
    sum_rest("qkv", 1)
    for i in range(n_full):
        collect_full(i)
    for i in reversed(range(1, n_blocks - 2)):
        scatter(1, i)
    sum_rest("qkv", 0)
    spread_first("qkv", 0)
    for name, p in (("fc2", 0), ("dense", 0), ("fc2", 1)):
        spread_rest(name, p)
    for i in range(n_full, n_blocks):
        collect_half(0, i)
    scatter(1, 0)
    spread_rest("fc1", 0)
    spread_rest("dense", 1)
    collect_norm(n_blocks - 1)
    spread_first("qkv", 1)
    for i in reversed(range(1, n_blocks - 1)):
        collect_norm(i)
    spread_rest("fc1", 1)
    collect_norm(0)
    swap = remote(tot.at[0], tot.at[1], tot_send_p.at[0], tot_recv_p.at[0], across)
    swap.start()
    small_copy(0).start()
    swap.wait()
    tot[0] = tot[0] + tot[1]
    tot_copies = [
        remote(
            tot.at[0],
            tot.at[1 + s],
            tot_send_p.at[s],
            tot_recv_p.at[s],
            to(d, r, lax.rem(c + s, n_col)),
        )
        for s in range(1, n_col)
    ]
    for copy in tot_copies:
        copy.start()
    spread_rest("qkv", 0)
    for b in range(n_bits):
        small_copy(b).wait()
        small_v[...] = small_v[...] + small_r[b]
        if b + 1 < n_bits:
            small_copy(b + 1).start()
    small_p[...] = small_v[...]
    for i in range(n_full):
        swap_out(i).wait_recv()
    for i in range(n_blocks):
        rows = slice(i * BLOCK, (i + 1) * BLOCK)
        v = stagez[1, rows, :].astype(F32) + in_grad_p[rows, :] + out_bias_p[...]
        if i < n_full:
            v = v + xl_p[rows, :].astype(F32)
        y_out_p[rows, :] = v.astype(BF)
    spread_rest("qkv", 1)
    for copy in tot_copies:
        copy.wait()
    tot[1] = tot[0]
    for s in range(1, n_col):
        tot[1] = tot[1] + tot[1 + s]

    def in_final(i, _):
        rows = at(i * BLOCK, BLOCK)
        mu, inv = mean_p[rows, :], rstd_p[rows, :]
        sums = jnp.transpose(
            jnp.concatenate([tot[1, :, rows], jnp.zeros((120, BLOCK), F32)], axis=0)
        ) * (1.0 / full)
        one, two = sums[:, 0:1], sums[:, 1:2]
        for t in range(width // 128):
            lanes = slice(t * 128, (t + 1) * 128)
            hat = (stagez[1, rows, lanes].astype(F32) - mu) * inv
            sg = dv_s[t, rows, :] * gain_own_p[:, lanes]
            in_grad_p[rows, lanes] = stagez[0, rows, lanes].astype(F32) + inv * (
                sg - one - hat * two
            )
        return 0

    lax.fori_loop(0, n_blocks, in_final, 0)
    for name in tensors:
        for p in range(2):
            spread_next(name, p, 0)
    for name in tensors:
        finish(name)
    for i in range(6):
        weight_across(i).wait_send()
        weight_up(i).wait_send()
        for h in range(2):
            weight_share(i, h).wait_send()
    for i in range(n_full):
        swap_out(i).wait_send()
        for s in range(1, n_col):
            for h in range(2):
                full_on(i, s, h).wait_send()
    for n in range(2):
        for i in range(n_full if n == 0 else 0, n_blocks):
            for s in range(1, n_col):
                part_on(n, i, s).wait_send()


def widen_kernel(widths, *refs):
    n_wide = 6
    for src, dst in zip(refs[:n_wide], refs[n_wide + 1 : 2 * n_wide + 1]):
        dst[...] = src[...].astype(dst.dtype)
    small = refs[n_wide]
    qkv_ref, fc1_ref, bias_a, bias_b, gain_ref, shift_ref = refs[2 * n_wide + 1 :]
    qw, hid, width = widths

    @pl.when(pl.program_id(0) == 0)
    def _():
        for s in range(3):
            qkv_ref[s, 0, 0:1, :] = small[0:1, s * qw : (s + 1) * qw]
        at = 3 * qw
        fc1_ref[0, 0:1, :] = small[0:1, at : at + hid]
        at = at + hid
        for i, dsts in enumerate(((bias_a, bias_b), (gain_ref,), (shift_ref,))):
            for dst in dsts:
                dst[...] = small[0, at + i * width : at + (i + 1) * width]


def widen(arrays, small, widths):
    steps = 2
    qw, hid, width = widths

    def spec(shape):
        block = shape[:-2] + (shape[-2] // steps, shape[-1])
        lead = len(shape) - 2
        return pl.BlockSpec(block, lambda i: (0,) * lead + (i, 0))

    def whole(shape):
        return pl.BlockSpec(shape, lambda i: (0,) * len(shape))

    wide = [jax.ShapeDtypeStruct(a.shape, t) for a, t in arrays]
    shapes = [(3, 1, 1, qw), (1, 1, hid)] + [(width,)] * 4
    specs = [spec(a.shape) for a, _ in arrays]
    return pl.pallas_call(
        functools.partial(widen_kernel, widths),
        grid=(steps,),
        out_shape=wide + [jax.ShapeDtypeStruct(z, F32) for z in shapes],
        in_specs=specs + [whole(small.shape)],
        out_specs=specs + [whole(z) for z in shapes],
        compiler_params=pltpu.CompilerParams(vmem_limit_bytes=64 * 2**20),
        cost_estimate=pl.CostEstimate(
            flops=0, bytes_accessed=40 * 2**20, transcendentals=0
        ),
    )(*[a for a, _ in arrays], small)


def local(
    block_input,
    segment_ids,
    positions,
    ln_gain,
    ln_bias,
    qkv_weight,
    qkv_bias,
    dense_weight,
    dense_bias,
    fc1_weight,
    fc1_bias,
    fc2_weight,
    fc2_bias,
    cotangent,
):
    n_col = lax.axis_size("col")
    n_dp = lax.axis_size("dp")
    n_bits = n_dp.bit_length() - 1
    tokens, width = block_input.shape
    full = width * n_col * 2
    half = full // 2
    qw = qkv_weight.shape[2] // 2
    hid = fc1_weight.shape[1] // 2
    pairs = qw // 128
    small_w = 3 * qw + hid + 3 * width
    lane = np.arange(128) % HEAD_DIM
    steps = (lane % (ROT_DIM // 2)).astype(np.float32)
    freq = np.exp(steps * np.float32(-2.0 * math.log(10000.0) / ROT_DIM), dtype=np.float32)
    freq = jnp.asarray(np.where(lane < ROT_DIM, freq, np.float32(0.0))[None])
    hbm = pl.BlockSpec(memory_space=pl.ANY)
    vmem = pl.BlockSpec(memory_space=pltpu.VMEM)
    dma = pltpu.SemaphoreType.DMA
    bits = max(n_bits, 1)
    sds = jax.ShapeDtypeStruct
    outs = (
        (vmem, sds((tokens, width), BF)),
        (vmem, sds((tokens, width), F32)),
        (vmem, sds((8, small_w), F32)),
        (hbm, sds((half, 2 * hid), BF)),
        (hbm, sds((2, hid, half), BF)),
        (hbm, sds((2, qw, half), BF)),
        (hbm, sds((3, half, 2 * qw), BF)),
        (hbm, sds((2, half, hid), BF)),
        (hbm, sds((2, qw, half), BF)),
        (hbm, sds((2, 3, half, qw), BF)),
        (hbm, sds((n_col - 1, tokens, width), BF)),
        (hbm, sds((n_col - 1, tokens, width), BF)),
        (hbm, sds((n_col - 1, 2, tokens, width), BF)),
    )
    v = pltpu.VMEM
    scratch = [
        v((tokens, full), BF),
        v((tokens, full), BF),
        v((16, full), F32),
        v((full, 3 * qw), BF),
        v((full, hid), BF),
        v((hid, full), BF),
        v((qw, full), BF),
        v((tokens, full), BF),
        v((tokens, hid), BF),
        v((tokens, hid), BF),
        v((pairs, tokens, 128), BF),
        v((pairs, tokens, 128), BF),
        v((pairs, tokens, 128), BF),
        v((pairs, tokens, 128), F32),
        v((pairs, tokens, 128), F32),
        v((BLOCK, tokens), F32),
        v((tokens, 128), F32),
        v((tokens, 128), F32),
        v((tokens, qw), BF),
        v((tokens, qw), BF),
        v((tokens, 3 * qw), BF),
        v((tokens, 128), F32),
        v((2, half, hid), BF),
        v((2, hid, half), BF),
        v((2, qw, half), BF),
        v((2, 3, half, qw), BF),
        v((half // 2, hid), BF),
        v((qw // 2, half), BF),
        v((3, half // 2, qw), BF),
        v((2, tokens, width), BF),
        v((n_col - 1, 2, BLOCK, width), BF),
        v((tokens, width), BF),
        v((16, width), F32),
        v((2, width), F32),
        v((2, tokens), F32),
        v((tokens, 128), F32),
        v((2, hid - (hid >> bits), half), BF),
        v((tokens, 1), F32),
        v((tokens, 1), F32),
        v((n_col + 1, 8, tokens), F32),
        v((8, small_w), F32),
        v((bits, 8, small_w), F32),
        dma((2, 3, n_col)),
        dma((2, n_col)),
        dma((1, 2, n_col)),
        dma((1, n_col)),
        dma((n_col,)),
        dma((n_col,)),
        dma((2, 3, n_col)),
        dma((2, n_col)),
        dma((1, 2, n_col)),
        dma((1, n_col)),
        dma((n_col,)),
        dma((n_col,)),
        dma((6,)),
        dma((6,)),
        dma((6,)),
        dma((6,)),
        dma((6, 2)),
        dma((6, 2)),
        dma((9,)),
        dma((4, 2, bits, n_col)),
        dma((4, 2, bits, n_col)),
        dma((4,)),
        dma((4,)),
        dma((4, 2, bits)),
        dma((4, 2, bits)),
        dma((4,)),
        dma((4,)),
        dma((2, tokens // BLOCK)),
        dma((2, tokens // BLOCK)),
        dma((2, tokens // BLOCK, n_col - 1)),
        dma((2, tokens // BLOCK, n_col - 1)),
        dma((tokens // BLOCK, n_col - 1, 2)),
        dma((tokens // BLOCK, n_col - 1, 2)),
        dma((tokens // BLOCK,)),
        dma((tokens // BLOCK,)),
        dma((n_col,)),
        dma((n_col,)),
        dma((bits,)),
        dma((bits,)),
        pltpu.SemaphoreType.REGULAR((2,)),
    ]
    res = pl.pallas_call(
        functools.partial(kernel, n_dp, n_col),
        out_shape=tuple(o[1] for o in outs),
        in_specs=[hbm] * 6 + [vmem] * 9,
        out_specs=tuple(o[0] for o in outs),
        scratch_shapes=scratch,
        compiler_params=pltpu.CompilerParams(
            collective_id=0,
            has_side_effects=True,
            vmem_limit_bytes=64 * 2**20,
            fuse_transposed_lhs_in_matmul=True,
        ),
        cost_estimate=pl.CostEstimate(
            flops=45 * 10**9, bytes_accessed=64 * 2**20, transcendentals=8 * 2**20
        ),
    )(
        block_input,
        cotangent,
        jnp.transpose(qkv_weight, (1, 0, 2)),
        fc1_weight,
        fc2_weight,
        dense_weight,
        ln_gain,
        ln_bias,
        dense_bias,
        fc2_bias,
        qkv_bias,
        fc1_bias,
        segment_ids,
        positions,
        freq,
    )
    y_out, in_grad, small, f1, f2, fd, fq = res[:7]
    res = widen(
        ((f1, F32), (f2, F32), (fd, F32), (fq, F32), (y_out, BF), (in_grad, F32)), small, (qw, hid, width)
    )
    f1, f2, fd, fq, y_out, in_grad, qkv_b, fc1_b, bias_a, bias_b, gain_grad, shift_grad = res
    return (
        y_out,
        in_grad,
        gain_grad,
        shift_grad,
        jnp.transpose(fq, (1, 0, 2)),
        qkv_b,
        fd.reshape(dense_weight.shape),
        bias_a,
        f1,
        fc1_b,
        f2.reshape(fc2_weight.shape),
        bias_b,
    )


def solution(mesh):
    return jax.shard_map(
        local,
        mesh=mesh,
        in_specs=(
            P("dp", ("row", "col")),
            P("dp"),
            P("dp"),
            P(("row", "col")),
            P(("row", "col")),
            P("row", None, "col"),
            P(None, "col", "row", None),
            P("col", "row"),
            P(("row", "col")),
            P("row", "col"),
            P("col", "row", None),
            P("col", "row"),
            P(("row", "col")),
            P("dp", ("row", "col")),
        ),
        out_specs=(
            P("dp", ("row", "col")),
            P("dp", ("row", "col")),
            P(("row", "col")),
            P(("row", "col")),
            P("row", None, "col"),
            P(None, "col", "row", None),
            P("col", "row"),
            P(("row", "col")),
            P("row", "col"),
            P("col", "row", None),
            P("col", "row"),
            P(("row", "col")),
        ),
        check_vma=False,
    )
```

```python
import functools
import math

import jax
import jax.numpy as jnp
import numpy as np
from jax import lax
from jax.experimental import pallas as pl
from jax.experimental.pallas import tpu as pltpu
from jax.sharding import PartitionSpec as P

HEAD_DIM = 64
ROT_DIM = 32
NORM_EPSILON = 1e-05
MASKED_SCORE = -1e30
BLOCK = 256
MESH = pl.DeviceIdType.MESH
BF = jnp.bfloat16
F32 = jnp.float32
GELU_A = math.sqrt(2.0 / math.pi)
GELU_B = 0.044715
NN = (((1,), (0,)), ((), ()))
NT = (((1,), (1,)), ((), ()))
TN = (((0,), (0,)), ((), ()))


def dot(a, b, dims):
    return lax.dot_general(a, b, dims, preferred_element_type=F32)


def kernel(
    n_dp,
    n_col,
    x_p,
    cot_p,
    wq_p,
    w1_p,
    w2_p,
    wd_p,
    gain_1d_p,
    shift_1d_p,
    dense_1d_p,
    fc2_1d_p,
    qkv_bias_p,
    fc1_bias_p,
    seg_1d_p,
    pos_1d_p,
    freq_p,
    y_out_p,
    in_grad_p,
    small_p,
    f1_p,
    f2_p,
    fd_p,
    fq_p,
    rb1_p,
    rbd_p,
    rbq_p,
    rzo_p,
    rzn_p,
    rza_p,
    xf_p,
    cf_p,
    gf_p,
    wqf_p,
    w1f_p,
    w2f_p,
    wdf_p,
    normed_p,
    hidden_p,
    pg_p,
    q_p,
    k_p,
    v_p,
    dk_p,
    dv_p,
    bias_p,
    cos_p,
    sin_p,
    ctx_p,
    dctx_p,
    mg_p,
    lse_p,
    g1_p,
    g2_p,
    gd_p,
    gq_p,
    stage1_p,
    staged_p,
    stageq_p,
    stagez_p,
    stageo_p,
    xl_p,
    gb_p,
    vec_p,
    token_p,
    places_p,
    rb2_p,
    mean_p,
    rstd_p,
    tot_p,
    small_v_p,
    small_r_p,
    x_send_p,
    x_recv_p,
    v_send_p,
    v_recv_p,
    vx_send_p,
    vx_recv_p,
    g_send_p,
    g_recv_p,
    c_send_p,
    c_recv_p,
    cx_send_p,
    cx_recv_p,
    w_send_p,
    w_recv_p,
    y_send_p,
    y_recv_p,
    s_send_p,
    s_recv_p,
    load_sem_p,
    rs_send_p,
    rs_recv_p,
    xs_send_p,
    xs_recv_p,
    ag_send_p,
    ag_recv_p,
    part_sem_p,
    stage_sem_p,
    ox_send_p,
    ox_recv_p,
    oz_send_p,
    oz_recv_p,
    za_send_p,
    za_recv_p,
    xo_send_p,
    xo_recv_p,
    tot_send_p,
    tot_recv_p,
    sm_send_p,
    sm_recv_p,
    free_sem_p,
):
    xf, cf, gf = xf_p, cf_p, gf_p
    wqf, w1f, w2f, wdf = wqf_p, w1f_p, w2f_p, wdf_p
    normed, hidden, pg = normed_p, hidden_p, pg_p
    q_s, k_s, v_s, dk_s, dv_s = q_p, k_p, v_p, dk_p, dv_p
    ctx, dctx, mg, lse = ctx_p, dctx_p, mg_p, lse_p
    cos_ref, sin_ref, bias_s = cos_p, sin_p, bias_p
    load_sem, stage_sem = load_sem_p, stage_sem_p

    d = lax.axis_index("dp")
    r = lax.axis_index("row")
    c = lax.axis_index("col")
    n_bits = n_dp.bit_length() - 1
    core = lax.rem(d, 2)
    sibling = d + 1 - 2 * core
    other = 1 - r
    has_right = c < n_col - 1
    has_left = c > 0
    right = jnp.minimum(c + 1, n_col - 1)
    left = jnp.maximum(c - 1, 0)
    tokens, width = x_p.shape
    full = width * n_col * 2
    half = full // 2
    heads_w = qw = ctx.shape[1]
    pairs = heads_w // 128
    n_blocks = tokens // BLOCK
    scale = HEAD_DIM**-0.5

    def to(dd, rr, cc):
        return dict(device_id=(dd, rr, cc), device_id_type=MESH)

    def bit(b):
        return lax.rem(lax.div(d, 1 << b), 2)

    def peer(b):
        return d + (1 - 2 * bit(b)) * (1 << b)

    def remote(src, dst, send, recv, dev):
        return pltpu.make_async_remote_copy(
            src_ref=src, dst_ref=dst, send_sem=send, recv_sem=recv, **dev
        )

    def at(start, size):
        return pl.ds(pl.multiple_of(start, math.gcd(size, 256)), size)

    across = to(d, other, c)

    barrier = pltpu.get_barrier_semaphore()
    pl.semaphore_signal(barrier, inc=1, **across)
    for s in range(1, n_col):
        pl.semaphore_signal(barrier, inc=1, **to(d, r, lax.rem(c + s, n_col)))
    for b in range(n_bits):
        pl.semaphore_signal(barrier, inc=1, **to(peer(b), r, c))

    own_gain = gain_1d_p[...].astype(F32).reshape(1, width)
    vec_p[0:1, :] = own_gain
    vec_p[1:2, :] = dense_1d_p[...].reshape(1, width) + fc2_1d_p[...].reshape(1, width)
    gain_own_p = vec_p.at[0:1, :]
    out_bias_p = vec_p.at[1:2, :]
    gb_p[0:8, :] = jnp.broadcast_to(own_gain, (8, width))
    gb_p[8:16, :] = jnp.broadcast_to(shift_1d_p[...].astype(F32).reshape(1, width), (8, width))
    token_p[0:1, :] = seg_1d_p[...].astype(F32).reshape(1, tokens)
    token_p[1:2, :] = pos_1d_p[...].astype(F32).reshape(1, tokens)

    top = slice(0, tokens // 2)
    low = slice(tokens // 2, tokens)

    def block(ref, rr, j, rows=slice(None)):
        return ref.at[rows, at((rr * n_col + j) * width, width)]

    def hop(way, own, rr, j, lane, step):
        whole, mine_ref, send, recv, rows = way
        dst = block(whole, rr, j, rows)
        return remote(
            mine_ref if own else dst,
            dst,
            send.at[lane, step, j],
            recv.at[lane, j],
            to(d, r, right if step == 0 else left),
        )

    def over(way, own, j, send, recv):
        dst = block(way[0], r, j, way[4])
        return remote(way[1] if own else dst, dst, send, recv, across)

    def landed(dst, recv):
        return remote(dst, dst, recv, recv, across)

    def start_hop(cond, way, own, rr, j, lane, step):
        @pl.when(cond)
        def _():
            hop(way, own, rr, j, lane, step).start()

    def start_both(way, own, rr, lane):
        start_hop(has_right, way, own, rr, c, lane, 0)
        start_hop(has_left, way, own, rr, c, lane, 1)

    def advance(way, rr, lane, s, then=None):
        whole, _, _, recv, rows = way

        @pl.when(c >= s)
        def _():
            j = c - s
            landed(block(whole, rr, j, rows), recv.at[lane, j]).wait_recv()
            start_hop(has_right, way, False, rr, j, lane, 0)
            if then is not None:
                then(j)

        @pl.when(c + s < n_col)
        def _():
            j = c + s
            landed(block(whole, rr, j, rows), recv.at[lane, j]).wait_recv()
            start_hop(has_left, way, False, rr, j, lane, 1)
            if then is not None:
                then(j)

    def drain(way, rr, lane):
        for s in range(n_col):

            @pl.when((c >= s) & has_right)
            def _():
                hop(way, False, rr, jnp.maximum(c - s, 0), lane, 0).wait_send()

            @pl.when((c + s < n_col) & has_left)
            def _():
                j = jnp.minimum(c + s, n_col - 1)
                hop(way, False, rr, j, lane, 1).wait_send()

    def piece(i, k, rr):
        if i < 3:
            depth = wq_p.shape[1] // 4
            return (
                wq_p.at[i, at(k * depth, depth), at((1 - rr) * qw, qw)],
                wqf.at[at((rr * 4 + k) * depth, depth), i * qw : (i + 1) * qw],
            )
        if i == 3:
            depth, part = w1_p.shape[0] // 4, w1_p.shape[1] // 2
            return (
                w1_p.at[at(k * depth, depth), at((1 - rr) * part, part)],
                w1f.at[at((rr * 4 + k) * depth, depth), :],
            )
        src, dst = (w2_p, w2f) if i == 4 else (wd_p, wdf)
        depth, part = src.shape[0] // 8, src.shape[1]
        return (
            src.at[at(((1 - rr) * 4 + k) * depth, depth), :],
            dst.at[at(k * depth, depth), at(rr * part, part)],
        )

    w_send, w_recv, y_send, y_recv = w_send_p, w_recv_p, y_send_p, y_recv_p
    s_send, s_recv = s_send_p, s_recv_p
    upper = bit(1)
    quarter = (core + 2 * upper, core + 2 * (1 - upper))
    quarter_sib = (1 - core + 2 * upper, 1 - core + 2 * (1 - upper))

    def weight_across(i):
        src, dst = piece(i, quarter[0], r)
        return remote(src, dst, w_send.at[i], w_recv.at[i], across)

    def weight_up(i):
        dst = piece(i, quarter[0], other)[1]
        return remote(dst, dst, y_send.at[i], y_recv.at[i], to(peer(1), r, c))

    def weight_share(i, h):
        dst = piece(i, quarter[h], other)[1]
        return remote(dst, dst, s_send.at[i, h], s_recv.at[i, h], to(sibling, r, c))

    def weights_first(group):
        for i in group:
            landed(piece(i, quarter[0], other)[1], w_recv.at[i]).wait_recv()
            weight_up(i).start()
            weight_share(i, 0).start()

    def weights_second(group):
        for i in group:
            landed(piece(i, quarter[1], other)[1], y_recv.at[i]).wait_recv()
            weight_share(i, 1).start()

    def weights_wait(group):
        for i in group:
            for h in range(2):
                landed(piece(i, quarter_sib[h], other)[1], s_recv.at[i, h]).wait_recv()

    x_way = (xf, x_p.at[top, :], x_send_p, x_recv_p, top)
    x_low = (xf, x_p.at[low, :], v_send_p, v_recv_p, low)
    g_way = (gf, gb_p, g_send_p, g_recv_p, slice(None))
    c_way = (cf, cot_p, c_send_p, c_recv_p, slice(None))
    cx_send, cx_recv, vx_send, vx_recv = cx_send_p, cx_recv_p, vx_send_p, vx_recv_p
    g_over = over(g_way, True, c, g_send_p.at[1, 2, c], g_recv_p.at[1, c])
    x_over = over(x_way, True, c, x_send_p.at[1, 2, c], x_recv_p.at[1, c])

    def low_over(j, own=False):
        return over(x_low, own, j, vx_send.at[j], vx_recv.at[j])

    def cot_over(j, own=False):
        return over(c_way, own, j, cx_send.at[j], cx_recv.at[j])

    own = [(x_p, block(xf, r, c)), (gb_p, block(gf, r, c)), (cot_p, block(cf, r, c))]
    depth = wq_p.shape[1]
    for s in range(3):
        own.append((wq_p.at[s, :, at(r * qw, qw)], wqf.at[at(r * depth, depth), s * qw : (s + 1) * qw]))
    depth, part = w1_p.shape[0], w1_p.shape[1] // 2
    own.append((w1_p.at[:, at(r * part, part)], w1f.at[at(r * depth, depth), :]))
    for src, dst in ((w2_p, w2f), (wd_p, wdf)):
        depth, part = src.shape[0] // 2, src.shape[1]
        own.append((src.at[at(r * depth, depth), :], dst.at[:, at(r * part, part)]))
    own = [pltpu.make_async_copy(a, b, load_sem.at[i]) for i, (a, b) in enumerate(own)]
    for copy in own:
        copy.start()

    pl.semaphore_wait(barrier, 1 + (n_col - 1) + n_bits)
    g_over.start()
    x_over.start()
    low_over(c, True).start()
    for way in (g_way, x_way, x_low):
        start_both(way, True, r, 0)

    def tables(i, _):
        rows = at(i * BLOCK, BLOCK)
        wide = jnp.concatenate([token_p[:, rows], jnp.zeros((126, BLOCK), F32)], axis=0)
        places_p[rows, :] = jnp.transpose(wide)
        angle = places_p[rows, 1:2] * freq_p[...]
        cos_ref[rows, :] = jnp.cos(angle)
        sin_ref[rows, :] = jnp.sin(angle)
        return 0

    for i in (3, 0, 1, 2):
        weight_across(i).start()
    for way in (g_way, x_way):
        landed(block(way[0], other, c, way[4]), way[3].at[1, c]).wait_recv()
        start_both(way, False, other, 1)

    def start_cot(s):
        start_hop(has_right & (c == s), c_way, True, r, c, 0, 0)
        start_hop(has_left & (c == n_col - 1 - s), c_way, True, r, c, 0, 1)

    start_cot(0)
    lax.fori_loop(0, n_blocks, tables, 0)
    for s in range(1, n_col):
        advance(g_way, r, 0, s)
        advance(x_way, r, 0, s)
        advance(x_low, r, 0, s, then=lambda j: low_over(j).start())
        advance(g_way, other, 1, s)
        advance(x_way, other, 1, s)
        start_cot(s)
        if s == 1:
            cot_over(c, True).start()
        if s == 2:
            weights_first((3,))
        if s == 3:
            for i in range(4, 6):
                weight_across(i).start()
            weights_first(range(3))
            weights_second((3,))

    def advance_cot(s):
        advance(c_way, r, 0, s, then=lambda j: cot_over(j).start())

    for copy in own:
        copy.wait()
    for s in range(n_col):
        landed(block(xf, other, s, low), vx_recv.at[s]).wait_recv()

    gain = gf[0:1, :]
    shift = gf[8:9, :]

    def norm_rows(i, _):
        rows = at(i * 64, 64)
        v = xf[rows, :].astype(F32)
        mu = jnp.sum(v, axis=1, keepdims=True) * (1.0 / full)
        v = v - mu
        inv = lax.rsqrt(jnp.sum(v * v, axis=1, keepdims=True) * (1.0 / full) + NORM_EPSILON)
        mean_p[rows, :] = mu
        rstd_p[rows, :] = inv
        normed[rows, :] = (v * inv * gain + shift).astype(BF)
        return 0


    lane_at = lax.broadcasted_iota(jnp.int32, (1, 128), 1)
    first = lane_at % HEAD_DIM < ROT_DIM // 2
    low_head = lane_at < HEAD_DIM

    def turn(v, cos, sin, sign):
        up = pltpu.roll(v, 128 - ROT_DIM // 2, 1)
        down = pltpu.roll(v, ROT_DIM // 2, 1)
        swapped = jnp.where(first, -up, down) * sin
        return v * cos + swapped if sign > 0 else v * cos - swapped

    def qkv_rows(i, _):
        rows = at(i * BLOCK, BLOCK)
        mixed = dot(normed[rows, :], wqf[...], NN)
        cos, sin = cos_ref[rows, :], sin_ref[rows, :]
        for s, dst in enumerate((q_s, k_s, v_s)):
            for t in range(pairs):
                lanes = slice(s * qw + t * 128, s * qw + (t + 1) * 128)
                v = mixed[:, lanes] + qkv_bias_p[s, 0, 0:1, t * 128 : (t + 1) * 128]
                dst[t, rows, :] = (turn(v, cos, sin, 1) if s < 2 else v).astype(BF)
        return 0


    def fc1_rows(i, _):
        rows = at(i * BLOCK, BLOCK)
        for h in range(2):
            cols = slice(h * 512, (h + 1) * 512)
            v = dot(normed[rows, :], w1f[:, cols], NN) + fc1_bias_p[0, 0:1, cols]
            th = jnp.tanh(GELU_A * (v + GELU_B * v * v * v))
            hidden[rows, cols] = (0.5 * v * (1.0 + th)).astype(BF)
            slope = 0.5 * (1.0 + th) + 0.5 * v * (1.0 - th * th) * (
                GELU_A * (1.0 + 3.0 * GELU_B * v * v)
            )
            pg[rows, cols] = slope.astype(BF)
        return 0

    def set_bias(i):
        keys = (i + 1) * BLOCK
        rows = slice(i * BLOCK, keys)
        row_at = lax.broadcasted_iota(jnp.int32, (BLOCK, keys), 0) + i * BLOCK
        key_at = lax.broadcasted_iota(jnp.int32, (BLOCK, keys), 1)
        allowed = (places_p[rows, 0:1] == token_p[0:1, :keys]) & (row_at >= key_at)
        bias_s[:, :keys] = jnp.where(allowed, 0.0, MASKED_SCORE)

    def mine(h, v):
        return jnp.where(low_head if h == 0 else ~low_head, v, jnp.zeros_like(v))

    def forward_block(i):
        keys = (i + 1) * BLOCK
        rows = slice(i * BLOCK, keys)
        set_bias(i)

        def pair(t, _):
            q, k, v = q_s[t, rows, :], k_s[t, :keys, :], v_s[t, :keys, :]
            outs = []
            logs = lse[rows, :]
            for h in range(2):
                s = dot(mine(h, q), k, NT) * scale + bias_s[:, :keys]
                top = jnp.max(s, axis=1, keepdims=True)
                e = jnp.exp(s - top)
                total = jnp.sum(e, axis=1, keepdims=True)
                low = (e * (1.0 / total)).astype(BF)
                outs.append(dot(low, v, NN))
                logs = jnp.where(lane_at == 2 * t + h, top + jnp.log(total), logs)
            lse[rows, :] = logs
            ctx[rows, at(t * 128, 128)] = jnp.where(low_head, outs[0], outs[1]).astype(BF)
            return 0

        lax.fori_loop(0, pairs, pair, 0)

    rs_send, rs_recv, xs_send, xs_recv = rs_send_p, rs_recv_p, xs_send_p, xs_recv_p
    ag_send, ag_recv, part_sem = ag_send_p, ag_recv_p, part_sem_p
    g1, g2, gd, gq = g1_p, g2_p, gd_p, gq_p
    tensors = dict(
        fc1=(0, g1, rb1_p, stage1_p, half),
        fc2=(1, g2, rb2_p, None, hidden.shape[1]),
        dense=(2, gd, rbd_p, staged_p, heads_w),
        qkv=(3, gq, rbq_p, stageq_p, half),
    )
    results = dict(fc1=f1_p, fc2=f2_p, dense=fd_p, qkv=fq_p)
    mine_at, theirs_at = r * half, other * half
    starts = (mine_at, theirs_at)

    def slab(ref, p, rows):
        return ref.at[p, :, rows, :] if len(ref.shape) == 4 else ref.at[p, rows, :]

    def offset(rows, upto):
        off = 0
        for b in range(upto):
            off = off + bit(b) * (rows >> (b + 1))
        return off

    def landing(rows, b):
        return slice(rows - (rows >> b), rows - (rows >> (b + 1)))

    def nth(k):
        j = c
        for here in range(n_col):
            turn_k = sorted(range(n_col), key=lambda v: (abs(v - here), v))[k]
            j = jnp.where(c == here, turn_k, j)
        return j

    def sum_copy(name, p, b, k=0):
        n, g, rb, _, rows = tensors[name]
        size = rows >> (b + 1)
        src = slab(g, p, at(offset(rows, b) + (1 - bit(b)) * size, size))
        dst = slab(rb, p, landing(rows, b))
        if name == "fc2":
            cols = at(nth(k) * width, width)
            src, dst = src.at[:, cols], dst.at[:, cols]
        return remote(src, dst, rs_send.at[n, p, b, k], rs_recv.at[n, p, b, k], to(peer(b), r, c))

    def place(name, rr, off, size):
        if name == "fc1":
            return f1_p.at[at(off, size), at(rr * hidden.shape[1], hidden.shape[1])]
        if name == "qkv":
            return fq_p.at[:, at(off, size), at(rr * qw, qw)]
        return results[name].at[rr, at(off, size), :]

    def kept(name, p):
        _, g, _, _, rows = tensors[name]
        size = rows >> n_bits
        off = offset(rows, n_bits)
        return slab(g, p, at(off, size)), off, size

    def part_copy(name):
        src, off, size = kept(name, 0)
        return pltpu.make_async_copy(src, place(name, r, off, size), part_sem.at[tensors[name][0]])

    def swap_copy(name):
        src, off, size = kept(name, 1)
        n = tensors[name][0]
        return remote(src, place(name, r, off, size), xs_send.at[n], xs_recv.at[n], across)

    def fc2_next(p, b, k):
        _, g, rb, _, rows = tensors["fc2"]
        size = rows >> (b + 1)
        off = offset(rows, b + 1)
        cols = at(nth(k) * width, width)
        sum_copy("fc2", p, b, k).wait_recv()
        chunk = min(size, 128)

        def add(i, _):
            there = (p, at(off + i * chunk, chunk), cols)
            here = (p, at(rows - (rows >> b) + i * chunk, chunk), cols)
            g[there] = (g[there].astype(F32) + rb[here].astype(F32)).astype(BF)
            return 0

        lax.fori_loop(0, size // chunk, add, 0)
        if b + 1 < n_bits:
            sum_copy("fc2", p, b + 1, k).start()

    def sum_next(name, p, b):
        n, g, rb, stage, rows = tensors[name]
        size = rows >> (b + 1)
        off = offset(rows, b + 1)
        sum_copy(name, p, b).wait_recv()
        four = len(g.shape) == 4
        chunk = min(size, 128)
        dst = stage.at[:, :size, :] if four else stage.at[:size, :]
        copy = pltpu.make_async_copy(slab(rb, p, landing(rows, b)), dst, stage_sem.at[0])
        copy.start()
        copy.wait()

        def add(i, _):
            if four:
                there = (p, slice(None), at(off + i * chunk, chunk), slice(None))
                here = (slice(None), at(i * chunk, chunk), slice(None))
            else:
                there = (p, at(off + i * chunk, chunk), slice(None))
                here = (at(i * chunk, chunk), slice(None))
            g[there] = (g[there].astype(F32) + stage[here].astype(F32)).astype(BF)
            return 0

        lax.fori_loop(0, size // chunk, add, 0)
        if b + 1 < n_bits:
            sum_copy(name, p, b + 1).start()
        elif p == 0:
            part_copy(name).start()
        else:
            swap_copy(name).start()

    def fc2_rest(p):
        for b in range(1, n_bits):
            for k in range(n_col):
                fc2_next(p, b, k)
        if p == 0:
            part_copy("fc2").start()
        else:
            swap_copy("fc2").start()

    def sum_rest(name, p):
        for b in range(1, n_bits):
            sum_next(name, p, b)

    def spread_copy(name, p, b):
        n, rows = tensors[name][0], tensors[name][4]
        ref = place(name, r if p == 0 else other, offset(rows, b + 1), rows >> (b + 1))
        return remote(ref, ref, ag_send_p.at[n, p, b], ag_recv_p.at[n, p, b], to(peer(b), r, c))

    def spread_landed(name, p, b):
        n, rows = tensors[name][0], tensors[name][4]
        size = rows >> (b + 1)
        off = offset(rows, b) + (1 - bit(b)) * size
        return landed(place(name, r if p == 0 else other, off, size), ag_recv_p.at[n, p, b])

    def spread_first(name, p):
        if p == 0:
            part_copy(name).wait()
        else:
            _, off, size = kept(name, 1)
            landed(place(name, other, off, size), xs_recv_p.at[tensors[name][0]]).wait_recv()
        spread_copy(name, p, n_bits - 1).start()

    def spread_next(name, p, b):
        spread_landed(name, p, b).wait_recv()
        if b > 0:
            spread_copy(name, p, b - 1).start()

    def spread_rest(name, p):
        for b in reversed(range(1, n_bits)):
            spread_next(name, p, b)

    def finish(name):
        for b in range(n_bits):
            for p in range(2):
                for k in range(n_col if name == "fc2" else 1):
                    sum_copy(name, p, b, k).wait_send()
                spread_copy(name, p, b).wait_send()
        swap_copy(name).wait_send()

    def fc2_grad(p, k):
        col = nth(k) * width

        def body(i, _):
            cols = at(i * BLOCK, BLOCK)
            g2[p, cols, at(col, width)] = dot(
                hidden[:, cols], cf[:, at(starts[p] + col, width)], TN
            ).astype(BF)
            return 0

        lax.fori_loop(0, hidden.shape[1] // BLOCK, body, 0)
        sum_copy("fc2", p, 0, k).start()

    def fc1_grad(p):
        def body(i, _):
            g1[p, at(i * BLOCK, BLOCK), :] = dot(
                normed[:, at(starts[p] + i * BLOCK, BLOCK)], pg[...], TN
            ).astype(BF)
            return 0

        lax.fori_loop(0, half // BLOCK, body, 0)
        sum_copy("fc1", p, 0).start()

    def dense_grad(p):
        gd[p] = dot(ctx[...], cf[:, at(starts[p], half)], TN).astype(BF)
        sum_copy("dense", p, 0).start()

    def qkv_grad(p):
        def body(i, _):
            v = dot(normed[:, at(starts[p] + i * BLOCK, BLOCK)], mg[...], TN).astype(BF)
            for s in range(3):
                gq[p, s, at(i * BLOCK, BLOCK), :] = v[:, s * qw : (s + 1) * qw]
            return 0

        lax.fori_loop(0, half // BLOCK, body, 0)
        sum_copy("qkv", p, 0).start()

    ox_send, ox_recv, oz_send, oz_recv = ox_send_p, ox_recv_p, oz_send_p, oz_recv_p
    free_sem = free_sem_p
    outputs = ((xf, rzo_p), (cf, rzn_p))

    def out_part(n, rows, start):
        if n == 0:
            return dot(ctx[rows, :], wdf[:, at(start, half)], NN) + dot(
                hidden[rows, :], w2f[:, at(start, half)], NN
            )
        return dot(mg[rows, :], wqf[at(start, half), :], NT) + dot(
            pg[rows, :], w1f[at(start, half), :], NT
        )

    def part_over(n, i):
        buf = outputs[n][0]
        rows = slice(i * BLOCK, (i + 1) * BLOCK)
        return remote(
            buf.at[rows, :half], buf.at[rows, half:], ox_send.at[n, i], ox_recv.at[n, i], across
        )

    def send_theirs(n, i):
        rows = slice(i * BLOCK, (i + 1) * BLOCK)
        outputs[n][0][rows, :half] = out_part(n, rows, theirs_at).astype(BF)
        part_over(n, i).start()

    def part_on(n, i, s):
        buf, landing_z = outputs[n]
        rows = slice(i * BLOCK, (i + 1) * BLOCK)
        j = lax.rem(c + s, n_col)
        return remote(
            buf.at[rows, at(j * width, width)],
            landing_z.at[s - 1, rows, :],
            oz_send.at[n, i, s - 1],
            oz_recv.at[n, i, s - 1],
            to(d, r, j),
        )

    def scatter(n, i):
        buf = outputs[n][0]
        rows = slice(i * BLOCK, (i + 1) * BLOCK)
        part_over(n, i).wait()
        v = out_part(n, rows, mine_at) + buf[rows, half:].astype(F32)
        bias_s[:, :half] = v
        buf[rows, :half] = v.astype(BF)
        for t in range(width // 128):
            own_part = bias_s[:, at(c * width + t * 128, 128)]
            if n == 0:
                in_grad_p[rows, t * 128 : (t + 1) * 128] = own_part
            else:
                dv_s[t, rows, :] = own_part
        for s in range(1, n_col):
            part_on(n, i, s).start()

    stagez, stageo = stagez_p, stageo_p

    def full_on(i, s, h):
        rows = slice(i * BLOCK, (i + 1) * BLOCK)
        j = lax.rem(c + s, n_col)
        return remote(
            xf.at[rows, at(starts[h] + j * width, width)],
            rza_p.at[s - 1, h, rows, :],
            za_send_p.at[i, s - 1, h],
            za_recv_p.at[i, s - 1, h],
            to(d, r, j),
        )

    def out_full(i):
        rows = slice(i * BLOCK, (i + 1) * BLOCK)
        for start in starts:
            xf[rows, at(start, half)] = out_part(0, rows, start).astype(BF)
        for s in range(1, n_col):
            for h in range(2):
                full_on(i, s, h).start()

    def swap_out(i):
        rows = slice(i * BLOCK, (i + 1) * BLOCK)
        return remote(
            xf.at[rows, at(theirs_at + c * width, width)],
            xl_p.at[rows, :],
            xo_send_p.at[i],
            xo_recv_p.at[i],
            across,
        )

    def collect_full(i):
        rows = slice(i * BLOCK, (i + 1) * BLOCK)
        for s in range(1, n_col):
            for h in range(2):
                full_on(i, s, h).wait_recv()
        load = pltpu.make_async_copy(rza_p.at[:, :, rows, :], stageo, stage_sem.at[1])
        load.start()
        load.wait()
        for h, start in enumerate(starts):
            own = at(start + c * width, width)
            v = xf[rows, own].astype(F32)
            for s in range(n_col - 1):
                v = v + stageo[s, h].astype(F32)
            if h == 0:
                in_grad_p[rows, :] = v
            else:
                xf[rows, own] = v.astype(BF)
        swap_out(i).start()

    def collect_half(n, i):
        rows = slice(i * BLOCK, (i + 1) * BLOCK)
        for s in range(1, n_col):
            part_on(n, i, s).wait_recv()
        landing_z = outputs[n][1]
        load = pltpu.make_async_copy(landing_z.at[:, rows, :], stageo.at[:, 0], stage_sem.at[1])
        load.start()
        load.wait()
        for t in range(width // 128):
            lanes = slice(t * 128, (t + 1) * 128)
            v = stageo[0, 0, :, lanes].astype(F32)
            for s in range(1, n_col - 1):
                v = v + stageo[s, 0, :, lanes].astype(F32)
            if n == 0:
                in_grad_p[rows, lanes] += v
            else:
                dv_s[t, rows, :] += v

    def backward_block(i):
        keys = (i + 1) * BLOCK
        rows = slice(i * BLOCK, keys)
        set_bias(i)

        def pair(t, _):
            lanes = at(t * 128, 128)
            q, k, v = q_s[t, rows, :], k_s[t, :keys, :], v_s[t, :keys, :]
            grad = dctx[rows, lanes]
            query_grads = []
            for h in range(2):
                qh, gh = mine(h, q), mine(h, grad)
                log_total = jnp.sum(
                    jnp.where(lane_at == 2 * t + h, lse[rows, :], 0.0), axis=1, keepdims=True
                )
                p = jnp.exp(dot(qh, k, NT) * scale + bias_s[:, :keys] - log_total)
                dp = dot(gh, v, NT)
                dv_s[t, :keys, :] += dot(p.astype(BF), gh, TN)
                centre = jnp.sum(p * dp, axis=1, keepdims=True)
                ds = (p * (dp - centre) * scale).astype(BF)
                query_grads.append(dot(ds, k, NN))
                dk_s[t, :keys, :] += dot(ds, qh, TN)
            dq = jnp.where(low_head, query_grads[0], query_grads[1])
            mg[rows, lanes] = turn(dq, cos_ref[rows, :], sin_ref[rows, :], -1).astype(BF)
            return 0

        lax.fori_loop(0, pairs, pair, 0)

    def grad_rows(i, _):
        rows = at(i * BLOCK, BLOCK)
        dctx[rows, :] = dot(cf[rows, :], wdf[...], NT).astype(BF)
        for h in range(2):
            cols = slice(h * 512, (h + 1) * 512)
            v = dot(cf[rows, :], w2f[cols, :], NT)
            pg[rows, cols] = (v * pg[rows, cols].astype(F32)).astype(BF)
        return 0

    def theirs_came(k):
        j = nth(k)
        landed(block(cf, other, j), cx_recv.at[j]).wait_recv()

    def finish_mixed(i):
        rows = slice(i * BLOCK, (i + 1) * BLOCK)
        for t in range(pairs):
            lanes = slice(qw + t * 128, qw + (t + 1) * 128)
            mg[rows, lanes] = turn(dk_s[t, rows, :], cos_ref[rows, :], sin_ref[rows, :], -1).astype(BF)
            lanes = slice(2 * qw + t * 128, 2 * qw + (t + 1) * 128)
            mg[rows, lanes] = dv_s[t, rows, :].astype(BF)

    tot, small_v, small_r = tot_p, small_v_p, small_r_p
    n_mixed, n_pre = mg.shape[1], pg.shape[1]
    base = n_mixed + n_pre

    def column_sums(i, _):
        rows = at(i * BLOCK, BLOCK)
        for ref, lo, size in ((mg, 0, n_mixed), (pg, n_mixed, n_pre), (stagez.at[0], base, width)):
            small_v[0:1, lo : lo + size] += jnp.sum(ref[rows, :].astype(F32), axis=0, keepdims=True)
        return 0

    def collect_norm(i):
        collect_half(1, i)
        rows = slice(i * BLOCK, (i + 1) * BLOCK)
        mu, inv = mean_p[rows, :], rstd_p[rows, :]
        one = jnp.zeros((BLOCK, 1), F32)
        two = jnp.zeros((BLOCK, 1), F32)
        for t in range(width // 128):
            lanes = slice(t * 128, (t + 1) * 128)
            g = dv_s[t, rows, :]
            hat = (stagez[1, rows, lanes].astype(F32) - mu) * inv
            sg = g * gain_own_p[:, lanes]
            one = one + jnp.sum(sg, axis=1, keepdims=True)
            two = two + jnp.sum(sg * hat, axis=1, keepdims=True)
            lo = base + width + t * 128
            small_v[0:1, lo : lo + 128] += jnp.sum(g * hat, axis=0, keepdims=True)
            lo = base + 2 * width + t * 128
            small_v[0:1, lo : lo + 128] += jnp.sum(g, axis=0, keepdims=True)
        packed = jnp.where(lane_at == 0, one, jnp.where(lane_at == 1, two, 0.0))
        tot[0, :, rows] = jnp.transpose(packed)[0:8, :]

    def small_copy(b):
        return remote(small_v, small_r.at[b], sm_send_p.at[b], sm_recv_p.at[b], to(peer(b), r, c))

    lax.fori_loop(0, tokens // 64, norm_rows, 0)
    advance_cot(1)
    weights_second(range(3))
    weights_wait((3,))
    lax.fori_loop(0, n_blocks, fc1_rows, 0)
    fc2_grad(0, 0)
    theirs_came(0)
    fc2_grad(1, 0)
    fc2_grad(0, 1)
    weights_wait(range(3))
    lax.fori_loop(0, n_blocks, qkv_rows, 0)
    advance_cot(2)
    weights_first(range(4, 6))
    for p, k in ((0, 0), (1, 0), (0, 1)):
        fc2_next(p, 0, k)
    fc2_grad(0, 2)
    lse[...] = jnp.zeros_like(lse)
    for i in range(n_blocks):
        if i == n_blocks - 2:
            theirs_came(1)
            fc2_grad(1, 1)
            fc2_next(0, 0, 2)
            weights_second(range(4, 6))
        if i == n_blocks - 1:
            advance_cot(3)
            fc2_grad(0, 3)
            fc2_next(1, 0, 1)
        forward_block(i)
    dense_grad(0)
    fc2_next(0, 0, 3)
    weights_wait(range(4, 6))
    for way in (g_way, x_way):
        drain(way, r, 0)
        drain(way, other, 1)
    drain(x_low, r, 0)
    for s in range(n_col):
        low_over(s).wait_send()
    g_over.wait_send()
    x_over.wait_send()
    pl.semaphore_signal(free_sem.at[0], inc=1, **across)
    n_full = n_blocks // 2
    for i in range(n_full):
        out_full(i)
        if i == 0:
            sum_next("dense", 0, 0)
    pl.semaphore_wait(free_sem.at[0], 1)
    for i in range(n_full, n_blocks):
        send_theirs(0, i)
    theirs_came(2)
    fc2_grad(1, 2)
    fc2_rest(0)
    spread_first("fc2", 0)
    fc2_next(1, 0, 2)
    theirs_came(3)
    fc2_grad(1, 3)
    lax.fori_loop(0, n_blocks, grad_rows, 0)
    dense_grad(1)
    fc2_next(1, 0, 3)
    fc1_grad(1)
    sum_rest("dense", 0)
    spread_first("dense", 0)
    sum_next("dense", 1, 0)
    drain(c_way, r, 0)
    for s in range(n_col):
        cot_over(s).wait_send()
    pl.semaphore_signal(free_sem.at[1], inc=1, **across)
    sum_next("fc1", 1, 0)
    fc1_grad(0)
    fc2_rest(1)
    scatter(0, n_full)
    sum_next("fc1", 0, 0)
    sum_rest("dense", 1)
    dk_s[...] = jnp.zeros_like(dk_s)
    dv_s[...] = jnp.zeros_like(dv_s)
    pl.semaphore_wait(free_sem.at[1], 1)
    for i in reversed(range(n_blocks)):
        backward_block(i)
        finish_mixed(i)
        send_theirs(1, i)
        if i == n_blocks - 1:
            for m in range(n_full + 1, n_blocks):
                scatter(0, m)
            spread_first("fc2", 1)
        if i == n_blocks // 2:
            for p in (1, 0):
                sum_rest("fc1", p)
            spread_first("fc1", 0)
        if i == 1:
            scatter(1, n_blocks - 1)
    for p in (1, 0):
        qkv_grad(p)
    loads = [
        pltpu.make_async_copy(ref, stagez.at[m], stage_sem.at[2 + m])
        for m, ref in enumerate((cot_p, x_p))
    ]
    for load in loads:
        load.start()
    small_v[...] = jnp.zeros_like(small_v)
    sum_next("qkv", 1, 0)
    scatter(1, n_blocks - 2)
    sum_next("qkv", 0, 0)
    spread_first("dense", 1)
    for load in loads:
        load.wait()
    lax.fori_loop(0, n_blocks, column_sums, 0)
    spread_first("fc1", 1)
    sum_rest("qkv", 1)
    for i in range(n_full):
        collect_full(i)
    for i in reversed(range(1, n_blocks - 2)):
        scatter(1, i)
    sum_rest("qkv", 0)
    spread_first("qkv", 0)
    for name, p in (("fc2", 0), ("dense", 0), ("fc2", 1)):
        spread_rest(name, p)
    for i in range(n_full, n_blocks):
        collect_half(0, i)
    scatter(1, 0)
    spread_rest("fc1", 0)
    spread_rest("dense", 1)
    collect_norm(n_blocks - 1)
    spread_first("qkv", 1)
    for i in reversed(range(1, n_blocks - 1)):
        collect_norm(i)
    spread_rest("fc1", 1)
    collect_norm(0)
    swap = remote(tot.at[0], tot.at[1], tot_send_p.at[0], tot_recv_p.at[0], across)
    swap.start()
    small_copy(0).start()
    swap.wait()
    tot[0] = tot[0] + tot[1]
    tot_copies = [
        remote(
            tot.at[0],
            tot.at[1 + s],
            tot_send_p.at[s],
            tot_recv_p.at[s],
            to(d, r, lax.rem(c + s, n_col)),
        )
        for s in range(1, n_col)
    ]
    for copy in tot_copies:
        copy.start()
    spread_rest("qkv", 0)
    for b in range(n_bits):
        small_copy(b).wait()
        small_v[...] = small_v[...] + small_r[b]
        if b + 1 < n_bits:
            small_copy(b + 1).start()
    small_p[...] = small_v[...]
    for i in range(n_full):
        swap_out(i).wait_recv()
    for i in range(n_blocks):
        rows = slice(i * BLOCK, (i + 1) * BLOCK)
        v = stagez[1, rows, :].astype(F32) + in_grad_p[rows, :] + out_bias_p[...]
        if i < n_full:
            v = v + xl_p[rows, :].astype(F32)
        y_out_p[rows, :] = v.astype(BF)
    spread_rest("qkv", 1)
    for copy in tot_copies:
        copy.wait()
    tot[1] = tot[0]
    for s in range(1, n_col):
        tot[1] = tot[1] + tot[1 + s]

    def in_final(i, _):
        rows = at(i * BLOCK, BLOCK)
        mu, inv = mean_p[rows, :], rstd_p[rows, :]
        sums = jnp.transpose(
            jnp.concatenate([tot[1, :, rows], jnp.zeros((120, BLOCK), F32)], axis=0)
        ) * (1.0 / full)
        one, two = sums[:, 0:1], sums[:, 1:2]
        for t in range(width // 128):
            lanes = slice(t * 128, (t + 1) * 128)
            hat = (stagez[1, rows, lanes].astype(F32) - mu) * inv
            sg = dv_s[t, rows, :] * gain_own_p[:, lanes]
            in_grad_p[rows, lanes] = stagez[0, rows, lanes].astype(F32) + inv * (
                sg - one - hat * two
            )
        return 0

    lax.fori_loop(0, n_blocks, in_final, 0)
    for name in tensors:
        for p in range(2):
            spread_next(name, p, 0)
    for name in tensors:
        finish(name)
    for i in range(6):
        weight_across(i).wait_send()
        weight_up(i).wait_send()
        for h in range(2):
            weight_share(i, h).wait_send()
    for i in range(n_full):
        swap_out(i).wait_send()
        for s in range(1, n_col):
            for h in range(2):
                full_on(i, s, h).wait_send()
    for n in range(2):
        for i in range(n_full if n == 0 else 0, n_blocks):
            for s in range(1, n_col):
                part_on(n, i, s).wait_send()


def widen_kernel(widths, *refs):
    n_wide = 6
    for src, dst in zip(refs[:n_wide], refs[n_wide + 1 : 2 * n_wide + 1]):
        dst[...] = src[...].astype(dst.dtype)
    small = refs[n_wide]
    qkv_ref, fc1_ref, bias_a, bias_b, gain_ref, shift_ref = refs[2 * n_wide + 1 :]
    qw, hid, width = widths

    @pl.when(pl.program_id(0) == 0)
    def _():
        for s in range(3):
            qkv_ref[s, 0, 0:1, :] = small[0:1, s * qw : (s + 1) * qw]
        at = 3 * qw
        fc1_ref[0, 0:1, :] = small[0:1, at : at + hid]
        at = at + hid
        for i, dsts in enumerate(((bias_a, bias_b), (gain_ref,), (shift_ref,))):
            for dst in dsts:
                dst[...] = small[0, at + i * width : at + (i + 1) * width]


def widen(arrays, small, widths):
    steps = 2
    qw, hid, width = widths

    def spec(shape):
        block = shape[:-2] + (shape[-2] // steps, shape[-1])
        lead = len(shape) - 2
        return pl.BlockSpec(block, lambda i: (0,) * lead + (i, 0))

    def whole(shape):
        return pl.BlockSpec(shape, lambda i: (0,) * len(shape))

    wide = [jax.ShapeDtypeStruct(a.shape, t) for a, t in arrays]
    shapes = [(3, 1, 1, qw), (1, 1, hid)] + [(width,)] * 4
    specs = [spec(a.shape) for a, _ in arrays]
    return pl.pallas_call(
        functools.partial(widen_kernel, widths),
        grid=(steps,),
        out_shape=wide + [jax.ShapeDtypeStruct(z, F32) for z in shapes],
        in_specs=specs + [whole(small.shape)],
        out_specs=specs + [whole(z) for z in shapes],
        compiler_params=pltpu.CompilerParams(vmem_limit_bytes=64 * 2**20),
        cost_estimate=pl.CostEstimate(
            flops=0, bytes_accessed=40 * 2**20, transcendentals=0
        ),
    )(*[a for a, _ in arrays], small)


def local(
    block_input,
    segment_ids,
    positions,
    ln_gain,
    ln_bias,
    qkv_weight,
    qkv_bias,
    dense_weight,
    dense_bias,
    fc1_weight,
    fc1_bias,
    fc2_weight,
    fc2_bias,
    cotangent,
):
    n_col = lax.axis_size("col")
    n_dp = lax.axis_size("dp")
    n_bits = n_dp.bit_length() - 1
    tokens, width = block_input.shape
    full = width * n_col * 2
    half = full // 2
    qw = qkv_weight.shape[2] // 2
    hid = fc1_weight.shape[1] // 2
    pairs = qw // 128
    small_w = 3 * qw + hid + 3 * width
    lane = np.arange(128) % HEAD_DIM
    steps = (lane % (ROT_DIM // 2)).astype(np.float32)
    freq = np.exp(steps * np.float32(-2.0 * math.log(10000.0) / ROT_DIM), dtype=np.float32)
    freq = jnp.asarray(np.where(lane < ROT_DIM, freq, np.float32(0.0))[None])
    hbm = pl.BlockSpec(memory_space=pl.ANY)
    vmem = pl.BlockSpec(memory_space=pltpu.VMEM)
    dma = pltpu.SemaphoreType.DMA
    bits = max(n_bits, 1)
    sds = jax.ShapeDtypeStruct
    outs = (
        (vmem, sds((tokens, width), BF)),
        (vmem, sds((tokens, width), F32)),
        (vmem, sds((8, small_w), F32)),
        (hbm, sds((half, 2 * hid), BF)),
        (hbm, sds((2, hid, half), BF)),
        (hbm, sds((2, qw, half), BF)),
        (hbm, sds((3, half, 2 * qw), BF)),
        (hbm, sds((2, half, hid), BF)),
        (hbm, sds((2, qw, half), BF)),
        (hbm, sds((2, 3, half, qw), BF)),
        (hbm, sds((n_col - 1, tokens, width), BF)),
        (hbm, sds((n_col - 1, tokens, width), BF)),
        (hbm, sds((n_col - 1, 2, tokens, width), BF)),
    )
    v = pltpu.VMEM
    scratch = [
        v((tokens, full), BF),
        v((tokens, full), BF),
        v((16, full), F32),
        v((full, 3 * qw), BF),
        v((full, hid), BF),
        v((hid, full), BF),
        v((qw, full), BF),
        v((tokens, full), BF),
        v((tokens, hid), BF),
        v((tokens, hid), BF),
        v((pairs, tokens, 128), BF),
        v((pairs, tokens, 128), BF),
        v((pairs, tokens, 128), BF),
        v((pairs, tokens, 128), F32),
        v((pairs, tokens, 128), F32),
        v((BLOCK, tokens), F32),
        v((tokens, 128), F32),
        v((tokens, 128), F32),
        v((tokens, qw), BF),
        v((tokens, qw), BF),
        v((tokens, 3 * qw), BF),
        v((tokens, 128), F32),
        v((2, half, hid), BF),
        v((2, hid, half), BF),
        v((2, qw, half), BF),
        v((2, 3, half, qw), BF),
        v((half // 2, hid), BF),
        v((qw // 2, half), BF),
        v((3, half // 2, qw), BF),
        v((2, tokens, width), BF),
        v((n_col - 1, 2, BLOCK, width), BF),
        v((tokens, width), BF),
        v((16, width), F32),
        v((2, width), F32),
        v((2, tokens), F32),
        v((tokens, 128), F32),
        v((2, hid - (hid >> bits), half), BF),
        v((tokens, 1), F32),
        v((tokens, 1), F32),
        v((n_col + 1, 8, tokens), F32),
        v((8, small_w), F32),
        v((bits, 8, small_w), F32),
        dma((2, 3, n_col)),
        dma((2, n_col)),
        dma((1, 2, n_col)),
        dma((1, n_col)),
        dma((n_col,)),
        dma((n_col,)),
        dma((2, 3, n_col)),
        dma((2, n_col)),
        dma((1, 2, n_col)),
        dma((1, n_col)),
        dma((n_col,)),
        dma((n_col,)),
        dma((6,)),
        dma((6,)),
        dma((6,)),
        dma((6,)),
        dma((6, 2)),
        dma((6, 2)),
        dma((9,)),
        dma((4, 2, bits, n_col)),
        dma((4, 2, bits, n_col)),
        dma((4,)),
        dma((4,)),
        dma((4, 2, bits)),
        dma((4, 2, bits)),
        dma((4,)),
        dma((4,)),
        dma((2, tokens // BLOCK)),
        dma((2, tokens // BLOCK)),
        dma((2, tokens // BLOCK, n_col - 1)),
        dma((2, tokens // BLOCK, n_col - 1)),
        dma((tokens // BLOCK, n_col - 1, 2)),
        dma((tokens // BLOCK, n_col - 1, 2)),
        dma((tokens // BLOCK,)),
        dma((tokens // BLOCK,)),
        dma((n_col,)),
        dma((n_col,)),
        dma((bits,)),
        dma((bits,)),
        pltpu.SemaphoreType.REGULAR((2,)),
    ]
    res = pl.pallas_call(
        functools.partial(kernel, n_dp, n_col),
        out_shape=tuple(o[1] for o in outs),
        in_specs=[hbm] * 6 + [vmem] * 9,
        out_specs=tuple(o[0] for o in outs),
        scratch_shapes=scratch,
        compiler_params=pltpu.CompilerParams(
            collective_id=0,
            has_side_effects=True,
            vmem_limit_bytes=64 * 2**20,
            fuse_transposed_lhs_in_matmul=True,
        ),
        cost_estimate=pl.CostEstimate(
            flops=45 * 10**9, bytes_accessed=64 * 2**20, transcendentals=8 * 2**20
        ),
    )(
        block_input,
        cotangent,
        jnp.transpose(qkv_weight, (1, 0, 2)),
        fc1_weight,
        fc2_weight,
        dense_weight,
        ln_gain,
        ln_bias,
        dense_bias,
        fc2_bias,
        qkv_bias,
        fc1_bias,
        segment_ids,
        positions,
        freq,
    )
    y_out, in_grad, small, f1, f2, fd, fq = res[:7]
    res = widen(
        ((f1, F32), (f2, F32), (fd, F32), (fq, F32), (y_out, BF), (in_grad, F32)), small, (qw, hid, width)
    )
    f1, f2, fd, fq, y_out, in_grad, qkv_b, fc1_b, bias_a, bias_b, gain_grad, shift_grad = res
    return (
        y_out,
        in_grad,
        gain_grad,
        shift_grad,
        jnp.transpose(fq, (1, 0, 2)),
        qkv_b,
        fd.reshape(dense_weight.shape),
        bias_a,
        f1,
        fc1_b,
        f2.reshape(fc2_weight.shape),
        bias_b,
    )


def solution(mesh):
    return jax.shard_map(
        local,
        mesh=mesh,
        in_specs=(
            P("dp", ("row", "col")),
            P("dp"),
            P("dp"),
            P(("row", "col")),
            P(("row", "col")),
            P("row", None, "col"),
            P(None, "col", "row", None),
            P("col", "row"),
            P(("row", "col")),
            P("row", "col"),
            P("col", "row", None),
            P("col", "row"),
            P(("row", "col")),
            P("dp", ("row", "col")),
        ),
        out_specs=(
            P("dp", ("row", "col")),
            P("dp", ("row", "col")),
            P(("row", "col")),
            P(("row", "col")),
            P("row", None, "col"),
            P(None, "col", "row", None),
            P("col", "row"),
            P(("row", "col")),
            P("row", "col"),
            P("col", "row", None),
            P("col", "row"),
            P(("row", "col")),
        ),
        check_vma=False,
    )
```
